128 devices in a mesh: seq: 8 (over y, core), exp: 16 (over z, x).
Axes of the slice: x: 4, y: 4, z: 4, core: 2. Of those that a mesh axis runs over, the one named last changes fastest.
Arguments:
- qkv_in: bfloat16 [16384, 6144], P('exp', 'seq'), may hold values from -6 to 6
- qkv_grad: bfloat16 [16384, 6144], P('exp', 'seq'), may hold values from -6 to 6
- conv_weight: float32 [4, 6144], P(None, 'seq'), may hold values from -3 to 3
- doc_ids: int32 [16384], replicated, may hold values from 0 to 15, never falling along the last dimension, each value on 1 to 4096 neighbouring positions
- qkv_weight: bfloat16 [6144, 2304], P('seq'), may hold values from -0.0078125 to 0.0078125
- resid: bfloat16 [16384, 2304], P(('exp', 'seq')), may hold values from -54 to 54
- norm_gain: float32 [2304], replicated, may hold values from 0.5 to 1.5
- out_grad: bfloat16 [16384, 2304], P(('exp', 'seq')), may hold values from -0.59765625 to 0.59765625
- routes: int32 [16384, 8], P(('exp', 'seq')), may hold values from 0 to 127, all different within a row; in each aligned block of 128 rows (0 to 127, 128 to 255, ...) at most 16 rows name the same one
- route_weights: float32 [16384, 8], P(('exp', 'seq')), may hold values from 0.05 to 1
- expert_weights: bfloat16 [128, 2304, 1536], P(('seq', 'exp')), may hold values from -0.125 to 0.125
Outputs:
- qkv_in_grad: bfloat16 [16384, 6144], P(('exp', 'seq'))
- expert_grads: bfloat16 [128, 2304, 1536], P(('seq', 'exp'))
The draws below stay inside these ranges and needn't reach their ends.
Inputs may be any that keep to these rules, and one draw needn't show every extreme that they name: `routes`: each row names 8 different experts. In the rows of one device (aligned blocks of 128 rows) no expert is named more than 16 times, and in some block some expert is named exactly 16 times. `doc_ids`: document numbers never fall along the sequence; every document has 1 to 4096 positions, one exactly 4096.
All inputs are finite; a program needn't handle non-finite values.
Results may differ from the reference program's by a relative error of at most 0.019.
Values may be sent and summed in bfloat16 or wider, within the bound.
No kernel may reach another device: no remote copies, remote signals or barrier semaphores. Data moves between devices by JAX's collectives and lax.ppermute only.
A program may use at most 192 MiB of HBM per device.

```python
import math
import jax
import jax.numpy as jnp
import numpy as np
from jax import lax

D = 2304
EXP_FF = 512
TOP = 8
DOCS = 16
TOK_DEV = 128
EXPERTS = 128
CAP = 16
LENGTH = 16384
QKV = 6144
DOC_MOST = 4096
N_SEQ = 8


def draw_resid(key, part):
    key = jax.random.fold_in(key, 7)
    entry_key, row_key, col_key = jax.random.split(key, 3)
    row_scale = jnp.exp(jax.random.uniform(row_key, (LENGTH, 1), jnp.float32, math.log(0.3), math.log(3.0)))
    col_scale = jnp.exp(jax.random.uniform(col_key, (1, D), jnp.float32, math.log(0.3), math.log(3.0)))
    entries = jnp.clip(jax.random.normal(entry_key, (LENGTH, D), jnp.float32), -6.0, 6.0)
    return (entries * row_scale * col_scale).astype(jnp.bfloat16)


def block_levels(own_key, shape, pieces, low, largest):
    def one(position, blocks):
        steps = jax.random.uniform(jax.random.fold_in(jax.random.fold_in(own_key, 6), position), (blocks,), jnp.float32, low / len(pieces), largest / len(pieces))
        return jnp.repeat(jnp.exp(steps), shape[position] // blocks).reshape((-1,) + (1,) * (len(shape) - position - 1))

    level = one(*pieces[0])
    for cut in pieces[1:]:
        level = level * one(*cut)
    return level


def split_up(count, total, bound, lean):
    portions = [(1 << 20) // math.isqrt(standing ** lean) + 1 for standing in range(2, count + 1)]
    rest, counts = total - bound - (count - 1), [1] * (count - 1)
    while rest > 0:
        movable = [i for i in range(count - 1) if counts[i] < bound]
        mass, left = sum([portions[i] for i in movable]), rest
        for i in movable:
            addition = min(bound - counts[i], max(1, left * portions[i] // mass), rest)
            counts[i] = counts[i] + addition
            rest = rest - addition
    return np.array([bound] + counts)


def uneven(key, count, total, limit, skew):
    if count == 2:
        one = jax.random.randint(key, (), max(1, total - limit), min(limit, total - 1) + 1)
        return jnp.stack([one, total - one])
    lengths = jnp.asarray(split_up(count, total, limit, skew), jnp.int32)
    twos = (count - 1) // 2
    giver, taker = lengths[1:1 + 2 * twos:2], lengths[2:2 + 2 * twos:2]
    slack = jnp.minimum(giver - 1, limit - taker)
    passed = jax.random.randint(jax.random.fold_in(key, 1), (twos,), 0, 1 << 20) % (slack + 1)
    lengths = lengths.at[1:1 + 2 * twos:2].set(giver - passed).at[2:2 + 2 * twos:2].set(taker + passed)
    return lengths[jax.random.permutation(jax.random.fold_in(key, 2), count)]


def routed_block(own_key, own, number, rows, count, top, most, skew):
    ranking = jax.random.permutation(own_key, count)
    packed, common = load_shares(count, rows * top, most, skew, True), load_shares(count, rows * top, most, skew, False)
    places = jnp.arange(count)

    def named(sizes, turn):
        used = int((sizes > 0).sum())
        fixed = max(1, used // 4)
        moved = fixed + (places - fixed + turn * (used - fixed)) % max(1, count - fixed)
        return jnp.zeros((count,), jnp.int32).at[ranking[jnp.where(places < fixed, places, moved)]].set(jnp.asarray(sizes, jnp.int32))

    sizes = jnp.where(number % 4 == 0, named(packed, number // 4), named(common, number - number // 4 - 1))
    mixed = jax.random.permutation(jax.random.fold_in(own, 3), count)
    giver, receiver = mixed[0:count // 2 * 2:2], mixed[1:count // 2 * 2:2]
    slack = jnp.minimum(sizes[giver] - 1, most - sizes[receiver]) // 2
    slack = jnp.where((giver == ranking[0]) | (receiver == ranking[0]) | (sizes[receiver] == 0), 0, jnp.maximum(slack, 0))
    moved = jax.random.randint(jax.random.fold_in(own, 4), (count // 2,), 0, 1 << 20) % (slack + 1)
    sizes = sizes.at[giver].add(-moved).at[receiver].add(moved)
    labels = jnp.searchsorted(jnp.cumsum(sizes), jnp.arange(rows * top), side="right").astype(jnp.int32)
    table = labels.reshape(top, rows).T
    table = table[jax.random.permutation(jax.random.fold_in(own, 1), rows)]
    turn = jax.random.randint(jax.random.fold_in(own, 2), (rows, 1), 0, top)
    return jnp.take_along_axis(table, (jnp.arange(top)[None, :] + turn) % top, axis=1)


def load_shares(count, total, reach, slope, full):
    loads = [(1 << 20) // math.isqrt(standing ** slope) + 1 for standing in range(1, count + 1)]
    largest = reach if full else min(reach, max(-(-total // count), total * loads[0] // sum(loads)))
    least = 1 if total - largest >= count - 1 else 0
    counts, rest = [largest] + [least] * (count - 1), total - largest - least * (count - 1)
    while rest > 0:
        candidates = [i for i in range(1, count) if counts[i] < largest] or [i for i in range(1, count) if counts[i] < reach]
        whole, left = sum([loads[i] for i in candidates]), rest
        for i in candidates:
            addition = min(reach - counts[i], max(1, left * loads[i] // whole), rest)
            counts[i] = counts[i] + addition
            rest = rest - addition
    return np.array(counts)


def gaussian(own_key, dims, scale, bound, shards=(), kind=jnp.bfloat16):
    factor_of = block_levels(own_key, dims, shards, -0.22, 0.18) if shards else 1.0
    array = jax.random.normal(own_key, dims, jnp.float32) * scale * factor_of
    return jnp.minimum(jnp.maximum(array, -bound), bound).astype(kind)


def setup_inputs(seed: int = 0) -> dict:
    seeds = jax.random.split(jax.random.key(seed), 12)
    qkv_in = gaussian(seeds[0], (LENGTH, QKV), 1.0, 6.0, ((0, 16), (1, 8)))
    qkv_grad = gaussian(seeds[1], (LENGTH, QKV), 1.0, 6.0, ((0, 16), (1, 8)))
    conv_weight = gaussian(seeds[2], (4, QKV), 4 ** -0.5, 3.0, ((1, 8),), jnp.float32)
    doc_ids = jnp.searchsorted(jnp.cumsum(uneven(seeds[3], DOCS, LENGTH, DOC_MOST, 1)), jnp.arange(LENGTH), side="right").astype(jnp.int32)
    qkv_weight = gaussian(seeds[4], (QKV, D), (100 * QKV) ** -0.5, 0.0078125, ((0, 8),))
    resid = draw_resid(jax.random.fold_in(seeds[11], 71), 0)
    norm_gain = jnp.clip(1.0 + 0.1 * jax.random.normal(seeds[6], (D,), jnp.float32), 0.5, 1.5)
    out_grad = gaussian(seeds[7], (LENGTH, D), 0.1, 0.59765625, ((0, 128),))
    routes_keys = jax.random.split(jax.random.fold_in(seeds[8], 1), LENGTH // TOK_DEV)
    routes_turns = jax.random.permutation(jax.random.fold_in(seeds[8], 3), LENGTH // TOK_DEV)
    routes = jax.vmap(lambda own, number: routed_block(jax.random.fold_in(seeds[8], 2), own, number, TOK_DEV, EXPERTS, TOP, CAP, 2))(routes_keys, routes_turns).reshape((LENGTH, TOP))
    route_weights = jnp.clip(jnp.exp(math.log(1.0) - 2.9957323 * jax.random.uniform(seeds[9], (LENGTH, TOP), jnp.float32) ** block_levels(seeds[9], (LENGTH, TOP), ((0, 128),), -0.2, 0.2)), 0.05, 1.0)
    expert_weights = gaussian(seeds[10], (EXPERTS, D, 3 * EXP_FF), D ** -0.5, 0.125, ((0, 128),))
    return {"qkv_in": qkv_in, "qkv_grad": qkv_grad, "conv_weight": conv_weight, "doc_ids": doc_ids, "qkv_weight": qkv_weight, "resid": resid, "norm_gain": norm_gain, "out_grad": out_grad, "routes": routes, "route_weights": route_weights, "expert_weights": expert_weights}


def conv_block(inputs, grad_in, weight, doc_ids):
    seq_length = inputs.shape[0]
    inputs_f = inputs.astype(jnp.float32)
    grads_f = grad_in.astype(jnp.float32)
    padded_in = jnp.concatenate([jnp.zeros((3, inputs_f.shape[1]), jnp.float32), inputs_f], 0)
    ids_before = jnp.concatenate([jnp.full((3,), -1, jnp.int32), doc_ids.astype(jnp.int32)])
    summed = jnp.zeros_like(inputs_f)
    for back_by in range(4):
        matches = (ids_before[3 - back_by:3 - back_by + seq_length] == doc_ids).astype(jnp.float32)
        summed = summed + weight[back_by][None, :] * padded_in[3 - back_by:3 - back_by + seq_length] * matches[:, None]
    sigmoid_z = jax.nn.sigmoid(summed)
    pre_grad = grads_f * sigmoid_z * (1.0 + summed * (1.0 - sigmoid_z))
    padded_grad = jnp.concatenate([pre_grad, jnp.zeros((3, pre_grad.shape[1]), jnp.float32)], 0)
    ids_after = jnp.concatenate([doc_ids.astype(jnp.int32), jnp.full((3,), -1, jnp.int32)])
    result = jnp.zeros_like(inputs_f)
    for ahead_by in range(4):
        matches = (ids_after[ahead_by:ahead_by + seq_length] == doc_ids).astype(jnp.float32)
        result = result + weight[ahead_by][None, :] * padded_grad[ahead_by:ahead_by + seq_length] * matches[:, None]
    return result.astype(jnp.bfloat16)

def expert_terms(rows_h, rows_g, live_rows, own_weights, hidden):
    mixed_rows = jnp.dot(rows_h, own_weights[:, :2 * hidden], preferred_element_type=jnp.float32)
    gate_pre = mixed_rows[:, :hidden]
    up_value = mixed_rows[:, hidden:]
    gate_sig = jax.nn.sigmoid(gate_pre)
    keep_rows = live_rows.astype(jnp.float32)[:, None]
    activated = (gate_pre * gate_sig * up_value * keep_rows).astype(jnp.bfloat16)
    act_grad = jnp.dot(rows_g, own_weights[:, 2 * hidden:], preferred_element_type=jnp.float32)
    hidden_grad = jnp.concatenate([act_grad * up_value * gate_sig * (1.0 + gate_pre * (1.0 - gate_sig)), act_grad * gate_pre * gate_sig], 1)
    hidden_grad = (hidden_grad * keep_rows).astype(jnp.bfloat16)
    grad_gu = lax.dot_general(rows_h, hidden_grad, (((0,), (0,)), ((), ())), preferred_element_type=jnp.float32)
    grad_dn = lax.dot_general(rows_g, activated, (((0,), (0,)), ((), ())), preferred_element_type=jnp.float32)
    return (grad_gu, grad_dn)

def reference(qkv_in, qkv_grad, conv_weight, doc_ids, qkv_weight, resid, norm_gain, out_grad, routes, route_weights, expert_weights):
    block_width = QKV // N_SEQ
    blocks = []
    for column in range(N_SEQ):
        first_col = column * block_width
        blocks.append(conv_block(qkv_in[:, first_col:first_col + block_width], qkv_grad[:, first_col:first_col + block_width], conv_weight[:, first_col:first_col + block_width], doc_ids))
    qkv_in_grad = jnp.concatenate(blocks, 1)
    proj_grad = jnp.dot(qkv_in_grad, qkv_weight, preferred_element_type=jnp.float32)
    flow_grad = (out_grad.astype(jnp.float32) + proj_grad).astype(jnp.bfloat16)
    resid_f = resid.astype(jnp.float32)
    scale_rows = lax.rsqrt(lax.optimization_barrier(jnp.mean(resid_f * resid_f, axis=1, keepdims=True)) + 1e-06)
    normed = (resid_f * scale_rows * norm_gain[None, :]).astype(jnp.bfloat16)
    flat_routes = routes.reshape(-1).astype(jnp.int32)
    flat_weights = route_weights.reshape(-1)
    max_rows = EXPERTS * CAP
    tile_rows = 256
    hidden = EXP_FF

    def one_expert(expert):
        chosen = flat_routes == expert
        row_count = jnp.sum(chosen.astype(jnp.int32))
        pair_list = jnp.nonzero(chosen, size=max_rows, fill_value=0)[0].astype(jnp.int32)
        own_weights = expert_weights[expert]

        def tile_step(tile_index, totals):
            picked = lax.dynamic_slice_in_dim(pair_list, (tile_index * tile_rows).astype(jnp.int32), tile_rows)
            live_rows = tile_index * tile_rows + jnp.arange(tile_rows, dtype=jnp.int32) < row_count
            token_rows = picked // TOP
            rows_h = normed[token_rows]
            rows_g = (flat_weights[picked][:, None] * flow_grad[token_rows].astype(jnp.float32)).astype(jnp.bfloat16)
            part_gu, part_dn = expert_terms(rows_h, rows_g, live_rows, own_weights, hidden)
            return (totals[0] + part_gu, totals[1] + part_dn)
        tile_count = (row_count + tile_rows - 1) // tile_rows
        start_sums = (jnp.zeros((D, 2 * hidden), jnp.float32), jnp.zeros((D, hidden), jnp.float32))
        grad_gu, grad_dn = lax.fori_loop(jnp.int32(0), tile_count.astype(jnp.int32), tile_step, start_sums)
        return jnp.concatenate([grad_gu, grad_dn], 1).astype(jnp.bfloat16)
    expert_grads = lax.map(one_expert, jnp.arange(EXPERTS, dtype=jnp.int32))
    return (qkv_in_grad, expert_grads)
```

```python
import functools

import jax
import jax.numpy as jnp
from jax import lax
from jax.experimental import pallas as pl
from jax.experimental.pallas import tpu as pltpu
from jax.sharding import PartitionSpec as P

BF16 = jnp.bfloat16
F32 = jnp.float32
HALO = 16
MIB = 1024 * 1024
VMEM_LIMIT = 60 * MIB
EXTRA = 128
RING = 4


def call_cost(flops, nbytes):
    return pl.CostEstimate(flops=int(flops), bytes_accessed=int(nbytes), transcendentals=0)


def norm_kernel(resid_ref, gain_ref, routes_ref, out_ref):
    rows = resid_ref[...].astype(F32)
    dim = rows.shape[1]
    scale = lax.rsqrt(jnp.mean(rows * rows, axis=1, keepdims=True) + 1e-06)
    out_ref[:, :dim] = (rows * scale * gain_ref[...]).astype(BF16)
    out_ref[:, dim:] = jnp.zeros((rows.shape[0], EXTRA), BF16)
    out_ref[:, dim : dim + routes_ref.shape[1]] = routes_ref[...].astype(F32).astype(BF16)


def norm_rows(resid, gain, routes):
    tokens, dim = resid.shape
    return pl.pallas_call(
        norm_kernel,
        out_shape=jax.ShapeDtypeStruct((tokens, dim + EXTRA), BF16),
        compiler_params=pltpu.CompilerParams(vmem_limit_bytes=VMEM_LIMIT),
        cost_estimate=call_cost(resid.size * 6, resid.size * 4),
        name="norm_rows",
    )(resid, gain.reshape(1, -1), routes)


def conv_kernel(
    tile,
    seq_ref,
    in_ref,
    in_low_ref,
    in_high_ref,
    grad_ref,
    grad_high_ref,
    ids_ref,
    taps_ref,
    weight_ref,
    flow_ref,
    local_ref,
    part_ref,
    in_ext,
    grad_ext,
):
    step = pl.program_id(0)
    rows = in_ref.shape[0]

    @pl.when(step == 0)
    def _():
        in_ext[:HALO] = in_low_ref[...].astype(F32)
        in_ext[HALO : HALO + rows] = in_ref[...].astype(F32)
        in_ext[HALO + rows :] = in_high_ref[...].astype(F32)
        grad_ext[:rows] = grad_ref[...].astype(F32)
        grad_ext[rows:] = grad_high_ref[...].astype(F32)

    first = pl.multiple_of(step * tile, tile)
    span = tile + 8
    taps = taps_ref[...]
    window = in_ext[pl.ds(first + HALO - 8, span + 8)]
    ids = ids_ref[pl.ds(first + HALO - 8, span + 8)]
    here = ids[8:]
    same = [None] + [(ids[8 - j : 8 - j + span] == here).astype(F32) for j in (1, 2, 3)]
    conv = taps[0:1] * window[8:]
    for j in (1, 2, 3):
        conv = conv + taps[j : j + 1] * window[8 - j : 8 - j + span] * same[j]
    gate = jax.nn.sigmoid(conv)
    pre = grad_ext[pl.ds(first, span)] * gate * (1.0 + conv * (1.0 - gate))
    result = taps[0:1] * pre[:tile]
    for j in (1, 2, 3):
        result = result + taps[j : j + 1] * (pre * same[j])[j : j + tile]
    local = result.astype(BF16)
    local_ref[...] = local
    part = jnp.dot(local, weight_ref[...], preferred_element_type=F32)
    part_ref[...] = part.astype(BF16)
    block = flow_ref.shape[0]
    per_tile = tile // block
    for inner in range(per_tile):

        @pl.when(step * per_tile + inner == seq_ref[0])
        def _():
            own = slice(inner * block, (inner + 1) * block)
            part_ref[own] = (part[own] + flow_ref[...].astype(F32)).astype(BF16)


def conv_project(seq_index, qkv_in, low, high, qkv_grad, grad_high, ids, taps, weight, out_grad):
    rows, width = qkv_in.shape
    dim = weight.shape[1]
    tile = 256
    whole = lambda shape: pl.BlockSpec(shape, lambda i, s: (0,) * len(shape))
    return pl.pallas_call(
        functools.partial(conv_kernel, tile),
        grid_spec=pltpu.PrefetchScalarGridSpec(
            num_scalar_prefetch=1,
            grid=(rows // tile,),
            in_specs=[
                whole(qkv_in.shape),
                whole(low.shape),
                whole(high.shape),
                whole(qkv_grad.shape),
                whole(grad_high.shape),
                whole(ids.shape),
                whole(taps.shape),
                whole(weight.shape),
                whole(out_grad.shape),
            ],
            out_specs=[
                pl.BlockSpec((tile, width), lambda i, s: (i, 0)),
                pl.BlockSpec((tile, dim), lambda i, s: (i, 0)),
            ],
            scratch_shapes=[
                pltpu.VMEM((rows + 2 * HALO, width), F32),
                pltpu.VMEM((rows + HALO, width), F32),
            ],
        ),
        out_shape=[
            jax.ShapeDtypeStruct((rows, width), BF16),
            jax.ShapeDtypeStruct((rows, dim), BF16),
        ],
        compiler_params=pltpu.CompilerParams(vmem_limit_bytes=VMEM_LIMIT),
        cost_estimate=call_cost(2 * rows * width * dim, 4 * rows * width * 2 + rows * dim * 2),
        name="conv_project",
    )(seq_index, qkv_in, low, high, qkv_grad, grad_high, ids, taps, weight, out_grad)


def seq_shift(s, dy, dc, sign):
    return (((s >> 1) + sign * dy) & (RING - 1)) * 2 + ((s & 1) ^ dc)


def exp_shift(e, dz, dx, sign):
    return (((e >> 2) + sign * dz) & (RING - 1)) * RING + ((e + sign * dx) & (RING - 1))


def slot_picker(names, own, capacity):
    count, tokens = own.shape
    match = [(names[k : k + 1] == own) for k in range(names.shape[0])]
    named = functools.reduce(jnp.logical_or, match)
    source = lax.broadcasted_iota(jnp.int32, (tokens, tokens), 0)
    target = lax.broadcasted_iota(jnp.int32, (tokens, tokens), 1)
    earlier = (source < target).astype(BF16)
    rank = jnp.dot(named.astype(BF16), earlier, preferred_element_type=F32).astype(jnp.int32)
    rank = jnp.where(named, rank, -1)
    slot = lax.broadcasted_iota(jnp.int32, (count, capacity, tokens), 1)
    picker = (rank[:, None, :] == slot).astype(F32)
    return picker, match


def pick_norm_kernel(per_token, capacity, place_ref, rows_ref, *out_refs):
    count = len(out_refs)
    tokens = rows_ref.shape[1]
    dim = out_refs[0].shape[2]
    names = rows_ref[0, :, dim:].astype(F32).T[:per_token].astype(jnp.int32)
    turn = lax.broadcasted_iota(jnp.int32, (count, tokens), 0)
    own = seq_shift(place_ref[0], turn >> 1, turn & 1, 1) * (RING * RING) + place_ref[1]
    picker, _ = slot_picker(names, own, capacity)
    picker = picker.reshape(count * capacity, tokens).astype(BF16)
    picked = jnp.dot(picker, rows_ref[0, :, :dim], preferred_element_type=F32).astype(BF16)
    for index, out_ref in enumerate(out_refs):
        out_ref[0] = picked[index * capacity : (index + 1) * capacity]


def pick_norm(place, rows, dim, per_token, capacity, count):
    blocks, tokens, width = rows.shape
    return pl.pallas_call(
        functools.partial(pick_norm_kernel, per_token, capacity),
        grid_spec=pltpu.PrefetchScalarGridSpec(
            num_scalar_prefetch=1,
            grid=(blocks,),
            in_specs=[
                pl.BlockSpec(
                    (1, tokens, width), lambda i, p: (exp_shift(p[1], i >> 2, i & 3, -1), 0, 0)
                )
            ],
            out_specs=[pl.BlockSpec((1, capacity, dim), lambda i, p: (i, 0, 0))] * count,
        ),
        out_shape=[jax.ShapeDtypeStruct((blocks, capacity, dim), BF16)] * count,
        compiler_params=pltpu.CompilerParams(vmem_limit_bytes=VMEM_LIMIT),
        cost_estimate=call_cost(
            2 * count * capacity * blocks * tokens * dim,
            2 * dim * blocks * (tokens + count * capacity),
        ),
        name="pick_norm",
    )(place, rows)


def pick_grad_kernel(per_token, capacity, place_ref, table_ref, rows_ref, *out_refs):
    count = len(out_refs)
    tokens = rows_ref.shape[1]
    names = table_ref[0, :per_token].astype(jnp.int32)
    turn = lax.broadcasted_iota(jnp.int32, (count, tokens), 0)
    own = place_ref[0] * (RING * RING) + exp_shift(place_ref[1], turn >> 2, turn & 3, 1)
    picker, match = slot_picker(names, own, capacity)
    weights = table_ref[0, per_token:]
    scale = functools.reduce(
        jnp.add, [jnp.where(match[k], weights[k : k + 1], 0.0) for k in range(per_token)]
    )
    scales = jnp.sum(picker * scale[:, None, :], axis=2, keepdims=True)
    picker = picker.reshape(count * capacity, tokens).astype(BF16)
    picked = jnp.dot(picker, rows_ref[0], preferred_element_type=F32)
    picked = (picked * scales.reshape(count * capacity, 1)).astype(BF16)
    for index, out_ref in enumerate(out_refs):
        out_ref[0] = picked[index * capacity : (index + 1) * capacity]


def pick_grad(place, table, rows, per_token, capacity, count):
    blocks, tokens, dim = rows.shape
    source = lambda i, p: (seq_shift(p[0], i >> 1, i & 1, -1), 0, 0)
    return pl.pallas_call(
        functools.partial(pick_grad_kernel, per_token, capacity),
        grid_spec=pltpu.PrefetchScalarGridSpec(
            num_scalar_prefetch=1,
            grid=(blocks,),
            in_specs=[
                pl.BlockSpec((1, 2 * per_token, tokens), source),
                pl.BlockSpec((1, tokens, dim), source),
            ],
            out_specs=[pl.BlockSpec((1, capacity, dim), lambda i, p: (i, 0, 0))] * count,
        ),
        out_shape=[jax.ShapeDtypeStruct((blocks, capacity, dim), BF16)] * count,
        compiler_params=pltpu.CompilerParams(vmem_limit_bytes=VMEM_LIMIT),
        cost_estimate=call_cost(
            2 * count * capacity * blocks * tokens * dim,
            2 * dim * blocks * (tokens + count * capacity),
        ),
        name="pick_grad",
    )(place, table, rows)


def forward_kernel(sources, *refs):
    row_refs = refs[:sources]
    weight_ref, rows_out, act_ref, gate_ref, up_ref = refs[sources:]
    pair, capacity, _ = row_refs[0].shape
    for inner in range(pair):
        for index in range(sources):
            at = (inner * sources + index) * capacity
            rows_out[at : at + capacity] = row_refs[index][inner]
    hidden = act_ref.shape[1]
    mixed = jnp.dot(rows_out[...], weight_ref[...], preferred_element_type=F32)
    gate = mixed[:, :hidden]
    up = mixed[:, hidden:]
    sig = jax.nn.sigmoid(gate)
    silu = gate * sig
    act_ref[...] = (silu * up).astype(BF16)
    gate_ref[...] = up * sig * (1.0 + gate * (1.0 - sig))
    up_ref[...] = silu


def expert_forward(rows, weight, hidden):
    sources = len(rows)
    blocks, capacity, dim = rows[0].shape
    pair = 2
    tile = sources * pair * capacity
    total = sources * blocks * capacity
    row_spec = lambda width: pl.BlockSpec((tile, width), lambda i: (i, 0))
    return pl.pallas_call(
        functools.partial(forward_kernel, sources),
        grid=(blocks // pair,),
        in_specs=[pl.BlockSpec((pair, capacity, dim), lambda i: (i, 0, 0))] * sources
        + [pl.BlockSpec((dim, 2 * hidden), lambda i: (0, 0))],
        out_specs=[row_spec(dim), row_spec(hidden), row_spec(hidden), row_spec(hidden)],
        out_shape=[
            jax.ShapeDtypeStruct((total, dim), BF16),
            jax.ShapeDtypeStruct((total, hidden), BF16),
            jax.ShapeDtypeStruct((total, hidden), F32),
            jax.ShapeDtypeStruct((total, hidden), F32),
        ],
        compiler_params=pltpu.CompilerParams(vmem_limit_bytes=VMEM_LIMIT),
        cost_estimate=call_cost(4 * total * dim * hidden, 4 * total * dim + 10 * total * hidden),
        name="expert_forward",
    )(*rows, weight)


def backward_kernel(sources, *refs):
    grad_refs = refs[:sources]
    gate_ref, up_ref, weight_ref, rows_ref, act_ref, out_ref = refs[sources : sources + 6]
    grads_all, hidden_all, sems = refs[sources + 6 :]
    step = pl.program_id(0)
    tile = gate_ref.shape[0]
    hidden = act_ref.shape[1]
    width = rows_ref.shape[1]
    size = grad_refs[0].shape[0]
    per_tile = tile // size
    row_steps = sources // per_tile
    copies = [
        pltpu.make_async_copy(
            grad_refs[index], grads_all.at[pl.ds(index * size, size)], sems.at[index]
        )
        for index in range(sources)
    ]

    @pl.when(step == 0)
    def _():
        for copy in copies:
            copy.start()

    for turn in range(row_steps):

        @pl.when(step == turn)
        def _():
            for copy in copies[turn * per_tile : (turn + 1) * per_tile]:
                copy.wait()

    @pl.when(step < row_steps)
    def _():
        where = pl.ds(pl.multiple_of(step * tile, tile), tile)
        act_grad = jnp.dot(grads_all[where], weight_ref[...], preferred_element_type=F32)
        hidden_all[where, :hidden] = (act_grad * gate_ref[...]).astype(BF16)
        hidden_all[where, hidden:] = (act_grad * up_ref[...]).astype(BF16)

    @pl.when(step >= row_steps)
    def _():
        columns = pl.ds(pl.multiple_of((step - row_steps) * width, width), width)
        over_rows = (((0,), (0,)), ((), ()))
        out_ref[:, : 2 * hidden] = lax.dot_general(
            rows_ref[...], hidden_all[...], over_rows, preferred_element_type=F32
        ).astype(BF16)
        out_ref[:, 2 * hidden :] = lax.dot_general(
            grads_all[:, columns], act_ref[...], over_rows, preferred_element_type=F32
        ).astype(BF16)


def expert_backward(grads, gate, up, weights, rows, act):
    sources = len(grads)
    total, dim = rows.shape
    hidden = act.shape[1]
    tile, width = 256, 256
    row_steps, column_steps = total // tile, dim // width
    row_spec = lambda cols: pl.BlockSpec(
        (tile, cols), lambda i: (jnp.minimum(i, row_steps - 1), 0)
    )
    column_of = lambda i: jnp.maximum(i - row_steps, 0)
    return pl.pallas_call(
        functools.partial(backward_kernel, sources),
        grid=(row_steps + column_steps,),
        in_specs=[pl.BlockSpec(memory_space=pl.ANY)] * sources
        + [
            row_spec(hidden),
            row_spec(hidden),
            pl.BlockSpec((dim, hidden), lambda i: (0, 2)),
            pl.BlockSpec((total, width), lambda i: (0, column_of(i))),
            pl.BlockSpec((total, hidden), lambda i: (0, 0)),
        ],
        out_specs=pl.BlockSpec((width, 3 * hidden), lambda i: (column_of(i), 0)),
        out_shape=jax.ShapeDtypeStruct((dim, 3 * hidden), BF16),
        scratch_shapes=[
            pltpu.VMEM((total, dim), BF16),
            pltpu.VMEM((total, 2 * hidden), BF16),
            pltpu.SemaphoreType.DMA((sources,)),
        ],
        compiler_params=pltpu.CompilerParams(vmem_limit_bytes=VMEM_LIMIT),
        cost_estimate=call_cost(8 * total * dim * hidden, 4 * total * dim + 20 * total * hidden),
        name="expert_backward",
    )(*grads, gate, up, weights, rows, act)


def exchange_seq(blocks, n_seq):
    got = [blocks[0]]
    for r in range(1, n_seq):
        pairs = [(s, seq_shift(s, r >> 1, r & 1, 1)) for s in range(n_seq)]
        got.append(lax.ppermute(blocks[r], "seq", pairs))
    return got


def exchange_exp(blocks, n_exp):
    got = [blocks[0]]
    for q in range(1, n_exp):
        pairs = [(e, exp_shift(e, q >> 2, q & 3, 1)) for e in range(n_exp)]
        got.append(lax.ppermute(blocks[q], "exp", pairs))
    return got


def per_device(
    qkv_in,
    qkv_grad,
    conv_weight,
    doc_ids,
    qkv_weight,
    resid,
    norm_gain,
    out_grad,
    routes,
    route_weights,
    expert_weights,
):
    rows, width = qkv_in.shape
    tokens, dim = resid.shape
    per_token = routes.shape[1]
    hidden = expert_weights.shape[2] // 3
    n_seq, n_exp = lax.axis_size("seq"), lax.axis_size("exp")
    experts = n_seq * n_exp
    capacity = 2 * tokens * per_token // experts
    seq_index, exp_index = lax.axis_index("seq"), lax.axis_index("exp")
    own_weights = expert_weights[0]

    forward = [(i, i + 1) for i in range(n_exp - 1)]
    backward = [(i + 1, i) for i in range(n_exp - 1)]
    low = lax.ppermute(qkv_in[-HALO:], "exp", forward)
    high = lax.ppermute(qkv_in[:HALO], "exp", backward)
    grad_high = lax.ppermute(qkv_grad[:HALO], "exp", backward)

    place = jnp.stack([seq_index, exp_index]).astype(jnp.int32)
    table = jnp.concatenate([routes.astype(F32), route_weights], 1).T
    tables = jnp.broadcast_to(table[None], (n_seq,) + table.shape)
    tables = lax.all_to_all(tables, "seq", split_axis=0, concat_axis=0, tiled=True)
    normed = norm_rows(resid, norm_gain, routes)
    exp_normed = lax.all_gather(normed, "exp")

    edge = jnp.full((HALO,), -1, jnp.int32)
    ids = lax.dynamic_slice_in_dim(
        jnp.concatenate([edge, doc_ids, edge]), exp_index * rows, rows + 2 * HALO
    )
    local_grad, partial = conv_project(
        seq_index.reshape(1),
        qkv_in,
        low,
        high,
        qkv_grad,
        grad_high,
        ids.reshape(-1, 1),
        conv_weight,
        qkv_weight,
        out_grad,
    )
    flow = lax.psum(partial, "seq")
    flow, local_grad = lax.optimization_barrier((flow, local_grad))
    qkv_in_grad = lax.all_to_all(local_grad, "seq", split_axis=0, concat_axis=1, tiled=True)

    send_rows = pick_norm(place, exp_normed, dim, per_token, capacity, n_seq)
    got_rows = exchange_seq(send_rows, n_seq)
    rows_all, act, gate, up = expert_forward(got_rows, own_weights, hidden)

    flow = flow.reshape(n_seq, tokens, dim)
    send_grads = pick_grad(place, tables, flow, per_token, capacity, n_exp)
    got_grads = [g.reshape(-1, dim) for g in exchange_exp(send_grads, n_exp)]
    expert_grads = expert_backward(got_grads, gate, up, own_weights, rows_all, act)
    return (qkv_in_grad, expert_grads[None])


def solution(mesh):
    return jax.shard_map(
        per_device,
        mesh=mesh,
        in_specs=(
            P("exp", "seq"),
            P("exp", "seq"),
            P(None, "seq"),
            P(),
            P("seq", None),
            P(("exp", "seq"), None),
            P(),
            P(("exp", "seq"), None),
            P(("exp", "seq"), None),
            P(("exp", "seq"), None),
            P(("seq", "exp"), None, None),
        ),
        out_specs=(P(("exp", "seq"), None), P(("seq", "exp"), None, None)),
        check_vma=False,
    )
```

```python
import functools

import jax
import jax.numpy as jnp
from jax import lax
from jax.experimental import pallas as pl
from jax.experimental.pallas import tpu as pltpu
from jax.sharding import PartitionSpec as P

BF16 = jnp.bfloat16
F32 = jnp.float32
HALO = 16
MIB = 1024 * 1024
VMEM_LIMIT = 60 * MIB
EXTRA = 128


def call_cost(flops, nbytes):
    return pl.CostEstimate(flops=int(flops), bytes_accessed=int(nbytes), transcendentals=0)


def norm_kernel(resid_ref, gain_ref, routes_ref, out_ref):
    rows = resid_ref[...].astype(F32)
    dim = rows.shape[1]
    scale = lax.rsqrt(jnp.mean(rows * rows, axis=1, keepdims=True) + 1e-06)
    out_ref[:, :dim] = (rows * scale * gain_ref[...]).astype(BF16)
    out_ref[:, dim:] = jnp.zeros((rows.shape[0], EXTRA), BF16)
    out_ref[:, dim : dim + routes_ref.shape[1]] = routes_ref[...].astype(F32).astype(BF16)


def norm_rows(resid, gain, routes):
    tokens, dim = resid.shape
    return pl.pallas_call(
        norm_kernel,
        out_shape=jax.ShapeDtypeStruct((tokens, dim + EXTRA), BF16),
        compiler_params=pltpu.CompilerParams(vmem_limit_bytes=VMEM_LIMIT),
        cost_estimate=call_cost(resid.size * 6, resid.size * 4),
        name="norm_rows",
    )(resid, gain.reshape(1, -1), routes)


def conv_kernel(
    tile,
    place_ref,
    in_ref,
    in_low_ref,
    in_high_ref,
    grad_ref,
    grad_high_ref,
    ids_ref,
    taps_ref,
    local_ref,
    keep_ref,
    send_ref,
    in_ext,
    grad_ext,
):
    step = pl.program_id(0)
    rows = in_ref.shape[0]

    @pl.when(step == 0)
    def _():
        in_ext[:HALO] = in_low_ref[...].astype(F32)
        in_ext[HALO : HALO + rows] = in_ref[...].astype(F32)
        in_ext[HALO + rows :] = in_high_ref[...].astype(F32)
        grad_ext[:rows] = grad_ref[...].astype(F32)
        grad_ext[rows:] = grad_high_ref[...].astype(F32)

    first = pl.multiple_of(step * tile, tile)
    span = tile + 8
    taps = taps_ref[...]
    window = in_ext[pl.ds(first + HALO - 8, span + 8)]
    ids = ids_ref[pl.ds(first + HALO - 8, span + 8)]
    here = ids[8:]
    same = [None] + [(ids[8 - j : 8 - j + span] == here).astype(F32) for j in (1, 2, 3)]
    conv = taps[0:1] * window[8:]
    for j in (1, 2, 3):
        conv = conv + taps[j : j + 1] * window[8 - j : 8 - j + span] * same[j]
    gate = jax.nn.sigmoid(conv)
    pre = grad_ext[pl.ds(first, span)] * gate * (1.0 + conv * (1.0 - gate))
    result = taps[0:1] * pre[:tile]
    for j in (1, 2, 3):
        result = result + taps[j : j + 1] * (pre * same[j])[j : j + tile]
    local = result.astype(BF16)
    local_ref[...] = local
    half = tile // 2
    core = place_ref[0] & 1

    @pl.when(core == 0)
    def _():
        keep_ref[...] = local[:half]
        send_ref[...] = local[half:]

    @pl.when(core == 1)
    def _():
        keep_ref[...] = local[half:]
        send_ref[...] = local[:half]


def conv_back(place, qkv_in, low, high, qkv_grad, grad_high, ids, taps, block):
    rows, width = qkv_in.shape
    tile = 2 * block
    whole = lambda shape: pl.BlockSpec(shape, lambda i, p: (0,) * len(shape))
    part = lambda size: pl.BlockSpec((size, width), lambda i, p: (i, 0))
    return pl.pallas_call(
        functools.partial(conv_kernel, tile),
        grid_spec=pltpu.PrefetchScalarGridSpec(
            num_scalar_prefetch=1,
            grid=(rows // tile,),
            in_specs=[
                whole(qkv_in.shape),
                whole(low.shape),
                whole(high.shape),
                whole(qkv_grad.shape),
                whole(grad_high.shape),
                whole(ids.shape),
                whole(taps.shape),
            ],
            out_specs=[part(tile), part(block), part(block)],
            scratch_shapes=[
                pltpu.VMEM((rows + 2 * HALO, width), F32),
                pltpu.VMEM((rows + HALO, width), F32),
            ],
        ),
        out_shape=[
            jax.ShapeDtypeStruct((rows, width), BF16),
            jax.ShapeDtypeStruct((rows // 2, width), BF16),
            jax.ShapeDtypeStruct((rows // 2, width), BF16),
        ],
        compiler_params=pltpu.CompilerParams(vmem_limit_bytes=VMEM_LIMIT),
        cost_estimate=call_cost(40 * rows * width, 8 * rows * width),
        name="conv_back",
    )(place, qkv_in, low, high, qkv_grad, grad_high, ids, taps)


def project_kernel(place_ref, own_ref, other_ref, own_weight, other_weight, flow_ref, out_ref):
    block = flow_ref.shape[0]
    total = jnp.dot(own_ref[...], own_weight[...], preferred_element_type=F32)
    total = total + jnp.dot(other_ref[...], other_weight[...], preferred_element_type=F32)
    out_ref[...] = total.astype(BF16)
    for index in range(out_ref.shape[0] // block):

        @pl.when(index == place_ref[0] >> 1)
        def _():
            own = slice(index * block, (index + 1) * block)
            out_ref[own] = (total[own] + flow_ref[...].astype(F32)).astype(BF16)


def project(place, own, other, own_weight, other_weight, out_grad):
    rows, width = own.shape
    dim = own_weight.shape[1]
    tile = dim // 3
    whole = pl.BlockSpec((rows, width), lambda i, p: (0, 0))
    columns = lambda size: pl.BlockSpec((size, tile), lambda i, p: (0, i))
    return pl.pallas_call(
        project_kernel,
        grid_spec=pltpu.PrefetchScalarGridSpec(
            num_scalar_prefetch=1,
            grid=(dim // tile,),
            in_specs=[whole, whole, columns(width), columns(width), columns(out_grad.shape[0])],
            out_specs=columns(rows),
        ),
        out_shape=jax.ShapeDtypeStruct((rows, dim), BF16),
        compiler_params=pltpu.CompilerParams(vmem_limit_bytes=VMEM_LIMIT),
        cost_estimate=call_cost(4 * rows * width * dim, 4 * (rows + dim) * width + 2 * rows * dim),
        name="project",
    )(place, own, other, own_weight, other_weight, out_grad)


def slot_picker(names, own, capacity):
    count, tokens = own.shape
    match = [(names[k : k + 1] == own) for k in range(names.shape[0])]
    named = functools.reduce(jnp.logical_or, match)
    source = lax.broadcasted_iota(jnp.int32, (tokens, tokens), 0)
    target = lax.broadcasted_iota(jnp.int32, (tokens, tokens), 1)
    earlier = (source < target).astype(BF16)
    rank = jnp.dot(named.astype(BF16), earlier, preferred_element_type=F32).astype(jnp.int32)
    rank = jnp.where(named, rank, -1)
    slot = lax.broadcasted_iota(jnp.int32, (count, capacity, tokens), 1)
    picker = (rank[:, None, :] == slot).astype(F32)
    return picker, match


def pick_norm_kernel(per_token, capacity, n_exp, turns, place_ref, rows_ref, *out_refs):
    tokens = rows_ref.shape[1]
    dim = out_refs[0].shape[3]
    names = rows_ref[0, :, dim:].astype(F32).T[:per_token].astype(jnp.int32)
    own = jnp.concatenate(
        [jnp.full((1, tokens), (place_ref[0] ^ t) * n_exp + place_ref[1], jnp.int32) for t in turns]
    )
    picker, _ = slot_picker(names, own, capacity)
    picker = picker.reshape(len(turns) * capacity, tokens).astype(BF16)
    picked = jnp.dot(picker, rows_ref[0, :, :dim], preferred_element_type=F32).astype(BF16)
    for index in range(len(turns)):
        out_refs[index // 2][index % 2, 0] = picked[index * capacity : (index + 1) * capacity]


def pick_norm(place, rows, turns, first, count, dim, per_token, capacity):
    blocks, tokens, width = rows.shape
    outs = len(turns) // 2
    return pl.pallas_call(
        functools.partial(pick_norm_kernel, per_token, capacity, blocks, turns),
        grid_spec=pltpu.PrefetchScalarGridSpec(
            num_scalar_prefetch=1,
            grid=(count,),
            in_specs=[pl.BlockSpec((1, tokens, width), lambda i, p: (p[1] ^ (i + first), 0, 0))],
            out_specs=[pl.BlockSpec((2, 1, capacity, dim), lambda i, p: (0, i, 0, 0))] * outs,
        ),
        out_shape=[jax.ShapeDtypeStruct((2, count, capacity, dim), BF16)] * outs,
        compiler_params=pltpu.CompilerParams(vmem_limit_bytes=VMEM_LIMIT),
        cost_estimate=call_cost(
            2 * len(turns) * capacity * count * tokens * dim,
            2 * dim * count * (tokens + len(turns) * capacity),
        ),
        name="pick_norm",
    )(place, rows)


def pick_grad_kernel(per_token, capacity, n_exp, turns, place_ref, *refs):
    out_ref = refs[-1]
    tokens = refs[0].shape[2]
    own = jnp.concatenate(
        [jnp.full((1, tokens), place_ref[0] * n_exp + (place_ref[1] ^ t), jnp.int32) for t in turns]
    )
    for core in range(2):
        table_ref, rows_ref = refs[2 * core : 2 * core + 2]
        names = table_ref[0, :per_token].astype(jnp.int32)
        picker, match = slot_picker(names, own, capacity)
        weights = table_ref[0, per_token:]
        scale = functools.reduce(
            jnp.add, [jnp.where(match[k], weights[k : k + 1], 0.0) for k in range(per_token)]
        )
        scales = jnp.sum(picker * scale[:, None, :], axis=2, keepdims=True)
        picker = picker.reshape(len(turns) * capacity, tokens).astype(BF16)
        picked = jnp.dot(picker, rows_ref[...], preferred_element_type=F32)
        picked = (picked * scales.reshape(len(turns) * capacity, 1)).astype(BF16)
        for index in range(len(turns)):
            out_ref[index, core * capacity : (core + 1) * capacity] = picked[
                index * capacity : (index + 1) * capacity
            ]


def pick_grad(place, tables, flows, turns, quarter, n_exp, per_token, capacity):
    tokens = tables.shape[2]
    dim = flows[0].shape[1]
    table_spec = lambda core: pl.BlockSpec(
        (1, 2 * per_token, tokens), lambda i, p: (p[0] ^ (2 * quarter + core), 0, 0)
    )
    flow_spec = pl.BlockSpec((tokens, dim), lambda i, p: ((p[0] >> 1) ^ quarter, 0))
    shape = (len(turns), 2 * capacity, dim)
    return pl.pallas_call(
        functools.partial(pick_grad_kernel, per_token, capacity, n_exp, turns),
        grid_spec=pltpu.PrefetchScalarGridSpec(
            num_scalar_prefetch=1,
            grid=(1,),
            in_specs=[table_spec(0), flow_spec, table_spec(1), flow_spec],
            out_specs=pl.BlockSpec(shape, lambda i, p: (0, 0, 0)),
        ),
        out_shape=jax.ShapeDtypeStruct(shape, BF16),
        compiler_params=pltpu.CompilerParams(vmem_limit_bytes=VMEM_LIMIT),
        cost_estimate=call_cost(
            4 * len(turns) * capacity * tokens * dim,
            4 * dim * (tokens + len(turns) * capacity),
        ),
        name="pick_grad",
    )(place, tables, flows[0], tables, flows[1])


def forward_kernel(sources, *refs):
    row_refs = refs[:sources]
    weight_ref = refs[sources]
    rows_out, act_ref, gate_ref, up_ref = refs[-4:]
    _, pair, capacity, _ = row_refs[0].shape
    for inner in range(pair):
        for index in range(sources):
            at = (inner * sources + index) * capacity
            rows_out[at : at + capacity] = row_refs[index][0, inner]
    hidden = act_ref.shape[1]
    mixed = jnp.dot(rows_out[...], weight_ref[...], preferred_element_type=F32)
    gate = mixed[:, :hidden]
    up = mixed[:, hidden:]
    sig = jax.nn.sigmoid(gate)
    silu = gate * sig
    act_ref[...] = (silu * up).astype(BF16)
    gate_ref[...] = up * sig * (1.0 + gate * (1.0 - sig))
    up_ref[...] = silu


def expert_forward(pieces, weight, hidden, parts, part, before):
    sources = len(pieces)
    _, blocks, capacity, dim = pieces[0][0].shape
    pair = 2
    tile = sources * pair * capacity
    steps = blocks // pair
    total = sources * blocks * capacity * parts
    row_spec = lambda width: pl.BlockSpec((tile, width), lambda i: (i + part * steps, 0))
    piece_spec = lambda unit: pl.BlockSpec(
        (1, pair, capacity, dim), lambda i: (unit, i, 0, 0)
    )
    return pl.pallas_call(
        functools.partial(forward_kernel, sources),
        grid=(steps,),
        in_specs=[piece_spec(unit) for _, unit in pieces]
        + [pl.BlockSpec((dim, 2 * hidden), lambda i: (0, 0))]
        + [pl.BlockSpec(memory_space=pl.ANY)] * len(before),
        out_specs=[row_spec(dim), row_spec(hidden), row_spec(hidden), row_spec(hidden)],
        out_shape=[
            jax.ShapeDtypeStruct((total, dim), BF16),
            jax.ShapeDtypeStruct((total, hidden), BF16),
            jax.ShapeDtypeStruct((total, hidden), F32),
            jax.ShapeDtypeStruct((total, hidden), F32),
        ],
        input_output_aliases={sources + 1 + i: i for i in range(len(before))},
        compiler_params=pltpu.CompilerParams(vmem_limit_bytes=VMEM_LIMIT),
        cost_estimate=call_cost(
            4 * total * dim * hidden // parts, (4 * total * dim + 10 * total * hidden) // parts
        ),
        name="expert_forward",
    )(*[array for array, _ in pieces], weight, *before)


def backward_kernel(places, arrays, *refs):
    grad_refs = refs[:arrays]
    gate_ref, up_ref, weight_ref, rows_ref, act_ref, out_ref = refs[arrays : arrays + 6]
    grads_all, hidden_all, sems = refs[arrays + 6 :]
    step = pl.program_id(0)
    tile = gate_ref.shape[0]
    hidden = act_ref.shape[1]
    width = rows_ref.shape[1]
    row_steps = grads_all.shape[0] // tile
    copies = []
    for index, (array, unit, row, size) in enumerate(places):
        copy = pltpu.make_async_copy(
            grad_refs[array].at[unit], grads_all.at[pl.ds(row, size)], sems.at[index]
        )
        copies.append((row // tile, copy))

    @pl.when(step == 0)
    def _():
        for turn in range(row_steps):
            for at, copy in copies:
                if at == turn:
                    copy.start()

    for turn in range(row_steps):

        @pl.when(step == turn)
        def _():
            for at, copy in copies:
                if at == turn:
                    copy.wait()

    @pl.when(step < row_steps)
    def _():
        where = pl.ds(pl.multiple_of(step * tile, tile), tile)
        act_grad = jnp.dot(grads_all[where], weight_ref[...], preferred_element_type=F32)
        hidden_all[where, :hidden] = (act_grad * gate_ref[...]).astype(BF16)
        hidden_all[where, hidden:] = (act_grad * up_ref[...]).astype(BF16)

    @pl.when(step >= row_steps)
    def _():
        columns = pl.ds(pl.multiple_of((step - row_steps) * width, width), width)
        over_rows = (((0,), (0,)), ((), ()))
        out_ref[:, : 2 * hidden] = lax.dot_general(
            rows_ref[...], hidden_all[...], over_rows, preferred_element_type=F32
        ).astype(BF16)
        out_ref[:, 2 * hidden :] = lax.dot_general(
            grads_all[:, columns], act_ref[...], over_rows, preferred_element_type=F32
        ).astype(BF16)


def expert_backward(arrays, places, gate, up, weights, rows, act):
    total, dim = rows.shape
    hidden = act.shape[1]
    tile, width = 256, 256
    row_steps, column_steps = total // tile, dim // width
    row_spec = lambda cols: pl.BlockSpec(
        (tile, cols), lambda i: (jnp.minimum(i, row_steps - 1), 0)
    )
    column_of = lambda i: jnp.maximum(i - row_steps, 0)
    return pl.pallas_call(
        functools.partial(backward_kernel, places, len(arrays)),
        grid=(row_steps + column_steps,),
        in_specs=[pl.BlockSpec(memory_space=pl.ANY)] * len(arrays)
        + [
            row_spec(hidden),
            row_spec(hidden),
            pl.BlockSpec((dim, hidden), lambda i: (0, 2)),
            pl.BlockSpec((total, width), lambda i: (0, column_of(i))),
            pl.BlockSpec((total, hidden), lambda i: (0, 0)),
        ],
        out_specs=pl.BlockSpec((width, 3 * hidden), lambda i: (column_of(i), 0)),
        out_shape=jax.ShapeDtypeStruct((dim, 3 * hidden), BF16),
        scratch_shapes=[
            pltpu.VMEM((total, dim), BF16),
            pltpu.VMEM((total, 2 * hidden), BF16),
            pltpu.SemaphoreType.DMA((len(places),)),
        ],
        compiler_params=pltpu.CompilerParams(vmem_limit_bytes=VMEM_LIMIT),
        cost_estimate=call_cost(8 * total * dim * hidden, 4 * total * dim + 20 * total * hidden),
        name="expert_backward",
    )(*arrays, gate, up, weights, rows, act)


def swap(array, axis, flip):
    count = lax.axis_size(axis)
    return lax.ppermute(array, axis, [(i, i ^ flip) for i in range(count)])


def swap_gather(array, axis, flip):
    count, index = lax.axis_size(axis), lax.axis_index(axis)
    groups = [[i, i ^ flip] for i in range(count) if i < i ^ flip]
    both = lax.all_gather(array, axis, axis_index_groups=groups)
    other = (index < (index ^ flip)).astype(jnp.int32)
    return lax.dynamic_index_in_dim(both, other, 0, keepdims=False)


def mask_of(flips, bits):
    return functools.reduce(lambda a, b: a ^ b, [f for f, bit in zip(flips, bits) if bit], 0)


def exchange_rows(half, picks, exchange):
    keep, send, keep_far, send_far = picks
    flips = (1, 3) if half == 0 else (3, 1)
    send_got, keep_got = swap(send_far, "seq", 1), swap(keep_far, "seq", 1)
    first = exchange(jnp.concatenate([send, send_got]), "seq", 2 * flips[0])
    second = exchange(
        jnp.concatenate([keep[1:], keep_got[1:], first[1:2], first[3:4]]), "seq", 2 * flips[1]
    )
    found = {
        0: [(keep, 0), (keep_got, 0)],
        flips[0]: [(first, 0), (first, 2)],
        flips[1]: [(second, 0), (second, 1)],
        flips[0] ^ flips[1]: [(second, 2), (second, 3)],
    }
    return [found[r >> 1][r & 1] for r in range(8)]


def exchange_grads(flips, keep, send):
    first = swap(send, "exp", flips[0])
    second = swap(jnp.concatenate([keep[4:8], first[4:8]]), "exp", flips[1])
    third = swap(
        jnp.concatenate([keep[2:4], first[2:4], second[2:4], second[6:8]]), "exp", flips[2]
    )
    odd = lambda a: [a[i : i + 1] for i in (1, 3, 5, 7)]
    fourth = swap(
        jnp.concatenate(
            [keep[1:2], first[1:2], second[1:2], second[5:6]] + odd(third)
        ),
        "exp",
        flips[3],
    )
    arrays = [keep, first, second, third, fourth]
    found = {}
    found[0, 0, 0, 0] = (0, 0)
    found[1, 0, 0, 0] = (1, 0)
    found[0, 1, 0, 0] = (2, 0)
    found[1, 1, 0, 0] = (2, 4)
    for index, start in enumerate([(0, 0), (1, 0), (0, 1), (1, 1)]):
        found[start + (1, 0)] = (3, 2 * index)
    for index, start in enumerate([(0, 0), (1, 0), (0, 1), (1, 1)]):
        found[start + (0, 1)] = (4, index)
        found[start + (1, 1)] = (4, 4 + index)
    return arrays, {mask_of(flips, bits): at for bits, at in found.items()}


def per_device(
    qkv_in,
    qkv_grad,
    conv_weight,
    doc_ids,
    qkv_weight,
    resid,
    norm_gain,
    out_grad,
    routes,
    route_weights,
    expert_weights,
):
    rows, width = qkv_in.shape
    tokens, dim = resid.shape
    per_token = routes.shape[1]
    hidden = expert_weights.shape[2] // 3
    n_seq, n_exp = lax.axis_size("seq"), lax.axis_size("exp")
    experts = n_seq * n_exp
    capacity = 2 * tokens * per_token // experts
    seq_index, exp_index = lax.axis_index("seq"), lax.axis_index("exp")
    own_weights = expert_weights[0]

    place = jnp.stack([seq_index, exp_index]).astype(jnp.int32)
    normed = norm_rows(resid, norm_gain, routes)
    normed, qkv_grad = lax.optimization_barrier((normed, qkv_grad))
    exp_normed = lax.all_gather(normed, "exp")

    forward = [(i, i + 1) for i in range(n_exp - 1)]
    backward = [(i + 1, i) for i in range(n_exp - 1)]
    low = lax.ppermute(qkv_in[-HALO:], "exp", forward)
    high = lax.ppermute(qkv_in[:HALO], "exp", backward)
    grad_high = lax.ppermute(qkv_grad[:HALO], "exp", backward)
    weight_far = swap(qkv_weight, "seq", 1)

    table = jnp.concatenate([routes.astype(F32), route_weights], 1).T
    tables = jnp.broadcast_to(table[None], (n_seq,) + table.shape)
    tables = lax.all_to_all(tables, "seq", split_axis=0, concat_axis=0, tiled=True)

    edge = jnp.full((HALO,), -1, jnp.int32)
    ids = lax.dynamic_slice_in_dim(
        jnp.concatenate([edge, doc_ids, edge]), exp_index * rows, rows + 2 * HALO
    )
    local_grad, local_keep, local_send = conv_back(
        place, qkv_in, low, high, qkv_grad, grad_high, ids.reshape(-1, 1), conv_weight, tokens
    )
    local_got = swap(local_send, "seq", 1)
    partial = project(place, local_keep, local_got, qkv_weight, weight_far, out_grad)
    same_core = [[s for s in range(n_seq) if s % 2 == core] for core in range(2)]
    flow = lax.psum(partial, "seq", axis_index_groups=same_core)
    flow, local_grad = lax.optimization_barrier((flow, local_grad))
    flow_far = swap(flow, "seq", 1)
    qkv_in_grad = lax.all_to_all(local_grad, "seq", split_axis=0, concat_axis=1, tiled=True)

    halves = []
    for half in range(2):
        near = (0, 3, 1, 2) if half == 0 else (0, 1, 3, 2)
        turns = tuple(2 * m for m in near) + tuple(2 * m + 1 for m in near)
        picks = pick_norm(
            place, exp_normed, turns, half * n_exp // 2, n_exp // 2, dim, per_token, capacity
        )
        halves.append(exchange_rows(half, picks, swap if half == 0 else swap_gather))
    results = ()
    for half in range(2):
        results = expert_forward(halves[half], own_weights, hidden, 2, half, results)
    rows_all, act, gate, up = results

    flips = (1, 3, 4, 12)
    quarters = len(flips)
    orders = [flips[k:] + flips[:k] for k in range(quarters)]
    bit_rows = [tuple((j >> (2 - b)) & 1 for b in range(3)) for j in range(8)]
    turns_of = lambda k, bit: tuple(mask_of(orders[k], (bit,) + bits) for bits in bit_rows)
    picks = [
        [
            pick_grad(
                place, tables, (flow, flow_far), turns_of(k, bit), k, n_exp, per_token, capacity
            )
            for k in range(quarters)
        ]
        for bit in (1, 0)
    ]
    arrays, places = [], []
    for k in range(quarters):
        got, found = exchange_grads(orders[k], picks[1][k], picks[0][k])
        size = 2 * capacity
        for mask, (array, unit) in sorted(found.items()):
            row = mask * n_seq * capacity + k * size
            places.append((len(arrays) + array, unit, row, size))
        arrays += got
    expert_grads = expert_backward(arrays, tuple(places), gate, up, own_weights, rows_all, act)
    return (qkv_in_grad, expert_grads[None])


def solution(mesh):
    return jax.shard_map(
        per_device,
        mesh=mesh,
        in_specs=(
            P("exp", "seq"),
            P("exp", "seq"),
            P(None, "seq"),
            P(),
            P("seq", None),
            P(("exp", "seq"), None),
            P(),
            P(("exp", "seq"), None),
            P(("exp", "seq"), None),
            P(("exp", "seq"), None),
            P(("seq", "exp"), None, None),
        ),
        out_specs=(P(("exp", "seq"), None), P(("seq", "exp"), None, None)),
        check_vma=False,
    )
```

```python
import functools

import jax
import jax.numpy as jnp
from jax import lax
from jax.experimental import pallas as pl
from jax.experimental.pallas import tpu as pltpu
from jax.sharding import PartitionSpec as P

BF16 = jnp.bfloat16
F32 = jnp.float32
HALO = 16
MIB = 1024 * 1024
VMEM_LIMIT = 60 * MIB
EXTRA = 128


def call_cost(flops, nbytes):
    return pl.CostEstimate(flops=int(flops), bytes_accessed=int(nbytes), transcendentals=0)


def norm_kernel(resid_ref, gain_ref, routes_ref, out_ref):
    rows = resid_ref[...].astype(F32)
    dim = rows.shape[1]
    scale = lax.rsqrt(jnp.mean(rows * rows, axis=1, keepdims=True) + 1e-06)
    out_ref[:, :dim] = (rows * scale * gain_ref[...]).astype(BF16)
    out_ref[:, dim:] = jnp.zeros((rows.shape[0], EXTRA), BF16)
    names = routes_ref[...].astype(F32)
    pad = jnp.zeros((HALO - names.shape[0], EXTRA), F32)
    out_ref[:HALO, dim:] = jnp.concatenate([names, pad]).astype(BF16)


def norm_rows(resid, gain, names):
    tokens, dim = resid.shape
    return pl.pallas_call(
        norm_kernel,
        out_shape=jax.ShapeDtypeStruct((tokens, dim + EXTRA), BF16),
        compiler_params=pltpu.CompilerParams(vmem_limit_bytes=VMEM_LIMIT),
        cost_estimate=call_cost(resid.size * 6, resid.size * 4),
        name="norm_rows",
    )(resid, gain.reshape(1, -1), names)


def conv_kernel(
    tile,
    place_ref,
    in_ref,
    in_low_ref,
    in_high_ref,
    grad_ref,
    grad_high_ref,
    ids_ref,
    taps_ref,
    local_ref,
    keep_ref,
    send_ref,
    in_ext,
    grad_ext,
):
    step = pl.program_id(0)
    rows = in_ref.shape[0]

    @pl.when(step == 0)
    def _():
        in_ext[:HALO] = in_low_ref[...].astype(F32)
        in_ext[HALO : HALO + rows] = in_ref[...].astype(F32)
        in_ext[HALO + rows :] = in_high_ref[...].astype(F32)
        grad_ext[:rows] = grad_ref[...].astype(F32)
        grad_ext[rows:] = grad_high_ref[...].astype(F32)

    first = pl.multiple_of(step * tile, tile)
    span = tile + 8
    taps = taps_ref[...]
    window = in_ext[pl.ds(first + HALO - 8, span + 8)]
    ids = ids_ref[pl.ds(first + HALO - 8, span + 8)]
    here = ids[8:]
    same = [None] + [(ids[8 - j : 8 - j + span] == here).astype(F32) for j in (1, 2, 3)]
    conv = taps[0:1] * window[8:]
    for j in (1, 2, 3):
        conv = conv + taps[j : j + 1] * window[8 - j : 8 - j + span] * same[j]
    gate = jax.nn.sigmoid(conv)
    pre = grad_ext[pl.ds(first, span)] * gate * (1.0 + conv * (1.0 - gate))
    result = taps[0:1] * pre[:tile]
    for j in (1, 2, 3):
        result = result + taps[j : j + 1] * (pre * same[j])[j : j + tile]
    local = result.astype(BF16)
    local_ref[...] = local
    half = tile // 2
    core = place_ref[0] & 1

    @pl.when(core == 0)
    def _():
        keep_ref[...] = local[:half]
        send_ref[...] = local[half:]

    @pl.when(core == 1)
    def _():
        keep_ref[...] = local[half:]
        send_ref[...] = local[:half]


def conv_back(place, qkv_in, low, high, qkv_grad, grad_high, ids, taps, block):
    rows, width = qkv_in.shape
    tile = 2 * block
    whole = lambda shape: pl.BlockSpec(shape, lambda i, p: (0,) * len(shape))
    part = lambda size: pl.BlockSpec((size, width), lambda i, p: (i, 0))
    return pl.pallas_call(
        functools.partial(conv_kernel, tile),
        grid_spec=pltpu.PrefetchScalarGridSpec(
            num_scalar_prefetch=1,
            grid=(rows // tile,),
            in_specs=[
                whole(qkv_in.shape),
                whole(low.shape),
                whole(high.shape),
                whole(qkv_grad.shape),
                whole(grad_high.shape),
                whole(ids.shape),
                whole(taps.shape),
            ],
            out_specs=[part(tile), part(block), part(block)],
            scratch_shapes=[
                pltpu.VMEM((rows + 2 * HALO, width), F32),
                pltpu.VMEM((rows + HALO, width), F32),
            ],
        ),
        out_shape=[
            jax.ShapeDtypeStruct((rows, width), BF16),
            jax.ShapeDtypeStruct((rows // 2, width), BF16),
            jax.ShapeDtypeStruct((rows // 2, width), BF16),
        ],
        compiler_params=pltpu.CompilerParams(vmem_limit_bytes=VMEM_LIMIT),
        cost_estimate=call_cost(40 * rows * width, 8 * rows * width),
        name="conv_back",
    )(place, qkv_in, low, high, qkv_grad, grad_high, ids, taps)


def project_kernel(place_ref, own_ref, other_ref, own_weight, other_weight, flow_ref, out_ref):
    block = flow_ref.shape[0]
    total = jnp.dot(own_ref[...], own_weight[...], preferred_element_type=F32)
    total = total + jnp.dot(other_ref[...], other_weight[...], preferred_element_type=F32)
    out_ref[...] = total.astype(BF16)
    for index in range(out_ref.shape[0] // block):

        @pl.when(index == place_ref[0] >> 1)
        def _():
            own = slice(index * block, (index + 1) * block)
            out_ref[own] = (total[own] + flow_ref[...].astype(F32)).astype(BF16)


def project(place, own, other, own_weight, other_weight, out_grad):
    rows, width = own.shape
    dim = own_weight.shape[1]
    tile = dim // 3
    whole = pl.BlockSpec((rows, width), lambda i, p: (0, 0))
    columns = lambda size: pl.BlockSpec((size, tile), lambda i, p: (0, i))
    return pl.pallas_call(
        project_kernel,
        grid_spec=pltpu.PrefetchScalarGridSpec(
            num_scalar_prefetch=1,
            grid=(dim // tile,),
            in_specs=[whole, whole, columns(width), columns(width), columns(out_grad.shape[0])],
            out_specs=columns(rows),
        ),
        out_shape=jax.ShapeDtypeStruct((rows, dim), BF16),
        compiler_params=pltpu.CompilerParams(vmem_limit_bytes=VMEM_LIMIT),
        cost_estimate=call_cost(4 * rows * width * dim, 4 * (rows + dim) * width + 2 * rows * dim),
        name="project",
    )(place, own, other, own_weight, other_weight, out_grad)


def slot_picker(names, own, capacity):
    count, tokens = own.shape
    match = [(names[k : k + 1] == own) for k in range(names.shape[0])]
    named = functools.reduce(jnp.logical_or, match)
    source = lax.broadcasted_iota(jnp.int32, (tokens, tokens), 0)
    target = lax.broadcasted_iota(jnp.int32, (tokens, tokens), 1)
    earlier = (source < target).astype(BF16)
    rank = jnp.dot(named.astype(BF16), earlier, preferred_element_type=F32).astype(jnp.int32)
    rank = jnp.where(named, rank, -1)
    slot = lax.broadcasted_iota(jnp.int32, (count, capacity, tokens), 1)
    picker = (rank[:, None, :] == slot).astype(F32)
    return picker, match


def pick_norm_kernel(per_token, capacity, n_exp, turns, place_ref, rows_ref, *out_refs):
    tokens = rows_ref.shape[1]
    dim = out_refs[0].shape[3]
    names = rows_ref[0, :HALO, dim:].astype(F32)[:per_token].astype(jnp.int32)
    own = jnp.concatenate(
        [jnp.full((1, tokens), (place_ref[0] ^ t) * n_exp + place_ref[1], jnp.int32) for t in turns]
    )
    picker, _ = slot_picker(names, own, capacity)
    picker = picker.reshape(len(turns) * capacity, tokens).astype(BF16)
    picked = jnp.dot(picker, rows_ref[0, :, :dim], preferred_element_type=F32).astype(BF16)
    for index in range(len(turns)):
        out_refs[index // 2][index % 2, 0] = picked[index * capacity : (index + 1) * capacity]


def pick_norm(place, rows, turns, first, count, dim, per_token, capacity):
    blocks, tokens, width = rows.shape
    outs = len(turns) // 2
    return pl.pallas_call(
        functools.partial(pick_norm_kernel, per_token, capacity, blocks, turns),
        grid_spec=pltpu.PrefetchScalarGridSpec(
            num_scalar_prefetch=1,
            grid=(count,),
            in_specs=[pl.BlockSpec((1, tokens, width), lambda i, p: (p[1] ^ (i + first), 0, 0))],
            out_specs=[pl.BlockSpec((2, 1, capacity, dim), lambda i, p: (0, i, 0, 0))] * outs,
        ),
        out_shape=[jax.ShapeDtypeStruct((2, count, capacity, dim), BF16)] * outs,
        compiler_params=pltpu.CompilerParams(vmem_limit_bytes=VMEM_LIMIT),
        cost_estimate=call_cost(
            2 * len(turns) * capacity * count * tokens * dim,
            2 * dim * count * (tokens + len(turns) * capacity),
        ),
        name="pick_norm",
    )(place, rows)


def pick_grad_kernel(per_token, capacity, n_exp, turns, place_ref, tables_ref, *refs):
    flow_refs, out_refs = refs[:2], refs[2:-2]
    buffer, sems = refs[-2:]
    tokens = tables_ref.shape[2]
    copies = []
    for quarter, turn in enumerate(turns):
        count = len(turn)
        own = jnp.concatenate(
            [
                jnp.full((1, tokens), place_ref[0] * n_exp + (place_ref[1] ^ t), jnp.int32)
                for t in turn
            ]
        )
        first = pl.multiple_of(((place_ref[0] >> 1) ^ quarter) * tokens, tokens)
        for core in range(2):
            table = tables_ref[place_ref[0] ^ (2 * quarter + core)]
            names = table[:per_token].astype(jnp.int32)
            picker, match = slot_picker(names, own, capacity)
            weights = table[per_token:]
            scale = functools.reduce(
                jnp.add, [jnp.where(match[k], weights[k : k + 1], 0.0) for k in range(per_token)]
            )
            scales = jnp.sum(picker * scale[:, None, :], axis=2, keepdims=True)
            picker = picker.reshape(count * capacity, tokens).astype(BF16)
            picked = jnp.dot(
                picker, flow_refs[core][pl.ds(first, tokens)], preferred_element_type=F32
            )
            picked = (picked * scales.reshape(count * capacity, 1)).astype(BF16)
            for index in range(count):
                buffer[quarter, index, core * capacity : (core + 1) * capacity] = picked[
                    index * capacity : (index + 1) * capacity
                ]
        for part in range(2):
            at = 2 * quarter + part
            copy = pltpu.make_async_copy(
                buffer.at[quarter, pl.ds(part * count // 2, count // 2)],
                out_refs[at],
                sems.at[at],
            )
            copy.start()
            copies.append(copy)
    for copy in copies:
        copy.wait()


def pick_grad(place, tables, flows, turns, n_exp, per_token, capacity):
    dim = flows[0].shape[1]
    rows, count = 2 * capacity, len(turns[0])
    whole = lambda array: pl.BlockSpec(array.shape, lambda i, p: (0,) * array.ndim)
    outs = 2 * len(turns)
    return pl.pallas_call(
        functools.partial(pick_grad_kernel, per_token, capacity, n_exp, turns),
        grid_spec=pltpu.PrefetchScalarGridSpec(
            num_scalar_prefetch=1,
            grid=(1,),
            in_specs=[whole(tables), whole(flows[0]), whole(flows[1])],
            out_specs=[pl.BlockSpec(memory_space=pl.ANY)] * outs,
            scratch_shapes=[
                pltpu.VMEM((len(turns), count, rows, dim), BF16),
                pltpu.SemaphoreType.DMA((outs,)),
            ],
        ),
        out_shape=[jax.ShapeDtypeStruct((count // 2, rows, dim), BF16)] * outs,
        compiler_params=pltpu.CompilerParams(vmem_limit_bytes=VMEM_LIMIT),
        cost_estimate=call_cost(
            2 * len(turns) * count * rows * tables.shape[2] * dim,
            4 * dim * (flows[0].shape[0] + len(turns) * count * rows // 2),
        ),
        name="pick_grad",
    )(place, tables, *flows)


def forward_kernel(sources, *refs):
    row_refs = refs[1 : 1 + sources]
    weight_ref = refs[1 + sources]
    rows_out, act_ref, gate_ref, up_ref, rows = refs[-5:]
    _, group, capacity, _ = row_refs[0].shape
    for inner in range(group):
        for index in range(sources):
            at = (inner * sources + index) * capacity
            rows[at : at + capacity] = row_refs[index][0, inner]
    hidden = act_ref.shape[0]
    mixed = jnp.dot(rows[...], weight_ref[...], preferred_element_type=F32)
    rows_out[...] = rows[...].T
    gate = mixed[:, :hidden]
    up = mixed[:, hidden:]
    sig = jax.nn.sigmoid(gate)
    silu = gate * sig
    act_ref[...] = (silu * up).astype(BF16).T
    gate_ref[...] = up * sig * (1.0 + gate * (1.0 - sig))
    up_ref[...] = silu


def expert_forward(pieces, weight, hidden, shifts, parts, part, before):
    sources = len(pieces)
    _, blocks, capacity, dim = pieces[0][0].shape
    group = 16 // sources
    tile = sources * group * capacity
    steps = blocks // group
    total = tile * steps * parts
    at = lambda i: i + part * steps
    row_spec = lambda width: pl.BlockSpec((tile, width), lambda i, p: (at(i), 0))
    column_spec = lambda height: pl.BlockSpec((height, tile), lambda i, p: (0, at(i)))

    def piece_spec(unit, shift):
        return pl.BlockSpec(
            (1, group, capacity, dim),
            lambda i, p: (unit if shift is None else unit + p[shift], i, 0, 0),
        )

    return pl.pallas_call(
        functools.partial(forward_kernel, sources),
        grid_spec=pltpu.PrefetchScalarGridSpec(
            num_scalar_prefetch=1,
            grid=(steps,),
            in_specs=[piece_spec(unit, shift) for _, unit, shift in pieces]
            + [pl.BlockSpec((dim, 2 * hidden), lambda i, p: (0, 0))]
            + [pl.BlockSpec(memory_space=pl.ANY)] * len(before),
            out_specs=[column_spec(dim), column_spec(hidden), row_spec(hidden), row_spec(hidden)],
            scratch_shapes=[pltpu.VMEM((tile, dim), BF16)],
        ),
        out_shape=[
            jax.ShapeDtypeStruct((dim, total), BF16),
            jax.ShapeDtypeStruct((hidden, total), BF16),
            jax.ShapeDtypeStruct((total, hidden), F32),
            jax.ShapeDtypeStruct((total, hidden), F32),
        ],
        input_output_aliases={sources + 2 + i: i for i in range(len(before))},
        compiler_params=pltpu.CompilerParams(vmem_limit_bytes=VMEM_LIMIT),
        cost_estimate=call_cost(
            4 * total * dim * hidden // parts, (4 * total * dim + 10 * total * hidden) // parts
        ),
        name="expert_forward",
    )(shifts, *[array for array, _, _ in pieces], weight, *before)


def backward_kernel(places, arrays, *refs):
    grad_refs = refs[:arrays]
    gate_ref, up_ref, weight_ref, rows_ref, act_ref, out_ref = refs[arrays : arrays + 6]
    grads_all, hidden_all, sems = refs[arrays + 6 :]
    step = pl.program_id(0)
    tile = gate_ref.shape[0]
    hidden = act_ref.shape[0]
    width = rows_ref.shape[0]
    row_steps = grads_all.shape[0] // tile
    copies = []
    for index, (array, unit, row, size) in enumerate(places):
        copy = pltpu.make_async_copy(
            grad_refs[array].at[unit], grads_all.at[pl.ds(row, size)], sems.at[index]
        )
        copies.append((row // tile, copy))

    @pl.when(step == 0)
    def _():
        for turn in range(row_steps):
            for at, copy in copies:
                if at == turn:
                    copy.start()

    for turn in range(row_steps):

        @pl.when(step == turn)
        def _():
            for at, copy in copies:
                if at == turn:
                    copy.wait()

    @pl.when(step < row_steps)
    def _():
        where = pl.ds(pl.multiple_of(step * tile, tile), tile)
        act_grad = jnp.dot(grads_all[where], weight_ref[...], preferred_element_type=F32)
        hidden_all[where, :hidden] = (act_grad * gate_ref[...]).astype(BF16)
        hidden_all[where, hidden:] = (act_grad * up_ref[...]).astype(BF16)

    @pl.when(step >= row_steps)
    def _():
        columns = pl.ds(pl.multiple_of((step - row_steps) * width, width), width)
        out_ref[:, : 2 * hidden] = jnp.dot(
            rows_ref[...], hidden_all[...], preferred_element_type=F32
        ).astype(BF16)
        down = jnp.dot(act_ref[...], grads_all[:, columns], preferred_element_type=F32)
        out_ref[:, 2 * hidden :] = down.T.astype(BF16)


def expert_backward(arrays, places, gate, up, weights, rows, act):
    dim, total = rows.shape
    hidden = act.shape[0]
    tile, width = 256, 256
    row_steps, column_steps = total // tile, dim // width
    row_spec = lambda cols: pl.BlockSpec(
        (tile, cols), lambda i: (jnp.minimum(i, row_steps - 1), 0)
    )
    column_of = lambda i: jnp.maximum(i - row_steps, 0)
    return pl.pallas_call(
        functools.partial(backward_kernel, places, len(arrays)),
        grid=(row_steps + column_steps,),
        in_specs=[pl.BlockSpec(memory_space=pl.ANY)] * len(arrays)
        + [
            row_spec(hidden),
            row_spec(hidden),
            pl.BlockSpec((dim, hidden), lambda i: (0, 2)),
            pl.BlockSpec((width, total), lambda i: (column_of(i), 0)),
            pl.BlockSpec((hidden, total), lambda i: (0, 0)),
        ],
        out_specs=pl.BlockSpec((width, 3 * hidden), lambda i: (column_of(i), 0)),
        out_shape=jax.ShapeDtypeStruct((dim, 3 * hidden), BF16),
        scratch_shapes=[
            pltpu.VMEM((total, dim), BF16),
            pltpu.VMEM((total, 2 * hidden), BF16),
            pltpu.SemaphoreType.DMA((len(places),)),
        ],
        compiler_params=pltpu.CompilerParams(vmem_limit_bytes=VMEM_LIMIT),
        cost_estimate=call_cost(8 * total * dim * hidden, 4 * total * dim + 20 * total * hidden),
        name="expert_backward",
    )(*arrays, gate, up, weights, rows, act)


def swap(array, axis, flip):
    count = lax.axis_size(axis)
    return lax.ppermute(array, axis, [(i, i ^ flip) for i in range(count)])


def mask_of(flips, bits):
    return functools.reduce(lambda a, b: a ^ b, [f for f, bit in zip(flips, bits) if bit], 0)


def flips_of(half):
    return (1, 3) if half == 0 else (3, 1)


def sibling_rows(picks):
    keep, send, keep_far, send_far = picks
    send_got, keep_got = swap(send_far, "seq", 1), swap(keep_far, "seq", 1)
    return keep, keep_got, jnp.concatenate([send, send_got])


def swap_gather(array, axis, flip):
    count = lax.axis_size(axis)
    groups = [[i, i ^ flip] for i in range(count) if i < i ^ flip]
    both = lax.all_gather(array, axis, axis_index_groups=groups)
    return both.reshape((-1,) + array.shape[1:])


def exchange_grads(flips, keep, send):
    first = swap(send, "exp", flips[0])
    second = swap(jnp.concatenate([keep[4:8], first[4:8]]), "exp", flips[1])
    return keep, first, second


def finish_grads(flips, keep, first, second):
    third = swap(
        jnp.concatenate([keep[2:4], first[2:4], second[2:4], second[6:8]]), "exp", flips[2]
    )
    odd = lambda a: [a[i : i + 1] for i in (1, 3, 5, 7)]
    fourth = swap(
        jnp.concatenate([keep[1:2], first[1:2], second[1:2], second[5:6]] + odd(third)),
        "exp",
        flips[3],
    )
    arrays = [keep, first, second, third, fourth]
    found = {}
    found[0, 0, 0, 0] = (0, 0)
    found[1, 0, 0, 0] = (1, 0)
    found[0, 1, 0, 0] = (2, 0)
    found[1, 1, 0, 0] = (2, 4)
    for index, start in enumerate([(0, 0), (1, 0), (0, 1), (1, 1)]):
        found[start + (1, 0)] = (3, 2 * index)
        found[start + (0, 1)] = (4, index)
        found[start + (1, 1)] = (4, 4 + index)
    return arrays, {mask_of(flips, bits): at for bits, at in found.items()}


def per_device(
    qkv_in,
    qkv_grad,
    conv_weight,
    doc_ids,
    qkv_weight,
    resid,
    norm_gain,
    out_grad,
    routes,
    route_weights,
    expert_weights,
):
    rows, width = qkv_in.shape
    tokens, dim = resid.shape
    per_token = routes.shape[1]
    hidden = expert_weights.shape[2] // 3
    n_seq, n_exp = lax.axis_size("seq"), lax.axis_size("exp")
    experts = n_seq * n_exp
    capacity = 2 * tokens * per_token // experts
    seq_index, exp_index = lax.axis_index("seq"), lax.axis_index("exp")
    own_weights = expert_weights[0]

    place = jnp.stack([seq_index, exp_index]).astype(jnp.int32)
    forward = [(i, i + 1) for i in range(n_exp - 1)]
    backward = [(i + 1, i) for i in range(n_exp - 1)]
    low = lax.ppermute(qkv_in[-HALO:], "exp", forward)
    high = lax.ppermute(qkv_in[:HALO], "exp", backward)
    grad_high = lax.ppermute(qkv_grad[:HALO], "exp", backward)
    weight_far = swap(qkv_weight, "seq", 1)

    table = jnp.concatenate([routes.astype(F32), route_weights], 1).T
    tables = jnp.broadcast_to(table[None], (n_seq,) + table.shape)
    tables = lax.all_to_all(tables, "seq", split_axis=0, concat_axis=0, tiled=True)
    normed = norm_rows(resid, norm_gain, routes.T)
    normed, tables, conv_weight = lax.optimization_barrier((normed, tables, conv_weight))
    exp_normed = lax.all_gather(normed, "exp")

    edge = jnp.full((HALO,), -1, jnp.int32)
    ids = lax.dynamic_slice_in_dim(
        jnp.concatenate([edge, doc_ids, edge]), exp_index * rows, rows + 2 * HALO
    )
    local_grad, local_keep, local_send = conv_back(
        place, qkv_in, low, high, qkv_grad, grad_high, ids.reshape(-1, 1), conv_weight, tokens
    )
    local_got = swap(local_send, "seq", 1)
    partial = project(place, local_keep, local_got, qkv_weight, weight_far, out_grad)
    same_core = [[s for s in range(n_seq) if s % 2 == core] for core in range(2)]
    flow = lax.psum(partial, "seq", axis_index_groups=same_core)

    halves = []
    for half in range(2):
        flips = flips_of(half)
        near = (0, flips[1], flips[0], flips[0] ^ flips[1])
        turns = tuple(2 * m for m in near) + tuple(2 * m + 1 for m in near)
        picks = pick_norm(
            place, exp_normed, turns, half * n_exp // 2, n_exp // 2, dim, per_token, capacity
        )
        halves.append(sibling_rows(picks))
    (keep_a, far_a, message_a), (keep_b, far_b, message_b) = halves
    flow, far_a, far_b = lax.optimization_barrier((flow, far_a, far_b))
    flow_far = swap(flow, "seq", 1)

    flips = (1, 3, 4, 12)
    quarters = len(flips)
    orders = [flips[k:] + flips[:k] for k in range(quarters)]
    bit_rows = [tuple((j >> (3 - b)) & 1 for b in range(4)) for j in range(n_exp)]
    turns = tuple(tuple(mask_of(order, bits) for bits in bit_rows) for order in orders)
    sends = pick_grad(place, tables, (flow, flow_far), turns, n_exp, per_token, capacity)

    flips_a, flips_b = flips_of(0), flips_of(1)
    shifts = [(seq_index < seq_index ^ 2 * f).astype(jnp.int32) * 4 for f in flips_b]
    first_a = swap(message_a, "seq", 2 * flips_a[0])
    first_b = swap_gather(message_b, "seq", 2 * flips_b[0])
    states = [
        exchange_grads(orders[k], sends[2 * k], sends[2 * k + 1]) for k in range(quarters)
    ]
    first_a, first_b, states = lax.optimization_barrier((first_a, first_b, states))
    piece = lambda i: lax.dynamic_slice_in_dim(first_b, shifts[0] + i, 1, 0)
    second_a = swap(
        jnp.concatenate([keep_a[1:], far_a[1:], first_a[1:2], first_a[3:4]]),
        "seq",
        2 * flips_a[1],
    )
    second_b = swap_gather(
        jnp.concatenate([keep_b[1:], far_b[1:], piece(1), piece(3)]), "seq", 2 * flips_b[1]
    )
    local_grad, second_a, second_b = lax.optimization_barrier((local_grad, second_a, second_b))
    qkv_in_grad = lax.all_to_all(local_grad, "seq", split_axis=0, concat_axis=1, tiled=True)
    calls = [
        [(keep_a, 0, None), (far_a, 0, None), (first_a, 0, None), (first_a, 2, None)],
        [(keep_b, 0, None), (far_b, 0, None), (first_b, 0, 0), (first_b, 2, 0)],
        [(second_a, i, None) for i in range(4)],
        [(second_b, i, 1) for i in range(4)],
    ]
    results = ()
    for part, pieces in enumerate(calls):
        results = expert_forward(
            pieces, own_weights, hidden, jnp.stack(shifts), len(calls), part, results
        )
    rows_all, act, gate, up = results

    def row_of(mask, quarter):
        half, inner = mask >> 3, mask & 7
        flips = flips_of(half)
        order = (0, flips[0], flips[1], flips[0] ^ flips[1])
        spot = order.index(quarter)
        call = (spot >> 1) * 2 + half
        tile = call * 2 + (inner >> 2)
        return tile * n_exp * capacity + (inner & 3) * 4 * capacity + (spot & 1) * 2 * capacity

    arrays, places = [], []
    for k in range(quarters):
        got, found = finish_grads(orders[k], *states[k])
        for mask, (array, unit) in sorted(found.items()):
            places.append((len(arrays) + array, unit, row_of(mask, k), 2 * capacity))
        arrays += got
    expert_grads = expert_backward(arrays, tuple(places), gate, up, own_weights, rows_all, act)
    return (qkv_in_grad, expert_grads[None])


def solution(mesh):
    return jax.shard_map(
        per_device,
        mesh=mesh,
        in_specs=(
            P("exp", "seq"),
            P("exp", "seq"),
            P(None, "seq"),
            P(),
            P("seq", None),
            P(("exp", "seq"), None),
            P(),
            P(("exp", "seq"), None),
            P(("exp", "seq"), None),
            P(("exp", "seq"), None),
            P(("seq", "exp"), None, None),
        ),
        out_specs=(P(("exp", "seq"), None), P(("seq", "exp"), None, None)),
        check_vma=False,
    )
```

```python
import functools

import jax
import jax.numpy as jnp
from jax import lax
from jax.experimental import pallas as pl
from jax.experimental.pallas import tpu as pltpu
from jax.sharding import PartitionSpec as P

BF16 = jnp.bfloat16
F32 = jnp.float32
HALO = 16
MIB = 1024 * 1024
VMEM_LIMIT = 60 * MIB
EXTRA = 128


def call_cost(flops, nbytes):
    return pl.CostEstimate(flops=int(flops), bytes_accessed=int(nbytes), transcendentals=0)


def norm_kernel(resid_ref, gain_ref, routes_ref, out_ref):
    rows = resid_ref[...].astype(F32)
    dim = rows.shape[1]
    scale = lax.rsqrt(jnp.mean(rows * rows, axis=1, keepdims=True) + 1e-06)
    out_ref[:, :dim] = (rows * scale * gain_ref[...]).astype(BF16)
    out_ref[:, dim:] = jnp.zeros((rows.shape[0], EXTRA), BF16)
    names = routes_ref[...].astype(F32)
    pad = jnp.zeros((HALO - names.shape[0], EXTRA), F32)
    out_ref[:HALO, dim:] = jnp.concatenate([names, pad]).astype(BF16)


def norm_rows(resid, gain, names):
    tokens, dim = resid.shape
    return pl.pallas_call(
        norm_kernel,
        out_shape=jax.ShapeDtypeStruct((tokens, dim + EXTRA), BF16),
        compiler_params=pltpu.CompilerParams(vmem_limit_bytes=VMEM_LIMIT),
        cost_estimate=call_cost(resid.size * 6, resid.size * 4),
        name="norm_rows",
    )(resid, gain.reshape(1, -1), names)


def conv_kernel(
    tile,
    place_ref,
    in_ref,
    in_low_ref,
    in_high_ref,
    grad_ref,
    grad_high_ref,
    ids_ref,
    taps_ref,
    local_ref,
    keep_ref,
    send_ref,
    in_ext,
    grad_ext,
):
    step = pl.program_id(0)
    rows = in_ref.shape[0]

    @pl.when(step == 0)
    def _():
        in_ext[:HALO] = in_low_ref[...].astype(F32)
        in_ext[HALO : HALO + rows] = in_ref[...].astype(F32)
        in_ext[HALO + rows :] = in_high_ref[...].astype(F32)
        grad_ext[:rows] = grad_ref[...].astype(F32)
        grad_ext[rows:] = grad_high_ref[...].astype(F32)

    first = pl.multiple_of(step * tile, tile)
    span = tile + 8
    taps = taps_ref[...]
    window = in_ext[pl.ds(first + HALO - 8, span + 8)]
    ids = ids_ref[pl.ds(first + HALO - 8, span + 8)]
    here = ids[8:]
    same = [None] + [(ids[8 - j : 8 - j + span] == here).astype(F32) for j in (1, 2, 3)]
    conv = taps[0:1] * window[8:]
    for j in (1, 2, 3):
        conv = conv + taps[j : j + 1] * window[8 - j : 8 - j + span] * same[j]
    gate = jax.nn.sigmoid(conv)
    pre = grad_ext[pl.ds(first, span)] * gate * (1.0 + conv * (1.0 - gate))
    result = taps[0:1] * pre[:tile]
    for j in (1, 2, 3):
        result = result + taps[j : j + 1] * (pre * same[j])[j : j + tile]
    local = result.astype(BF16)
    local_ref[...] = local
    half = tile // 2
    core = place_ref[0] & 1

    @pl.when(core == 0)
    def _():
        keep_ref[...] = local[:half]
        send_ref[...] = local[half:]

    @pl.when(core == 1)
    def _():
        keep_ref[...] = local[half:]
        send_ref[...] = local[:half]


def conv_back(place, qkv_in, low, high, qkv_grad, grad_high, ids, taps, block):
    rows, width = qkv_in.shape
    tile = 2 * block
    whole = lambda shape: pl.BlockSpec(shape, lambda i, p: (0,) * len(shape))
    part = lambda size: pl.BlockSpec((size, width), lambda i, p: (i, 0))
    return pl.pallas_call(
        functools.partial(conv_kernel, tile),
        grid_spec=pltpu.PrefetchScalarGridSpec(
            num_scalar_prefetch=1,
            grid=(rows // tile,),
            in_specs=[
                whole(qkv_in.shape),
                whole(low.shape),
                whole(high.shape),
                whole(qkv_grad.shape),
                whole(grad_high.shape),
                whole(ids.shape),
                whole(taps.shape),
            ],
            out_specs=[part(tile), part(block), part(block)],
            scratch_shapes=[
                pltpu.VMEM((rows + 2 * HALO, width), F32),
                pltpu.VMEM((rows + HALO, width), F32),
            ],
        ),
        out_shape=[
            jax.ShapeDtypeStruct((rows, width), BF16),
            jax.ShapeDtypeStruct((rows // 2, width), BF16),
            jax.ShapeDtypeStruct((rows // 2, width), BF16),
        ],
        compiler_params=pltpu.CompilerParams(vmem_limit_bytes=VMEM_LIMIT),
        cost_estimate=call_cost(40 * rows * width, 8 * rows * width),
        name="conv_back",
    )(place, qkv_in, low, high, qkv_grad, grad_high, ids, taps)


def project_kernel(place_ref, own_ref, other_ref, own_weight, other_weight, flow_ref, out_ref):
    block = flow_ref.shape[0]
    total = jnp.dot(own_ref[...], own_weight[...], preferred_element_type=F32)
    total = total + jnp.dot(other_ref[...], other_weight[...], preferred_element_type=F32)
    out_ref[...] = total.astype(BF16)
    for index in range(out_ref.shape[0] // block):

        @pl.when(index == place_ref[0] >> 1)
        def _():
            own = slice(index * block, (index + 1) * block)
            out_ref[own] = (total[own] + flow_ref[...].astype(F32)).astype(BF16)


def project(place, own, other, own_weight, other_weight, out_grad):
    rows, width = own.shape
    dim = own_weight.shape[1]
    tile = dim // 3
    whole = pl.BlockSpec((rows, width), lambda i, p: (0, 0))
    columns = lambda size: pl.BlockSpec((size, tile), lambda i, p: (0, i))
    return pl.pallas_call(
        project_kernel,
        grid_spec=pltpu.PrefetchScalarGridSpec(
            num_scalar_prefetch=1,
            grid=(dim // tile,),
            in_specs=[whole, whole, columns(width), columns(width), columns(out_grad.shape[0])],
            out_specs=columns(rows),
        ),
        out_shape=jax.ShapeDtypeStruct((rows, dim), BF16),
        compiler_params=pltpu.CompilerParams(vmem_limit_bytes=VMEM_LIMIT),
        cost_estimate=call_cost(4 * rows * width * dim, 4 * (rows + dim) * width + 2 * rows * dim),
        name="project",
    )(place, own, other, own_weight, other_weight, out_grad)


def slot_picker(names, own, capacity):
    count, tokens = own.shape
    match = [(names[k : k + 1] == own) for k in range(names.shape[0])]
    named = functools.reduce(jnp.logical_or, match)
    source = lax.broadcasted_iota(jnp.int32, (tokens, tokens), 0)
    target = lax.broadcasted_iota(jnp.int32, (tokens, tokens), 1)
    earlier = (source < target).astype(BF16)
    rank = jnp.dot(named.astype(BF16), earlier, preferred_element_type=F32).astype(jnp.int32)
    rank = jnp.where(named, rank, -1)
    slot = lax.broadcasted_iota(jnp.int32, (count, capacity, tokens), 1)
    picker = (rank[:, None, :] == slot).astype(F32)
    return picker, match


def pick_norm_kernel(per_token, capacity, n_exp, turns, place_ref, *refs):
    halves = len(turns)
    out_refs = refs[halves:]
    outs = len(out_refs) // halves
    for half in range(halves):
        rows_ref = refs[half]
        tokens = rows_ref.shape[1]
        dim = out_refs[0].shape[3]
        count = len(turns[half])
        names = rows_ref[0, :HALO, dim:].astype(F32)[:per_token].astype(jnp.int32)
        own = jnp.concatenate(
            [
                jnp.full((1, tokens), (place_ref[0] ^ t) * n_exp + place_ref[1], jnp.int32)
                for t in turns[half]
            ]
        )
        picker, _ = slot_picker(names, own, capacity)
        picker = picker.reshape(count * capacity, tokens).astype(BF16)
        picked = jnp.dot(picker, rows_ref[0, :, :dim], preferred_element_type=F32).astype(BF16)
        for index in range(count):
            out_refs[half * outs + index // 2][index % 2, 0] = picked[
                index * capacity : (index + 1) * capacity
            ]


def pick_norm(place, rows, turns, dim, per_token, capacity):
    blocks, tokens, width = rows.shape
    halves = len(turns)
    count = blocks // halves
    outs = len(turns[0]) // 2 * halves
    row_spec = lambda first: pl.BlockSpec(
        (1, tokens, width), lambda i, p: (p[1] ^ (i + first), 0, 0)
    )
    return pl.pallas_call(
        functools.partial(pick_norm_kernel, per_token, capacity, blocks, turns),
        grid_spec=pltpu.PrefetchScalarGridSpec(
            num_scalar_prefetch=1,
            grid=(count,),
            in_specs=[row_spec(half * count) for half in range(halves)],
            out_specs=[pl.BlockSpec((2, 1, capacity, dim), lambda i, p: (0, i, 0, 0))] * outs,
        ),
        out_shape=[jax.ShapeDtypeStruct((2, count, capacity, dim), BF16)] * outs,
        compiler_params=pltpu.CompilerParams(vmem_limit_bytes=VMEM_LIMIT),
        cost_estimate=call_cost(
            2 * len(turns[0]) * capacity * blocks * tokens * dim,
            2 * dim * blocks * (tokens + len(turns[0]) * capacity),
        ),
        name="pick_norm",
    )(place, *[rows] * halves)


def pick_grad_kernel(per_token, capacity, n_exp, turns, place_ref, tables_ref, *refs):
    flow_refs, out_refs = refs[:2], refs[2:-2]
    buffer, sems = refs[-2:]
    tokens = tables_ref.shape[2]
    copies = []
    for quarter, turn in enumerate(turns):
        count = len(turn)
        own = jnp.concatenate(
            [
                jnp.full((1, tokens), place_ref[0] * n_exp + (place_ref[1] ^ t), jnp.int32)
                for t in turn
            ]
        )
        first = pl.multiple_of(((place_ref[0] >> 1) ^ quarter) * tokens, tokens)
        for core in range(2):
            table = tables_ref[place_ref[0] ^ (2 * quarter + core)]
            names = table[:per_token].astype(jnp.int32)
            picker, match = slot_picker(names, own, capacity)
            weights = table[per_token:]
            scale = functools.reduce(
                jnp.add, [jnp.where(match[k], weights[k : k + 1], 0.0) for k in range(per_token)]
            )
            scales = jnp.sum(picker * scale[:, None, :], axis=2, keepdims=True)
            picker = picker.reshape(count * capacity, tokens).astype(BF16)
            picked = jnp.dot(
                picker, flow_refs[core][pl.ds(first, tokens)], preferred_element_type=F32
            )
            picked = (picked * scales.reshape(count * capacity, 1)).astype(BF16)
            for index in range(count):
                buffer[quarter, index, core * capacity : (core + 1) * capacity] = picked[
                    index * capacity : (index + 1) * capacity
                ]
        for part in range(2):
            at = 2 * quarter + part
            copy = pltpu.make_async_copy(
                buffer.at[quarter, pl.ds(part * count // 2, count // 2)],
                out_refs[at],
                sems.at[at],
            )
            copy.start()
            copies.append(copy)
    for copy in copies:
        copy.wait()


def pick_grad(place, tables, flows, turns, n_exp, per_token, capacity):
    dim = flows[0].shape[1]
    rows, count = 2 * capacity, len(turns[0])
    whole = lambda array: pl.BlockSpec(array.shape, lambda i, p: (0,) * array.ndim)
    outs = 2 * len(turns)
    return pl.pallas_call(
        functools.partial(pick_grad_kernel, per_token, capacity, n_exp, turns),
        grid_spec=pltpu.PrefetchScalarGridSpec(
            num_scalar_prefetch=1,
            grid=(1,),
            in_specs=[whole(tables), whole(flows[0]), whole(flows[1])],
            out_specs=[pl.BlockSpec(memory_space=pl.ANY)] * outs,
            scratch_shapes=[
                pltpu.VMEM((len(turns), count, rows, dim), BF16),
                pltpu.SemaphoreType.DMA((outs,)),
            ],
        ),
        out_shape=[jax.ShapeDtypeStruct((count // 2, rows, dim), BF16)] * outs,
        compiler_params=pltpu.CompilerParams(vmem_limit_bytes=VMEM_LIMIT),
        cost_estimate=call_cost(
            2 * len(turns) * count * rows * tables.shape[2] * dim,
            4 * dim * (flows[0].shape[0] + len(turns) * count * rows // 2),
        ),
        name="pick_grad",
    )(place, tables, *flows)


def forward_kernel(sources, *refs):
    row_refs = refs[1 : 1 + sources]
    weight_ref = refs[1 + sources]
    rows_out, act_ref, gate_ref, up_ref, rows = refs[-5:]
    _, group, capacity, _ = row_refs[0].shape
    for inner in range(group):
        for index in range(sources):
            at = (inner * sources + index) * capacity
            rows[at : at + capacity] = row_refs[index][0, inner]
    hidden = act_ref.shape[0]
    mixed = jnp.dot(rows[...], weight_ref[...], preferred_element_type=F32)
    rows_out[...] = rows[...].T
    gate = mixed[:, :hidden]
    up = mixed[:, hidden:]
    sig = jax.nn.sigmoid(gate)
    silu = gate * sig
    act_ref[...] = (silu * up).astype(BF16).T
    gate_ref[...] = up * sig * (1.0 + gate * (1.0 - sig))
    up_ref[...] = silu


def expert_forward(pieces, weight, hidden, shifts, parts, part, before):
    sources = len(pieces)
    _, blocks, capacity, dim = pieces[0][0].shape
    group = 16 // sources
    tile = sources * group * capacity
    steps = blocks // group
    total = tile * steps * parts
    at = lambda i: i + part * steps
    row_spec = lambda width: pl.BlockSpec((tile, width), lambda i, p: (at(i), 0))
    column_spec = lambda height: pl.BlockSpec((height, tile), lambda i, p: (0, at(i)))

    def piece_spec(unit, shift):
        return pl.BlockSpec(
            (1, group, capacity, dim),
            lambda i, p: (unit if shift is None else unit + p[shift], i, 0, 0),
        )

    return pl.pallas_call(
        functools.partial(forward_kernel, sources),
        grid_spec=pltpu.PrefetchScalarGridSpec(
            num_scalar_prefetch=1,
            grid=(steps,),
            in_specs=[piece_spec(unit, shift) for _, unit, shift in pieces]
            + [pl.BlockSpec((dim, 2 * hidden), lambda i, p: (0, 0))]
            + [pl.BlockSpec(memory_space=pl.ANY)] * len(before),
            out_specs=[column_spec(dim), column_spec(hidden), row_spec(hidden), row_spec(hidden)],
            scratch_shapes=[pltpu.VMEM((tile, dim), BF16)],
        ),
        out_shape=[
            jax.ShapeDtypeStruct((dim, total), BF16),
            jax.ShapeDtypeStruct((hidden, total), BF16),
            jax.ShapeDtypeStruct((total, hidden), F32),
            jax.ShapeDtypeStruct((total, hidden), F32),
        ],
        input_output_aliases={sources + 2 + i: i for i in range(len(before))},
        compiler_params=pltpu.CompilerParams(vmem_limit_bytes=VMEM_LIMIT),
        cost_estimate=call_cost(
            4 * total * dim * hidden // parts, (4 * total * dim + 10 * total * hidden) // parts
        ),
        name="expert_forward",
    )(shifts, *[array for array, _, _ in pieces], weight, *before)


def backward_kernel(places, arrays, *refs):
    grad_refs = refs[:arrays]
    gate_ref, up_ref, weight_ref, rows_ref, act_ref, out_ref = refs[arrays : arrays + 6]
    grads_all, hidden_all, sems = refs[arrays + 6 :]
    step = pl.program_id(0)
    tile = gate_ref.shape[0]
    hidden = act_ref.shape[0]
    width = rows_ref.shape[0]
    row_steps = grads_all.shape[0] // tile
    copies = []
    for index, (array, unit, row, size) in enumerate(places):
        copy = pltpu.make_async_copy(
            grad_refs[array].at[unit], grads_all.at[pl.ds(row, size)], sems.at[index]
        )
        copies.append((row // tile, copy))

    @pl.when(step == 0)
    def _():
        for turn in range(row_steps):
            for at, copy in copies:
                if at == turn:
                    copy.start()

    for turn in range(row_steps):

        @pl.when(step == turn)
        def _():
            for at, copy in copies:
                if at == turn:
                    copy.wait()

    @pl.when(step < row_steps)
    def _():
        where = pl.ds(pl.multiple_of(step * tile, tile), tile)
        act_grad = jnp.dot(grads_all[where], weight_ref[...], preferred_element_type=F32)
        hidden_all[where, :hidden] = (act_grad * gate_ref[...]).astype(BF16)
        hidden_all[where, hidden:] = (act_grad * up_ref[...]).astype(BF16)

    @pl.when(step >= row_steps)
    def _():
        columns = pl.ds(pl.multiple_of((step - row_steps) * width, width), width)
        out_ref[:, : 2 * hidden] = jnp.dot(
            rows_ref[...], hidden_all[...], preferred_element_type=F32
        ).astype(BF16)
        down = jnp.dot(act_ref[...], grads_all[:, columns], preferred_element_type=F32)
        out_ref[:, 2 * hidden :] = down.T.astype(BF16)


def expert_backward(arrays, places, gate, up, weights, rows, act):
    dim, total = rows.shape
    hidden = act.shape[0]
    tile, width = 512, 768
    row_steps, column_steps = total // tile, dim // width
    row_spec = lambda cols: pl.BlockSpec(
        (tile, cols), lambda i: (jnp.minimum(i, row_steps - 1), 0)
    )
    column_of = lambda i: jnp.maximum(i - row_steps, 0)
    return pl.pallas_call(
        functools.partial(backward_kernel, places, len(arrays)),
        grid=(row_steps + column_steps,),
        in_specs=[pl.BlockSpec(memory_space=pl.ANY)] * len(arrays)
        + [
            row_spec(hidden),
            row_spec(hidden),
            pl.BlockSpec((dim, hidden), lambda i: (0, 2)),
            pl.BlockSpec((width, total), lambda i: (column_of(i), 0)),
            pl.BlockSpec((hidden, total), lambda i: (0, 0)),
        ],
        out_specs=pl.BlockSpec((width, 3 * hidden), lambda i: (column_of(i), 0)),
        out_shape=jax.ShapeDtypeStruct((dim, 3 * hidden), BF16),
        scratch_shapes=[
            pltpu.VMEM((total, dim), BF16),
            pltpu.VMEM((total, 2 * hidden), BF16),
            pltpu.SemaphoreType.DMA((len(places),)),
        ],
        compiler_params=pltpu.CompilerParams(vmem_limit_bytes=VMEM_LIMIT),
        cost_estimate=call_cost(8 * total * dim * hidden, 4 * total * dim + 20 * total * hidden),
        name="expert_backward",
    )(*arrays, gate, up, weights, rows, act)


def merge_kernel(parts, arrays, shift_ref, *refs):
    out_ref, sems = refs[arrays], refs[arrays + 1]
    copies = []
    for at, (array, unit, shift) in enumerate(parts):
        source = refs[array]
        first = unit if shift is None else unit + shift_ref[shift]
        half = source.shape[1] // 2
        for piece in range(2):
            rows = pl.ds(piece * half, half)
            copies.append(
                pltpu.make_async_copy(
                    source.at[first, rows], out_ref.at[at, rows], sems.at[2 * at + piece]
                )
            )
    for copy in copies:
        copy.start()
    for copy in copies:
        copy.wait()


def merge(shifts, parts):
    arrays, list_of = [], []
    for array, units, shift in parts:
        known = [i for i, other in enumerate(arrays) if other is array]
        if not known:
            arrays.append(array)
            known = [len(arrays) - 1]
        list_of += [(known[0], unit, shift) for unit in units]
    shape = (len(list_of),) + arrays[0].shape[1:]
    size = functools.reduce(lambda a, b: a * b, shape, 1)
    return pl.pallas_call(
        functools.partial(merge_kernel, tuple(list_of), len(arrays)),
        grid_spec=pltpu.PrefetchScalarGridSpec(
            num_scalar_prefetch=1,
            grid=(1,),
            in_specs=[pl.BlockSpec(memory_space=pl.ANY)] * len(arrays),
            out_specs=pl.BlockSpec(shape, lambda i, s: (0,) * len(shape)),
            scratch_shapes=[pltpu.SemaphoreType.DMA((2 * len(list_of),))],
        ),
        out_shape=jax.ShapeDtypeStruct(shape, BF16),
        compiler_params=pltpu.CompilerParams(vmem_limit_bytes=VMEM_LIMIT),
        cost_estimate=call_cost(0, 4 * size),
        name="merge_rows",
    )(shifts, *arrays)


def swap(array, axis, flip):
    count = lax.axis_size(axis)
    return lax.ppermute(array, axis, [(i, i ^ flip) for i in range(count)])


def mask_of(flips, bits):
    return functools.reduce(lambda a, b: a ^ b, [f for f, bit in zip(flips, bits) if bit], 0)


def flips_of(half):
    return (1, 3) if half == 0 else (3, 1)


def swap_gather(array, axis, flip):
    count = lax.axis_size(axis)
    groups = [[i, i ^ flip] for i in range(count) if i < i ^ flip]
    both = lax.all_gather(array, axis, axis_index_groups=groups)
    return both.reshape((-1,) + array.shape[1:])


def third_message(shifts, keep, first, second):
    parts = [(keep, (2, 3)), (first, (2, 3)), (second, (2, 3)), (second, (6, 7))]
    return merge(shifts, [(array, units, None) for array, units in parts])


def fourth_message(shifts, keep, first, second, third):
    parts = [(keep, (1,)), (first, (1,)), (second, (1, 5)), (third, (1, 3, 5, 7))]
    return merge(shifts, [(array, units, None) for array, units in parts])


def grad_places(flips):
    found = {}
    found[0, 0, 0, 0] = (0, 0)
    found[1, 0, 0, 0] = (1, 0)
    found[0, 1, 0, 0] = (2, 0)
    found[1, 1, 0, 0] = (2, 4)
    for index, start in enumerate([(0, 0), (1, 0), (0, 1), (1, 1)]):
        found[start + (1, 0)] = (3, 2 * index)
        found[start + (0, 1)] = (4, index)
        found[start + (1, 1)] = (4, 4 + index)
    return {mask_of(flips, bits): at for bits, at in found.items()}


def per_device(
    qkv_in,
    qkv_grad,
    conv_weight,
    doc_ids,
    qkv_weight,
    resid,
    norm_gain,
    out_grad,
    routes,
    route_weights,
    expert_weights,
):
    rows, width = qkv_in.shape
    tokens, dim = resid.shape
    per_token = routes.shape[1]
    hidden = expert_weights.shape[2] // 3
    n_seq, n_exp = lax.axis_size("seq"), lax.axis_size("exp")
    experts = n_seq * n_exp
    capacity = 2 * tokens * per_token // experts
    seq_index, exp_index = lax.axis_index("seq"), lax.axis_index("exp")
    own_weights = expert_weights[0]

    place = jnp.stack([seq_index, exp_index]).astype(jnp.int32)
    forward = [(i, i + 1) for i in range(n_exp - 1)]
    backward = [(i + 1, i) for i in range(n_exp - 1)]
    low = lax.ppermute(qkv_in[-HALO:], "exp", forward)
    high = lax.ppermute(qkv_in[:HALO], "exp", backward)
    grad_high = lax.ppermute(qkv_grad[:HALO], "exp", backward)
    weight_far = swap(qkv_weight, "seq", 1)

    table = jnp.concatenate([routes.astype(F32), route_weights], 1).T
    tables = jnp.broadcast_to(table[None], (n_seq,) + table.shape)
    tables = lax.all_to_all(tables, "seq", split_axis=0, concat_axis=0, tiled=True)
    normed = norm_rows(resid, norm_gain, routes.T)
    normed, conv_weight = lax.optimization_barrier((normed, conv_weight))
    exp_normed = lax.all_gather(normed, "exp")

    edge = jnp.full((HALO,), -1, jnp.int32)
    ids = lax.dynamic_slice_in_dim(
        jnp.concatenate([edge, doc_ids, edge]), exp_index * rows, rows + 2 * HALO
    )
    local_grad, local_keep, local_send = conv_back(
        place, qkv_in, low, high, qkv_grad, grad_high, ids.reshape(-1, 1), conv_weight, tokens
    )
    local_send, tables = lax.optimization_barrier((local_send, tables))
    local_got = swap(local_send, "seq", 1)
    partial = project(place, local_keep, local_got, qkv_weight, weight_far, out_grad)
    same_core = [[s for s in range(n_seq) if s % 2 == core] for core in range(2)]
    flow = lax.psum(partial, "seq", axis_index_groups=same_core)

    flips_a, flips_b = flips_of(0), flips_of(1)
    shifts = [(seq_index < seq_index ^ 2 * f).astype(jnp.int32) * 4 for f in flips_b]
    shifts = jnp.stack(shifts)
    turns = []
    for near in (flips_a, flips_b):
        near = (0, near[1], near[0], near[0] ^ near[1])
        turns.append(tuple(2 * m for m in near) + tuple(2 * m + 1 for m in near))
    picks = pick_norm(place, exp_normed, tuple(turns), dim, per_token, capacity)
    (keep_a, send_a, keep_far_a, send_far_a) = picks[:4]
    (keep_b, send_b, keep_far_b, send_far_b) = picks[4:]
    got_a, got_b = swap(send_far_a, "seq", 1), swap(send_far_b, "seq", 1)
    message_a = merge(shifts, [(send_a, (0, 1), None), (got_a, (0, 1), None)])
    message_a, got_b = lax.optimization_barrier((message_a, got_b))
    first_a = swap(message_a, "seq", 2 * flips_a[0])
    message_b = merge(shifts, [(send_b, (0, 1), None), (got_b, (0, 1), None)])
    far_a, far_b = swap(keep_far_a, "seq", 1), swap(keep_far_b, "seq", 1)
    flow, far_a, far_b, message_b, local_grad = lax.optimization_barrier(
        (flow, far_a, far_b, message_b, local_grad)
    )
    first_b = swap_gather(message_b, "seq", 2 * flips_b[0])
    qkv_in_grad = lax.all_to_all(local_grad, "seq", split_axis=0, concat_axis=1, tiled=True)
    flow_far = swap(flow, "seq", 1)

    flips = (1, 3, 4, 12)
    quarters = len(flips)
    orders = [flips[k:] + flips[:k] for k in range(quarters)]
    bit_rows = [tuple((j >> (3 - b)) & 1 for b in range(4)) for j in range(n_exp)]
    turns = tuple(tuple(mask_of(order, bits) for bits in bit_rows) for order in orders)
    sends = pick_grad(place, tables, (flow, flow_far), turns, n_exp, per_token, capacity)

    firsts = [swap(sends[2 * k + 1], "exp", orders[k][0]) for k in range(quarters)]
    seconds = [
        swap(
            merge(shifts, [(sends[2 * k], range(4, 8), None), (firsts[k], range(4, 8), None)]),
            "exp",
            orders[k][1],
        )
        for k in range(quarters)
    ]
    first_a, first_b, firsts = lax.optimization_barrier((first_a, first_b, firsts))
    message_a = merge(
        shifts, [(keep_a, (1,), None), (far_a, (1,), None), (first_a, (1, 3), None)]
    )
    message_b = merge(shifts, [(keep_b, (1,), None), (far_b, (1,), None), (first_b, (1, 3), 0)])
    second_a = swap(message_a, "seq", 2 * flips_a[1])
    second_b = swap_gather(message_b, "seq", 2 * flips_b[1])
    calls = [
        [(keep_a, 0, None), (far_a, 0, None), (first_a, 0, None), (first_a, 2, None)],
        [(keep_b, 0, None), (far_b, 0, None), (first_b, 0, 0), (first_b, 2, 0)],
        [(second_a, i, None) for i in range(4)],
        [(second_b, i, 1) for i in range(4)],
    ]
    thirds = []
    for k in range(quarters):
        message = third_message(shifts, sends[2 * k], firsts[k], seconds[k])
        thirds.append(swap(message, "exp", orders[k][2]))
    results = ()
    for part, pieces in enumerate(calls):
        results = expert_forward(
            pieces, own_weights, hidden, shifts, len(calls), part, results
        )
        if part == 1:
            results, thirds = lax.optimization_barrier((results, thirds))
    rows_all, act, gate, up = results

    def row_of(mask, quarter):
        half, inner = mask >> 3, mask & 7
        flips = flips_of(half)
        order = (0, flips[0], flips[1], flips[0] ^ flips[1])
        spot = order.index(quarter)
        call = (spot >> 1) * 2 + half
        tile = call * 2 + (inner >> 2)
        return tile * n_exp * capacity + (inner & 3) * 4 * capacity + (spot & 1) * 2 * capacity

    arrays, places = [], []
    for k in range(quarters):
        got = [sends[2 * k], firsts[k], seconds[k], thirds[k]]
        message = fourth_message(shifts, *got)
        got.append(swap(message, "exp", orders[k][3]))
        for mask, (array, unit) in sorted(grad_places(orders[k]).items()):
            places.append((len(arrays) + array, unit, row_of(mask, k), 2 * capacity))
        arrays += got
    expert_grads = expert_backward(arrays, tuple(places), gate, up, own_weights, rows_all, act)
    return (qkv_in_grad, expert_grads[None])


def solution(mesh):
    return jax.shard_map(
        per_device,
        mesh=mesh,
        in_specs=(
            P("exp", "seq"),
            P("exp", "seq"),
            P(None, "seq"),
            P(),
            P("seq", None),
            P(("exp", "seq"), None),
            P(),
            P(("exp", "seq"), None),
            P(("exp", "seq"), None),
            P(("exp", "seq"), None),
            P(("seq", "exp"), None, None),
        ),
        out_specs=(P(("exp", "seq"), None), P(("seq", "exp"), None, None)),
        check_vma=False,
    )
```

```python
import functools

import jax
import jax.numpy as jnp
from jax import lax
from jax.experimental import pallas as pl
from jax.experimental.pallas import tpu as pltpu
from jax.sharding import PartitionSpec as P

BF16 = jnp.bfloat16
F32 = jnp.float32
HALO = 16
MIB = 1024 * 1024
VMEM_LIMIT = 60 * MIB
EXTRA = 128


def call_cost(flops, nbytes):
    return pl.CostEstimate(flops=int(flops), bytes_accessed=int(nbytes), transcendentals=0)


def norm_kernel(resid_ref, gain_ref, routes_ref, out_ref):
    rows = resid_ref[...].astype(F32)
    dim = rows.shape[1]
    scale = lax.rsqrt(jnp.mean(rows * rows, axis=1, keepdims=True) + 1e-06)
    out_ref[:, :dim] = (rows * scale * gain_ref[...]).astype(BF16)
    out_ref[:, dim:] = jnp.zeros((rows.shape[0], EXTRA), BF16)
    names = routes_ref[...].astype(F32)
    pad = jnp.zeros((HALO - names.shape[0], EXTRA), F32)
    out_ref[:HALO, dim:] = jnp.concatenate([names, pad]).astype(BF16)


def norm_rows(resid, gain, names):
    tokens, dim = resid.shape
    return pl.pallas_call(
        norm_kernel,
        out_shape=jax.ShapeDtypeStruct((tokens, dim + EXTRA), BF16),
        compiler_params=pltpu.CompilerParams(vmem_limit_bytes=VMEM_LIMIT),
        cost_estimate=call_cost(resid.size * 6, resid.size * 4),
        name="norm_rows",
    )(resid, gain.reshape(1, -1), names)


def conv_kernel(
    tile,
    place_ref,
    in_ref,
    in_low_ref,
    in_high_ref,
    grad_ref,
    grad_high_ref,
    ids_ref,
    taps_ref,
    local_ref,
    keep_ref,
    send_ref,
    in_ext,
    grad_ext,
):
    step = pl.program_id(0)
    rows = in_ref.shape[0]

    @pl.when(step == 0)
    def _():
        in_ext[:HALO] = in_low_ref[...].astype(F32)
        in_ext[HALO : HALO + rows] = in_ref[...].astype(F32)
        in_ext[HALO + rows :] = in_high_ref[...].astype(F32)
        grad_ext[:rows] = grad_ref[...].astype(F32)
        grad_ext[rows:] = grad_high_ref[...].astype(F32)

    first = pl.multiple_of(step * tile, tile)
    span = tile + 8
    taps = taps_ref[...]
    window = in_ext[pl.ds(first + HALO - 8, span + 8)]
    ids = ids_ref[pl.ds(first + HALO - 8, span + 8)]
    here = ids[8:]
    same = [None] + [(ids[8 - j : 8 - j + span] == here).astype(F32) for j in (1, 2, 3)]
    conv = taps[0:1] * window[8:]
    for j in (1, 2, 3):
        conv = conv + taps[j : j + 1] * window[8 - j : 8 - j + span] * same[j]
    gate = jax.nn.sigmoid(conv)
    pre = grad_ext[pl.ds(first, span)] * gate * (1.0 + conv * (1.0 - gate))
    result = taps[0:1] * pre[:tile]
    for j in (1, 2, 3):
        result = result + taps[j : j + 1] * (pre * same[j])[j : j + tile]
    local = result.astype(BF16)
    local_ref[...] = local
    half = tile // 2
    core = place_ref[0] & 1

    @pl.when(core == 0)
    def _():
        keep_ref[...] = local[:half]
        send_ref[...] = local[half:]

    @pl.when(core == 1)
    def _():
        keep_ref[...] = local[half:]
        send_ref[...] = local[:half]


def conv_back(place, qkv_in, low, high, qkv_grad, grad_high, ids, taps, block):
    rows, width = qkv_in.shape
    tile = 2 * block
    whole = lambda shape: pl.BlockSpec(shape, lambda i, p: (0,) * len(shape))
    part = lambda size: pl.BlockSpec((size, width), lambda i, p: (i, 0))
    return pl.pallas_call(
        functools.partial(conv_kernel, tile),
        grid_spec=pltpu.PrefetchScalarGridSpec(
            num_scalar_prefetch=1,
            grid=(rows // tile,),
            in_specs=[
                whole(qkv_in.shape),
                whole(low.shape),
                whole(high.shape),
                whole(qkv_grad.shape),
                whole(grad_high.shape),
                whole(ids.shape),
                whole(taps.shape),
            ],
            out_specs=[part(tile), part(block), part(block)],
            scratch_shapes=[
                pltpu.VMEM((rows + 2 * HALO, width), F32),
                pltpu.VMEM((rows + HALO, width), F32),
            ],
        ),
        out_shape=[
            jax.ShapeDtypeStruct((rows, width), BF16),
            jax.ShapeDtypeStruct((rows // 2, width), BF16),
            jax.ShapeDtypeStruct((rows // 2, width), BF16),
        ],
        compiler_params=pltpu.CompilerParams(vmem_limit_bytes=VMEM_LIMIT),
        cost_estimate=call_cost(40 * rows * width, 8 * rows * width),
        name="conv_back",
    )(place, qkv_in, low, high, qkv_grad, grad_high, ids, taps)


def project_kernel(place_ref, own_ref, other_ref, own_weight, other_weight, flow_ref, out_ref):
    block = flow_ref.shape[0]
    total = jnp.dot(own_ref[...], own_weight[...], preferred_element_type=F32)
    total = total + jnp.dot(other_ref[...], other_weight[...], preferred_element_type=F32)
    out_ref[...] = total.astype(BF16)
    for index in range(out_ref.shape[0] // block):

        @pl.when(index == place_ref[0] >> 1)
        def _():
            own = slice(index * block, (index + 1) * block)
            out_ref[own] = (total[own] + flow_ref[...].astype(F32)).astype(BF16)


def project(place, own, other, own_weight, other_weight, out_grad):
    rows, width = own.shape
    dim = own_weight.shape[1]
    tile = dim // 3
    whole = pl.BlockSpec((rows, width), lambda i, p: (0, 0))
    columns = lambda size: pl.BlockSpec((size, tile), lambda i, p: (0, i))
    return pl.pallas_call(
        project_kernel,
        grid_spec=pltpu.PrefetchScalarGridSpec(
            num_scalar_prefetch=1,
            grid=(dim // tile,),
            in_specs=[whole, whole, columns(width), columns(width), columns(out_grad.shape[0])],
            out_specs=columns(rows),
        ),
        out_shape=jax.ShapeDtypeStruct((rows, dim), BF16),
        compiler_params=pltpu.CompilerParams(vmem_limit_bytes=VMEM_LIMIT),
        cost_estimate=call_cost(4 * rows * width * dim, 4 * (rows + dim) * width + 2 * rows * dim),
        name="project",
    )(place, own, other, own_weight, other_weight, out_grad)


def slot_picker(names, own, capacity):
    count, tokens = own.shape
    match = [(names[k : k + 1] == own) for k in range(names.shape[0])]
    named = functools.reduce(jnp.logical_or, match)
    source = lax.broadcasted_iota(jnp.int32, (tokens, tokens), 0)
    target = lax.broadcasted_iota(jnp.int32, (tokens, tokens), 1)
    earlier = (source < target).astype(BF16)
    rank = jnp.dot(named.astype(BF16), earlier, preferred_element_type=F32).astype(jnp.int32)
    rank = jnp.where(named, rank, -1)
    slot = lax.broadcasted_iota(jnp.int32, (count, capacity, tokens), 1)
    picker = (rank[:, None, :] == slot).astype(F32)
    return picker, match


def pick_norm_kernel(per_token, capacity, n_exp, turns, place_ref, *refs):
    halves = len(turns)
    out_refs = refs[halves:]
    outs = len(out_refs) // halves
    for half in range(halves):
        rows_ref = refs[half]
        tokens = rows_ref.shape[1]
        dim = out_refs[0].shape[3]
        count = len(turns[half])
        names = rows_ref[0, :HALO, dim:].astype(F32)[:per_token].astype(jnp.int32)
        own = jnp.concatenate(
            [
                jnp.full((1, tokens), (place_ref[0] ^ t) * n_exp + place_ref[1], jnp.int32)
                for t in turns[half]
            ]
        )
        picker, _ = slot_picker(names, own, capacity)
        picker = picker.reshape(count * capacity, tokens).astype(BF16)
        picked = jnp.dot(picker, rows_ref[0, :, :dim], preferred_element_type=F32).astype(BF16)
        for index in range(count):
            out_refs[half * outs + index // 2][index % 2, 0] = picked[
                index * capacity : (index + 1) * capacity
            ]


def pick_norm(place, rows, turns, dim, per_token, capacity):
    blocks, tokens, width = rows.shape
    halves = len(turns)
    count = blocks // halves
    outs = len(turns[0]) // 2 * halves
    row_spec = lambda first: pl.BlockSpec(
        (1, tokens, width), lambda i, p: (p[1] ^ (i + first), 0, 0)
    )
    return pl.pallas_call(
        functools.partial(pick_norm_kernel, per_token, capacity, blocks, turns),
        grid_spec=pltpu.PrefetchScalarGridSpec(
            num_scalar_prefetch=1,
            grid=(count,),
            in_specs=[row_spec(half * count) for half in range(halves)],
            out_specs=[pl.BlockSpec((2, 1, capacity, dim), lambda i, p: (0, i, 0, 0))] * outs,
        ),
        out_shape=[jax.ShapeDtypeStruct((2, count, capacity, dim), BF16)] * outs,
        compiler_params=pltpu.CompilerParams(vmem_limit_bytes=VMEM_LIMIT),
        cost_estimate=call_cost(
            2 * len(turns[0]) * capacity * blocks * tokens * dim,
            2 * dim * blocks * (tokens + len(turns[0]) * capacity),
        ),
        name="pick_norm",
    )(place, *[rows] * halves)


def pick_grad_kernel(per_token, capacity, n_exp, turns, place_ref, tables_ref, *refs):
    flow_refs, out_refs = refs[:2], refs[2:-2]
    buffer, sems = refs[-2:]
    tokens = tables_ref.shape[2]
    copies = []
    for quarter, turn in enumerate(turns):
        count = len(turn)
        own = jnp.concatenate(
            [
                jnp.full((1, tokens), place_ref[0] * n_exp + (place_ref[1] ^ t), jnp.int32)
                for t in turn
            ]
        )
        first = pl.multiple_of(((place_ref[0] >> 1) ^ quarter) * tokens, tokens)
        for core in range(2):
            table = tables_ref[place_ref[0] ^ (2 * quarter + core)]
            names = table[:per_token].astype(jnp.int32)
            picker, match = slot_picker(names, own, capacity)
            weights = table[per_token:]
            scale = functools.reduce(
                jnp.add, [jnp.where(match[k], weights[k : k + 1], 0.0) for k in range(per_token)]
            )
            scales = jnp.sum(picker * scale[:, None, :], axis=2, keepdims=True)
            picker = picker.reshape(count * capacity, tokens).astype(BF16)
            picked = jnp.dot(
                picker, flow_refs[core][pl.ds(first, tokens)], preferred_element_type=F32
            )
            picked = (picked * scales.reshape(count * capacity, 1)).astype(BF16)
            for index in range(count):
                buffer[quarter, index, core * capacity : (core + 1) * capacity] = picked[
                    index * capacity : (index + 1) * capacity
                ]
        for part in range(2):
            at = 2 * quarter + part
            copy = pltpu.make_async_copy(
                buffer.at[quarter, pl.ds(part * count // 2, count // 2)],
                out_refs[at],
                sems.at[at],
            )
            copy.start()
            copies.append(copy)
    for copy in copies:
        copy.wait()


def pick_grad(place, tables, flows, turns, n_exp, per_token, capacity):
    dim = flows[0].shape[1]
    rows, count = 2 * capacity, len(turns[0])
    whole = lambda array: pl.BlockSpec(array.shape, lambda i, p: (0,) * array.ndim)
    outs = 2 * len(turns)
    return pl.pallas_call(
        functools.partial(pick_grad_kernel, per_token, capacity, n_exp, turns),
        grid_spec=pltpu.PrefetchScalarGridSpec(
            num_scalar_prefetch=1,
            grid=(1,),
            in_specs=[whole(tables), whole(flows[0]), whole(flows[1])],
            out_specs=[pl.BlockSpec(memory_space=pl.ANY)] * outs,
            scratch_shapes=[
                pltpu.VMEM((len(turns), count, rows, dim), BF16),
                pltpu.SemaphoreType.DMA((outs,)),
            ],
        ),
        out_shape=[jax.ShapeDtypeStruct((count // 2, rows, dim), BF16)] * outs,
        compiler_params=pltpu.CompilerParams(vmem_limit_bytes=VMEM_LIMIT),
        cost_estimate=call_cost(
            2 * len(turns) * count * rows * tables.shape[2] * dim,
            4 * dim * (flows[0].shape[0] + len(turns) * count * rows // 2),
        ),
        name="pick_grad",
    )(place, tables, *flows)


def forward_kernel(sources, *refs):
    row_refs = refs[1 : 1 + sources]
    weight_ref = refs[1 + sources]
    rows_out, act_ref, gate_ref, up_ref, rows = refs[-5:]
    _, group, capacity, _ = row_refs[0].shape
    for inner in range(group):
        for index in range(sources):
            at = (inner * sources + index) * capacity
            rows[at : at + capacity] = row_refs[index][0, inner]
    hidden = act_ref.shape[0]
    mixed = jnp.dot(rows[...], weight_ref[...], preferred_element_type=F32)
    rows_out[...] = rows[...].T
    gate = mixed[:, :hidden]
    up = mixed[:, hidden:]
    sig = jax.nn.sigmoid(gate)
    silu = gate * sig
    act_ref[...] = (silu * up).astype(BF16).T
    gate_ref[...] = up * sig * (1.0 + gate * (1.0 - sig))
    up_ref[...] = silu


def expert_forward(pieces, weight, hidden, shifts, parts, part, before):
    sources = len(pieces)
    _, blocks, capacity, dim = pieces[0][0].shape
    group = 16 // sources
    tile = sources * group * capacity
    steps = blocks // group
    total = tile * steps * parts
    at = lambda i: i + part * steps
    row_spec = lambda width: pl.BlockSpec((tile, width), lambda i, p: (at(i), 0))
    column_spec = lambda height: pl.BlockSpec((height, tile), lambda i, p: (0, at(i)))

    def piece_spec(unit, shift):
        return pl.BlockSpec(
            (1, group, capacity, dim),
            lambda i, p: (unit if shift is None else unit + p[shift], i, 0, 0),
        )

    return pl.pallas_call(
        functools.partial(forward_kernel, sources),
        grid_spec=pltpu.PrefetchScalarGridSpec(
            num_scalar_prefetch=1,
            grid=(steps,),
            in_specs=[piece_spec(unit, shift) for _, unit, shift in pieces]
            + [pl.BlockSpec((dim, 2 * hidden), lambda i, p: (0, 0))]
            + [pl.BlockSpec(memory_space=pl.ANY)] * len(before),
            out_specs=[column_spec(dim), column_spec(hidden), row_spec(hidden), row_spec(hidden)],
            scratch_shapes=[pltpu.VMEM((tile, dim), BF16)],
        ),
        out_shape=[
            jax.ShapeDtypeStruct((dim, total), BF16),
            jax.ShapeDtypeStruct((hidden, total), BF16),
            jax.ShapeDtypeStruct((total, hidden), F32),
            jax.ShapeDtypeStruct((total, hidden), F32),
        ],
        input_output_aliases={sources + 2 + i: i for i in range(len(before))},
        compiler_params=pltpu.CompilerParams(vmem_limit_bytes=VMEM_LIMIT),
        cost_estimate=call_cost(
            4 * total * dim * hidden // parts, (4 * total * dim + 10 * total * hidden) // parts
        ),
        name="expert_forward",
    )(shifts, *[array for array, _, _ in pieces], weight, *before)


def backward_kernel(places, arrays, *refs):
    grad_refs = refs[:arrays]
    gate_ref, up_ref, weight_ref, rows_ref, act_ref, out_ref = refs[arrays : arrays + 6]
    grads_all, hidden_all, sems = refs[arrays + 6 :]
    step = pl.program_id(0)
    tile = gate_ref.shape[0]
    hidden = act_ref.shape[0]
    width = rows_ref.shape[0]
    row_steps = grads_all.shape[0] // tile
    copies = []
    for index, (array, unit, row, size) in enumerate(places):
        copy = pltpu.make_async_copy(
            grad_refs[array].at[unit], grads_all.at[pl.ds(row, size)], sems.at[index]
        )
        copies.append((row // tile, copy))

    @pl.when(step == 0)
    def _():
        for turn in range(row_steps):
            for at, copy in copies:
                if at == turn:
                    copy.start()

    for turn in range(row_steps):

        @pl.when(step == turn)
        def _():
            for at, copy in copies:
                if at == turn:
                    copy.wait()

    @pl.when(step < row_steps)
    def _():
        where = pl.ds(pl.multiple_of(step * tile, tile), tile)
        act_grad = jnp.dot(grads_all[where], weight_ref[...], preferred_element_type=F32)
        hidden_all[where, :hidden] = (act_grad * gate_ref[...]).astype(BF16)
        hidden_all[where, hidden:] = (act_grad * up_ref[...]).astype(BF16)

    @pl.when(step >= row_steps)
    def _():
        columns = pl.ds(pl.multiple_of((step - row_steps) * width, width), width)
        out_ref[:, : 2 * hidden] = jnp.dot(
            rows_ref[...], hidden_all[...], preferred_element_type=F32
        ).astype(BF16)
        down = jnp.dot(act_ref[...], grads_all[:, columns], preferred_element_type=F32)
        out_ref[:, 2 * hidden :] = down.T.astype(BF16)


def expert_backward(arrays, places, gate, up, weights, rows, act):
    dim, total = rows.shape
    hidden = act.shape[0]
    tile, width = 512, 768
    row_steps, column_steps = total // tile, dim // width
    row_spec = lambda cols: pl.BlockSpec(
        (tile, cols), lambda i: (jnp.minimum(i, row_steps - 1), 0)
    )
    column_of = lambda i: jnp.maximum(i - row_steps, 0)
    return pl.pallas_call(
        functools.partial(backward_kernel, places, len(arrays)),
        grid=(row_steps + column_steps,),
        in_specs=[pl.BlockSpec(memory_space=pl.ANY)] * len(arrays)
        + [
            row_spec(hidden),
            row_spec(hidden),
            pl.BlockSpec((dim, hidden), lambda i: (0, 2)),
            pl.BlockSpec((width, total), lambda i: (column_of(i), 0)),
            pl.BlockSpec((hidden, total), lambda i: (0, 0)),
        ],
        out_specs=pl.BlockSpec((width, 3 * hidden), lambda i: (column_of(i), 0)),
        out_shape=jax.ShapeDtypeStruct((dim, 3 * hidden), BF16),
        scratch_shapes=[
            pltpu.VMEM((total, dim), BF16),
            pltpu.VMEM((total, 2 * hidden), BF16),
            pltpu.SemaphoreType.DMA((len(places),)),
        ],
        compiler_params=pltpu.CompilerParams(vmem_limit_bytes=VMEM_LIMIT),
        cost_estimate=call_cost(8 * total * dim * hidden, 4 * total * dim + 20 * total * hidden),
        name="expert_backward",
    )(*arrays, gate, up, weights, rows, act)


def merge_kernel(plans, arrays, shift_ref, *refs):
    sources, refs = refs[:arrays], refs[arrays + refs_after(refs, arrays, plans) :]
    outs, buffers = refs[: len(plans)], refs[len(plans) : 2 * len(plans)]
    in_sems, out_sems = refs[2 * len(plans) :]
    reads, count = [], 0
    for plan, buffer in zip(plans, buffers):
        copies = []
        for at, (array, unit, shift) in enumerate(plan):
            first = unit if shift is None else unit + shift_ref[shift]
            half = buffer.shape[1] // 2
            for piece in range(2):
                rows = pl.ds(piece * half, half)
                copies.append(
                    pltpu.make_async_copy(
                        sources[array].at[first, rows], buffer.at[at, rows], in_sems.at[count]
                    )
                )
                count += 1
        reads.append(copies)
    for copies in reads:
        for copy in copies:
            copy.start()
    writes = []
    for index, copies in enumerate(reads):
        for copy in copies:
            copy.wait()
        writes.append(pltpu.make_async_copy(buffers[index], outs[index], out_sems.at[index]))
        writes[-1].start()
    for copy in writes:
        copy.wait()


def refs_after(refs, arrays, plans):
    return len(refs) - arrays - 2 * len(plans) - 2


def merge(shifts, messages, after=()):
    arrays, plans = [], []
    for parts in messages:
        plan = []
        for array, units, shift in parts:
            known = [i for i, other in enumerate(arrays) if other is array]
            if not known:
                arrays.append(array)
                known = [len(arrays) - 1]
            plan += [(known[0], unit, shift) for unit in units]
        plans.append(tuple(plan))
    shapes = [(len(plan),) + arrays[plan[0][0]].shape[1:] for plan in plans]
    size = sum(functools.reduce(lambda a, b: a * b, shape, 1) for shape in shapes)
    any_spec = pl.BlockSpec(memory_space=pl.ANY)
    return pl.pallas_call(
        functools.partial(merge_kernel, tuple(plans), len(arrays)),
        grid_spec=pltpu.PrefetchScalarGridSpec(
            num_scalar_prefetch=1,
            grid=(1,),
            in_specs=[any_spec] * (len(arrays) + len(after)),
            out_specs=[any_spec] * len(plans),
            scratch_shapes=[pltpu.VMEM(shape, BF16) for shape in shapes]
            + [
                pltpu.SemaphoreType.DMA((2 * sum(len(plan) for plan in plans),)),
                pltpu.SemaphoreType.DMA((len(plans),)),
            ],
        ),
        out_shape=[jax.ShapeDtypeStruct(shape, BF16) for shape in shapes],
        compiler_params=pltpu.CompilerParams(vmem_limit_bytes=VMEM_LIMIT),
        cost_estimate=call_cost(0, 4 * size),
        name="merge_rows",
    )(shifts, *arrays, *after)


def swap(array, axis, flip):
    count = lax.axis_size(axis)
    return lax.ppermute(array, axis, [(i, i ^ flip) for i in range(count)])


def mask_of(flips, bits):
    return functools.reduce(lambda a, b: a ^ b, [f for f, bit in zip(flips, bits) if bit], 0)


def flips_of(half):
    return (1, 3) if half == 0 else (3, 1)


def swap_gather(array, axis, flip):
    count = lax.axis_size(axis)
    groups = [[i, i ^ flip] for i in range(count) if i < i ^ flip]
    both = lax.all_gather(array, axis, axis_index_groups=groups)
    return both.reshape((-1,) + array.shape[1:])


def second_parts(keep, first):
    return [(keep, range(4, 8), None), (first, range(4, 8), None)]


def third_parts(keep, first, second):
    return [
        (keep, (2, 3), None),
        (first, (2, 3), None),
        (second, (2, 3, 6, 7), None),
    ]


def fourth_parts(keep, first, second, third):
    return [
        (keep, (1,), None),
        (first, (1,), None),
        (second, (1, 5), None),
        (third, (1, 3, 5, 7), None),
    ]


def grad_places(flips):
    found = {}
    found[0, 0, 0, 0] = (0, 0)
    found[1, 0, 0, 0] = (1, 0)
    found[0, 1, 0, 0] = (2, 0)
    found[1, 1, 0, 0] = (2, 4)
    for index, start in enumerate([(0, 0), (1, 0), (0, 1), (1, 1)]):
        found[start + (1, 0)] = (3, 2 * index)
        found[start + (0, 1)] = (4, index)
        found[start + (1, 1)] = (4, 4 + index)
    return {mask_of(flips, bits): at for bits, at in found.items()}


def per_device(
    qkv_in,
    qkv_grad,
    conv_weight,
    doc_ids,
    qkv_weight,
    resid,
    norm_gain,
    out_grad,
    routes,
    route_weights,
    expert_weights,
):
    rows, width = qkv_in.shape
    tokens, dim = resid.shape
    per_token = routes.shape[1]
    hidden = expert_weights.shape[2] // 3
    n_seq, n_exp = lax.axis_size("seq"), lax.axis_size("exp")
    experts = n_seq * n_exp
    capacity = 2 * tokens * per_token // experts
    seq_index, exp_index = lax.axis_index("seq"), lax.axis_index("exp")
    own_weights = expert_weights[0]

    place = jnp.stack([seq_index, exp_index]).astype(jnp.int32)
    forward = [(i, i + 1) for i in range(n_exp - 1)]
    backward = [(i + 1, i) for i in range(n_exp - 1)]
    low = lax.ppermute(qkv_in[-HALO:], "exp", forward)
    high = lax.ppermute(qkv_in[:HALO], "exp", backward)
    grad_high = lax.ppermute(qkv_grad[:HALO], "exp", backward)
    weight_far = swap(qkv_weight, "seq", 1)

    table = jnp.concatenate([routes.astype(F32), route_weights], 1).T
    tables = jnp.broadcast_to(table[None], (n_seq,) + table.shape)
    tables = lax.all_to_all(tables, "seq", split_axis=0, concat_axis=0, tiled=True)
    normed = norm_rows(resid, norm_gain, routes.T)
    normed, conv_weight = lax.optimization_barrier((normed, conv_weight))
    exp_normed = lax.all_gather(normed, "exp")

    edge = jnp.full((HALO,), -1, jnp.int32)
    ids = lax.dynamic_slice_in_dim(
        jnp.concatenate([edge, doc_ids, edge]), exp_index * rows, rows + 2 * HALO
    )
    local_grad, local_keep, local_send = conv_back(
        place, qkv_in, low, high, qkv_grad, grad_high, ids.reshape(-1, 1), conv_weight, tokens
    )
    local_send, tables = lax.optimization_barrier((local_send, tables))
    local_got = swap(local_send, "seq", 1)
    partial = project(place, local_keep, local_got, qkv_weight, weight_far, out_grad)
    same_core = [[s for s in range(n_seq) if s % 2 == core] for core in range(2)]
    flow = lax.psum(partial, "seq", axis_index_groups=same_core)

    flips_a, flips_b = flips_of(0), flips_of(1)
    shifts = [(seq_index < seq_index ^ 2 * f).astype(jnp.int32) * 4 for f in flips_b]
    shifts = jnp.stack(shifts)
    turns = []
    for near in (flips_a, flips_b):
        near = (0, near[1], near[0], near[0] ^ near[1])
        turns.append(tuple(2 * m for m in near) + tuple(2 * m + 1 for m in near))
    picks = pick_norm(place, exp_normed, tuple(turns), dim, per_token, capacity)
    (keep_a, send_a, keep_far_a, send_far_a) = picks[:4]
    (keep_b, send_b, keep_far_b, send_far_b) = picks[4:]
    got_a, got_b = swap(send_far_a, "seq", 1), swap(send_far_b, "seq", 1)
    message_a, message_b = merge(
        shifts,
        [
            [(send_a, (0, 1), None), (got_a, (0, 1), None)],
            [(send_b, (0, 1), None), (got_b, (0, 1), None)],
        ],
    )
    first_a = swap(message_a, "seq", 2 * flips_a[0])
    far_a, far_b = swap(keep_far_a, "seq", 1), swap(keep_far_b, "seq", 1)
    flow, far_a, far_b, message_b, local_grad = lax.optimization_barrier(
        (flow, far_a, far_b, message_b, local_grad)
    )
    first_b = swap_gather(message_b, "seq", 2 * flips_b[0])
    qkv_in_grad = lax.all_to_all(local_grad, "seq", split_axis=0, concat_axis=1, tiled=True)
    flow_far = swap(flow, "seq", 1)

    flips = (1, 3, 4, 12)
    quarters = len(flips)
    orders = [flips[k:] + flips[:k] for k in range(quarters)]
    bit_rows = [tuple((j >> (3 - b)) & 1 for b in range(4)) for j in range(n_exp)]
    turns = tuple(tuple(mask_of(order, bits) for bits in bit_rows) for order in orders)
    sends = pick_grad(place, tables, (flow, flow_far), turns, n_exp, per_token, capacity)

    streams = range(quarters)
    keeps = [sends[2 * k] for k in streams]
    firsts = [swap(sends[2 * k + 1], "exp", orders[k][0]) for k in streams]
    messages = merge(shifts, [second_parts(keeps[k], firsts[k]) for k in streams])
    seconds = [swap(messages[k], "exp", orders[k][1]) for k in streams]
    (message_a,) = merge(
        shifts,
        [[(keep_a, (1,), None), (far_a, (1,), None), (first_a, (1, 3), None)]],
        messages,
    )
    (message_b,) = merge(
        shifts,
        [[(keep_b, (1,), None), (far_b, (1,), None), (first_b, (1, 3), 0)]],
        messages,
    )
    second_a = swap(message_a, "seq", 2 * flips_a[1])
    second_b = swap_gather(message_b, "seq", 2 * flips_b[1])
    calls = [
        [(keep_a, 0, None), (far_a, 0, None), (first_a, 0, None), (first_a, 2, None)],
        [(keep_b, 0, None), (far_b, 0, None), (first_b, 0, 0), (first_b, 2, 0)],
        [(second_a, i, None) for i in range(4)],
        [(second_b, i, 1) for i in range(4)],
    ]
    messages = merge(shifts, [third_parts(keeps[k], firsts[k], seconds[k]) for k in streams])
    thirds = [swap(messages[k], "exp", orders[k][2]) for k in streams]
    results = ()
    for part, pieces in enumerate(calls):
        results = expert_forward(
            pieces, own_weights, hidden, shifts, len(calls), part, results
        )
        if part == 1:
            results, thirds = lax.optimization_barrier((results, thirds))
    rows_all, act, gate, up = results

    def row_of(mask, quarter):
        half, inner = mask >> 3, mask & 7
        flips = flips_of(half)
        order = (0, flips[0], flips[1], flips[0] ^ flips[1])
        spot = order.index(quarter)
        call = (spot >> 1) * 2 + half
        tile = call * 2 + (inner >> 2)
        return tile * n_exp * capacity + (inner & 3) * 4 * capacity + (spot & 1) * 2 * capacity

    messages = merge(
        shifts, [fourth_parts(keeps[k], firsts[k], seconds[k], thirds[k]) for k in streams]
    )
    fourths = [swap(messages[k], "exp", orders[k][3]) for k in streams]
    arrays, places = [], []
    for k in streams:
        got = [keeps[k], firsts[k], seconds[k], thirds[k], fourths[k]]
        for mask, (array, unit) in sorted(grad_places(orders[k]).items()):
            places.append((len(arrays) + array, unit, row_of(mask, k), 2 * capacity))
        arrays += got
    expert_grads = expert_backward(arrays, tuple(places), gate, up, own_weights, rows_all, act)
    return (qkv_in_grad, expert_grads[None])


def solution(mesh):
    return jax.shard_map(
        per_device,
        mesh=mesh,
        in_specs=(
            P("exp", "seq"),
            P("exp", "seq"),
            P(None, "seq"),
            P(),
            P("seq", None),
            P(("exp", "seq"), None),
            P(),
            P(("exp", "seq"), None),
            P(("exp", "seq"), None),
            P(("exp", "seq"), None),
            P(("seq", "exp"), None, None),
        ),
        out_specs=(P(("exp", "seq"), None), P(("seq", "exp"), None, None)),
        check_vma=False,
    )
```

```python
import functools

import jax
import jax.numpy as jnp
from jax import lax
from jax.experimental import pallas as pl
from jax.experimental.pallas import tpu as pltpu
from jax.sharding import PartitionSpec as P

BF16 = jnp.bfloat16
F32 = jnp.float32
HALO = 16
MIB = 1024 * 1024
VMEM_LIMIT = 127 * MIB // 2
EXTRA = 128


def call_cost(flops, nbytes):
    return pl.CostEstimate(flops=int(flops), bytes_accessed=int(nbytes), transcendentals=0)


def norm_kernel(resid_ref, gain_ref, routes_ref, out_ref):
    rows = resid_ref[...].astype(F32)
    dim = rows.shape[1]
    scale = lax.rsqrt(jnp.mean(rows * rows, axis=1, keepdims=True) + 1e-06)
    out_ref[:, :dim] = (rows * scale * gain_ref[...]).astype(BF16)
    out_ref[:, dim:] = jnp.zeros((rows.shape[0], EXTRA), BF16)
    names = routes_ref[...].astype(F32)
    pad = jnp.zeros((HALO - names.shape[0], EXTRA), F32)
    out_ref[:HALO, dim:] = jnp.concatenate([names, pad]).astype(BF16)


def norm_rows(resid, gain, names):
    tokens, dim = resid.shape
    return pl.pallas_call(
        norm_kernel,
        out_shape=jax.ShapeDtypeStruct((tokens, dim + EXTRA), BF16),
        compiler_params=pltpu.CompilerParams(vmem_limit_bytes=VMEM_LIMIT),
        cost_estimate=call_cost(resid.size * 6, resid.size * 4),
        name="norm_rows",
    )(resid, gain.reshape(1, -1), names)


def conv_kernel(
    tile,
    place_ref,
    in_ref,
    in_low_ref,
    in_high_ref,
    grad_ref,
    grad_high_ref,
    ids_ref,
    taps_ref,
    local_ref,
    keep_ref,
    send_ref,
    in_ext,
    grad_ext,
):
    step = pl.program_id(0)
    rows = in_ref.shape[0]

    @pl.when(step == 0)
    def _():
        in_ext[:HALO] = in_low_ref[...].astype(F32)
        in_ext[HALO : HALO + rows] = in_ref[...].astype(F32)
        in_ext[HALO + rows :] = in_high_ref[...].astype(F32)
        grad_ext[:rows] = grad_ref[...].astype(F32)
        grad_ext[rows:] = grad_high_ref[...].astype(F32)

    first = pl.multiple_of(step * tile, tile)
    span = tile + 8
    taps = taps_ref[...]
    window = in_ext[pl.ds(first + HALO - 8, span + 8)]
    ids = ids_ref[pl.ds(first + HALO - 8, span + 8)]
    here = ids[8:]
    same = [None] + [(ids[8 - j : 8 - j + span] == here).astype(F32) for j in (1, 2, 3)]
    conv = taps[0:1] * window[8:]
    for j in (1, 2, 3):
        conv = conv + taps[j : j + 1] * window[8 - j : 8 - j + span] * same[j]
    gate = jax.nn.sigmoid(conv)
    pre = grad_ext[pl.ds(first, span)] * gate * (1.0 + conv * (1.0 - gate))
    result = taps[0:1] * pre[:tile]
    for j in (1, 2, 3):
        result = result + taps[j : j + 1] * (pre * same[j])[j : j + tile]
    local = result.astype(BF16)
    local_ref[...] = local
    half = tile // 2
    core = place_ref[0] & 1

    @pl.when(core == 0)
    def _():
        keep_ref[...] = local[:half]
        send_ref[...] = local[half:]

    @pl.when(core == 1)
    def _():
        keep_ref[...] = local[half:]
        send_ref[...] = local[:half]


def conv_back(place, qkv_in, low, high, qkv_grad, grad_high, ids, taps, block):
    rows, width = qkv_in.shape
    tile = 2 * block
    whole = lambda shape: pl.BlockSpec(shape, lambda i, p: (0,) * len(shape))
    part = lambda size: pl.BlockSpec((size, width), lambda i, p: (i, 0))
    return pl.pallas_call(
        functools.partial(conv_kernel, tile),
        grid_spec=pltpu.PrefetchScalarGridSpec(
            num_scalar_prefetch=1,
            grid=(rows // tile,),
            in_specs=[
                whole(qkv_in.shape),
                whole(low.shape),
                whole(high.shape),
                whole(qkv_grad.shape),
                whole(grad_high.shape),
                whole(ids.shape),
                whole(taps.shape),
            ],
            out_specs=[part(tile), part(block), part(block)],
            scratch_shapes=[
                pltpu.VMEM((rows + 2 * HALO, width), F32),
                pltpu.VMEM((rows + HALO, width), F32),
            ],
        ),
        out_shape=[
            jax.ShapeDtypeStruct((rows, width), BF16),
            jax.ShapeDtypeStruct((rows // 2, width), BF16),
            jax.ShapeDtypeStruct((rows // 2, width), BF16),
        ],
        compiler_params=pltpu.CompilerParams(vmem_limit_bytes=VMEM_LIMIT),
        cost_estimate=call_cost(40 * rows * width, 8 * rows * width),
        name="conv_back",
    )(place, qkv_in, low, high, qkv_grad, grad_high, ids, taps)


def project_kernel(place_ref, own_ref, other_ref, own_weight, other_weight, flow_ref, out_ref):
    block = flow_ref.shape[0]
    total = jnp.dot(own_ref[...], own_weight[...], preferred_element_type=F32)
    total = total + jnp.dot(other_ref[...], other_weight[...], preferred_element_type=F32)
    out_ref[...] = total.astype(BF16)
    for index in range(out_ref.shape[0] // block):

        @pl.when(index == place_ref[0] >> 1)
        def _():
            own = slice(index * block, (index + 1) * block)
            out_ref[own] = (total[own] + flow_ref[...].astype(F32)).astype(BF16)


def project(place, own, other, own_weight, other_weight, out_grad):
    rows, width = own.shape
    dim = own_weight.shape[1]
    tile = dim // 3
    whole = pl.BlockSpec((rows, width), lambda i, p: (0, 0))
    columns = lambda size: pl.BlockSpec((size, tile), lambda i, p: (0, i))
    return pl.pallas_call(
        project_kernel,
        grid_spec=pltpu.PrefetchScalarGridSpec(
            num_scalar_prefetch=1,
            grid=(dim // tile,),
            in_specs=[whole, whole, columns(width), columns(width), columns(out_grad.shape[0])],
            out_specs=columns(rows),
        ),
        out_shape=jax.ShapeDtypeStruct((rows, dim), BF16),
        compiler_params=pltpu.CompilerParams(vmem_limit_bytes=VMEM_LIMIT),
        cost_estimate=call_cost(4 * rows * width * dim, 4 * (rows + dim) * width + 2 * rows * dim),
        name="project",
    )(place, own, other, own_weight, other_weight, out_grad)


def slot_picker(names, own, capacity):
    count, tokens = own.shape
    match = [(names[k : k + 1] == own) for k in range(names.shape[0])]
    named = functools.reduce(jnp.logical_or, match)
    source = lax.broadcasted_iota(jnp.int32, (tokens, tokens), 0)
    target = lax.broadcasted_iota(jnp.int32, (tokens, tokens), 1)
    earlier = (source < target).astype(BF16)
    rank = jnp.dot(named.astype(BF16), earlier, preferred_element_type=F32).astype(jnp.int32)
    rank = jnp.where(named, rank, -1)
    slot = lax.broadcasted_iota(jnp.int32, (count, capacity, tokens), 1)
    picker = (rank[:, None, :] == slot).astype(F32)
    return picker, match


def pick_norm_kernel(per_token, capacity, n_exp, turns, place_ref, *refs):
    halves = len(turns)
    out_refs = refs[halves:]
    outs = len(out_refs) // halves
    for half in range(halves):
        rows_ref = refs[half]
        tokens = rows_ref.shape[1]
        dim = out_refs[0].shape[3]
        count = len(turns[half])
        names = rows_ref[0, :HALO, dim:].astype(F32)[:per_token].astype(jnp.int32)
        own = jnp.concatenate(
            [
                jnp.full((1, tokens), (place_ref[0] ^ t) * n_exp + place_ref[1], jnp.int32)
                for t in turns[half]
            ]
        )
        picker, _ = slot_picker(names, own, capacity)
        picker = picker.reshape(count * capacity, tokens).astype(BF16)
        picked = jnp.dot(picker, rows_ref[0, :, :dim], preferred_element_type=F32).astype(BF16)
        for index in range(count):
            out_refs[half * outs + index // 2][index % 2, 0] = picked[
                index * capacity : (index + 1) * capacity
            ]


def pick_norm(place, rows, turns, dim, per_token, capacity):
    blocks, tokens, width = rows.shape
    halves = len(turns)
    count = blocks // halves
    outs = len(turns[0]) // 2 * halves
    row_spec = lambda first: pl.BlockSpec(
        (1, tokens, width), lambda i, p: (p[1] ^ (i + first), 0, 0)
    )
    return pl.pallas_call(
        functools.partial(pick_norm_kernel, per_token, capacity, blocks, turns),
        grid_spec=pltpu.PrefetchScalarGridSpec(
            num_scalar_prefetch=1,
            grid=(count,),
            in_specs=[row_spec(half * count) for half in range(halves)],
            out_specs=[pl.BlockSpec((2, 1, capacity, dim), lambda i, p: (0, i, 0, 0))] * outs,
        ),
        out_shape=[jax.ShapeDtypeStruct((2, count, capacity, dim), BF16)] * outs,
        compiler_params=pltpu.CompilerParams(vmem_limit_bytes=VMEM_LIMIT),
        cost_estimate=call_cost(
            2 * len(turns[0]) * capacity * blocks * tokens * dim,
            2 * dim * blocks * (tokens + len(turns[0]) * capacity),
        ),
        name="pick_norm",
    )(place, *[rows] * halves)


def pick_grad_kernel(per_token, capacity, n_exp, turns, place_ref, tables_ref, *refs):
    flow_refs, out_refs = refs[:2], refs[2:-2]
    buffer, sems = refs[-2:]
    tokens = tables_ref.shape[2]
    copies = []
    for quarter, turn in enumerate(turns):
        count = len(turn)
        own = jnp.concatenate(
            [
                jnp.full((1, tokens), place_ref[0] * n_exp + (place_ref[1] ^ t), jnp.int32)
                for t in turn
            ]
        )
        first = pl.multiple_of(((place_ref[0] >> 1) ^ quarter) * tokens, tokens)
        for core in range(2):
            table = tables_ref[place_ref[0] ^ (2 * quarter + core)]
            names = table[:per_token].astype(jnp.int32)
            picker, match = slot_picker(names, own, capacity)
            weights = table[per_token:]
            scale = functools.reduce(
                jnp.add, [jnp.where(match[k], weights[k : k + 1], 0.0) for k in range(per_token)]
            )
            scales = jnp.sum(picker * scale[:, None, :], axis=2, keepdims=True)
            picker = picker.reshape(count * capacity, tokens).astype(BF16)
            picked = jnp.dot(
                picker, flow_refs[core][pl.ds(first, tokens)], preferred_element_type=F32
            )
            picked = (picked * scales.reshape(count * capacity, 1)).astype(BF16)
            for index in range(count):
                buffer[quarter, index, core * capacity : (core + 1) * capacity] = picked[
                    index * capacity : (index + 1) * capacity
                ]
        copy = pltpu.make_async_copy(buffer.at[quarter], out_refs[quarter], sems.at[quarter])
        copy.start()
        copies.append(copy)
    for copy in copies:
        copy.wait()


def pick_grad(place, tables, flows, turns, n_exp, per_token, capacity):
    dim = flows[0].shape[1]
    rows, count = 2 * capacity, len(turns[0])
    whole = lambda array: pl.BlockSpec(array.shape, lambda i, p: (0,) * array.ndim)
    outs = len(turns)
    return pl.pallas_call(
        functools.partial(pick_grad_kernel, per_token, capacity, n_exp, turns),
        grid_spec=pltpu.PrefetchScalarGridSpec(
            num_scalar_prefetch=1,
            grid=(1,),
            in_specs=[whole(tables), whole(flows[0]), whole(flows[1])],
            out_specs=[pl.BlockSpec(memory_space=pl.ANY)] * outs,
            scratch_shapes=[
                pltpu.VMEM((len(turns), count, rows, dim), BF16),
                pltpu.SemaphoreType.DMA((outs,)),
            ],
        ),
        out_shape=[jax.ShapeDtypeStruct((count, rows, dim), BF16)] * outs,
        compiler_params=pltpu.CompilerParams(vmem_limit_bytes=VMEM_LIMIT),
        cost_estimate=call_cost(
            2 * len(turns) * count * rows * tables.shape[2] * dim,
            4 * dim * (flows[0].shape[0] + len(turns) * count * rows // 2),
        ),
        name="pick_grad",
    )(place, tables, *flows)


def forward_kernel(sources, *refs):
    row_refs = refs[1 : 1 + sources]
    weight_ref = refs[1 + sources]
    rows_out, act_ref, gate_ref, up_ref, rows = refs[-5:]
    _, group, capacity, _ = row_refs[0].shape
    for inner in range(group):
        for index in range(sources):
            at = (inner * sources + index) * capacity
            rows[at : at + capacity] = row_refs[index][0, inner]
    hidden = act_ref.shape[0]
    mixed = jnp.dot(rows[...], weight_ref[...], preferred_element_type=F32)
    rows_out[...] = rows[...].T
    gate = mixed[:, :hidden]
    up = mixed[:, hidden:]
    sig = jax.nn.sigmoid(gate)
    silu = gate * sig
    act_ref[...] = (silu * up).astype(BF16).T
    gate_ref[...] = (up * sig * (1.0 + gate * (1.0 - sig))).astype(BF16)
    up_ref[...] = silu.astype(BF16)


def expert_forward(pieces, weight, hidden, shifts, parts, part, before):
    sources = len(pieces)
    _, blocks, capacity, dim = pieces[0][0].shape
    group = 16 // sources
    tile = sources * group * capacity
    steps = blocks // group
    total = tile * steps * parts
    at = lambda i: i + part * steps
    row_spec = lambda width: pl.BlockSpec((tile, width), lambda i, p: (at(i), 0))
    column_spec = lambda height: pl.BlockSpec((height, tile), lambda i, p: (0, at(i)))

    def piece_spec(unit, shift):
        return pl.BlockSpec(
            (1, group, capacity, dim),
            lambda i, p: (unit if shift is None else unit + p[shift], i, 0, 0),
        )

    return pl.pallas_call(
        functools.partial(forward_kernel, sources),
        grid_spec=pltpu.PrefetchScalarGridSpec(
            num_scalar_prefetch=1,
            grid=(steps,),
            in_specs=[piece_spec(unit, shift) for _, unit, shift in pieces]
            + [pl.BlockSpec((dim, 2 * hidden), lambda i, p: (0, 0))]
            + [pl.BlockSpec(memory_space=pl.ANY)] * len(before),
            out_specs=[column_spec(dim), column_spec(hidden), row_spec(hidden), row_spec(hidden)],
            scratch_shapes=[pltpu.VMEM((tile, dim), BF16)],
        ),
        out_shape=[
            jax.ShapeDtypeStruct((dim, total), BF16),
            jax.ShapeDtypeStruct((hidden, total), BF16),
            jax.ShapeDtypeStruct((total, hidden), BF16),
            jax.ShapeDtypeStruct((total, hidden), BF16),
        ],
        input_output_aliases={sources + 2 + i: i for i in range(len(before))},
        compiler_params=pltpu.CompilerParams(vmem_limit_bytes=VMEM_LIMIT),
        cost_estimate=call_cost(
            4 * total * dim * hidden // parts, (4 * total * dim + 10 * total * hidden) // parts
        ),
        name="expert_forward",
    )(shifts, *[array for array, _, _ in pieces], weight, *before)


def backward_kernel(places, arrays, *refs):
    grad_refs = refs[:arrays]
    gate_ref, up_ref, weight_ref, rows_ref, act_ref, out_ref = refs[arrays : arrays + 6]
    grads_all, hidden_all, sems = refs[arrays + 6 :]
    step = pl.program_id(0)
    tile = gate_ref.shape[0]
    hidden = act_ref.shape[0]
    width = rows_ref.shape[0]
    row_steps = grads_all.shape[0] // tile
    copies = []
    for index, (array, unit, row, size) in enumerate(places):
        copy = pltpu.make_async_copy(
            grad_refs[array].at[unit], grads_all.at[pl.ds(row, size)], sems.at[index]
        )
        copies.append((row // tile, copy))

    @pl.when(step == 0)
    def _():
        for turn in range(row_steps):
            for at, copy in copies:
                if at == turn:
                    copy.start()

    for turn in range(row_steps):

        @pl.when(step == turn)
        def _():
            for at, copy in copies:
                if at == turn:
                    copy.wait()

    @pl.when(step < row_steps)
    def _():
        where = pl.ds(pl.multiple_of(step * tile, tile), tile)
        act_grad = jnp.dot(grads_all[where], weight_ref[...], preferred_element_type=F32)
        hidden_all[where, :hidden] = (act_grad * gate_ref[...].astype(F32)).astype(BF16)
        hidden_all[where, hidden:] = (act_grad * up_ref[...].astype(F32)).astype(BF16)

    @pl.when(step >= row_steps)
    def _():
        columns = pl.ds(pl.multiple_of((step - row_steps) * width, width), width)
        out_ref[:, : 2 * hidden] = jnp.dot(
            rows_ref[...], hidden_all[...], preferred_element_type=F32
        ).astype(BF16)
        down = jnp.dot(act_ref[...], grads_all[:, columns], preferred_element_type=F32)
        out_ref[:, 2 * hidden :] = down.T.astype(BF16)


def expert_backward(arrays, places, gate, up, weights, rows, act):
    dim, total = rows.shape
    hidden = act.shape[0]
    tile, width = 512, 768
    row_steps, column_steps = total // tile, dim // width
    row_spec = lambda cols: pl.BlockSpec(
        (tile, cols), lambda i: (jnp.minimum(i, row_steps - 1), 0)
    )
    column_of = lambda i: jnp.maximum(i - row_steps, 0)
    return pl.pallas_call(
        functools.partial(backward_kernel, places, len(arrays)),
        grid=(row_steps + column_steps,),
        in_specs=[pl.BlockSpec(memory_space=pl.ANY)] * len(arrays)
        + [
            row_spec(hidden),
            row_spec(hidden),
            pl.BlockSpec((dim, hidden), lambda i: (0, 2)),
            pl.BlockSpec((width, total), lambda i: (column_of(i), 0)),
            pl.BlockSpec((hidden, total), lambda i: (0, 0)),
        ],
        out_specs=pl.BlockSpec((width, 3 * hidden), lambda i: (column_of(i), 0)),
        out_shape=jax.ShapeDtypeStruct((dim, 3 * hidden), BF16),
        scratch_shapes=[
            pltpu.VMEM((total, dim), BF16),
            pltpu.VMEM((total, 2 * hidden), BF16),
            pltpu.SemaphoreType.DMA((len(places),)),
        ],
        compiler_params=pltpu.CompilerParams(vmem_limit_bytes=VMEM_LIMIT),
        cost_estimate=call_cost(8 * total * dim * hidden, 4 * total * dim + 20 * total * hidden),
        name="expert_backward",
    )(*arrays, gate, up, weights, rows, act)


def merge_kernel(plans, arrays, shift_ref, *refs):
    sources, refs = refs[:arrays], refs[arrays + refs_after(refs, arrays, plans) :]
    outs, buffers = refs[: len(plans)], refs[len(plans) : 2 * len(plans)]
    in_sems, out_sems = refs[2 * len(plans) :]
    reads, count = [], 0
    for plan, buffer in zip(plans, buffers):
        copies = []
        for at, (array, unit, shift) in enumerate(plan):
            first = unit if shift is None else unit + shift_ref[shift]
            half = buffer.shape[1] // 2
            for piece in range(2):
                rows = pl.ds(piece * half, half)
                copies.append(
                    pltpu.make_async_copy(
                        sources[array].at[first, rows], buffer.at[at, rows], in_sems.at[count]
                    )
                )
                count += 1
        reads.append(copies)
    for copies in reads:
        for copy in copies:
            copy.start()
    writes = []
    for index, copies in enumerate(reads):
        for copy in copies:
            copy.wait()
        writes.append(pltpu.make_async_copy(buffers[index], outs[index], out_sems.at[index]))
        writes[-1].start()
    for copy in writes:
        copy.wait()


def refs_after(refs, arrays, plans):
    return len(refs) - arrays - 2 * len(plans) - 2


def merge(shifts, messages, after=()):
    arrays, plans = [], []
    for parts in messages:
        plan = []
        for array, units, shift in parts:
            known = [i for i, other in enumerate(arrays) if other is array]
            if not known:
                arrays.append(array)
                known = [len(arrays) - 1]
            plan += [(known[0], unit, shift) for unit in units]
        plans.append(tuple(plan))
    shapes = [(len(plan),) + arrays[plan[0][0]].shape[1:] for plan in plans]
    size = sum(functools.reduce(lambda a, b: a * b, shape, 1) for shape in shapes)
    any_spec = pl.BlockSpec(memory_space=pl.ANY)
    return pl.pallas_call(
        functools.partial(merge_kernel, tuple(plans), len(arrays)),
        grid_spec=pltpu.PrefetchScalarGridSpec(
            num_scalar_prefetch=1,
            grid=(1,),
            in_specs=[any_spec] * (len(arrays) + len(after)),
            out_specs=[any_spec] * len(plans),
            scratch_shapes=[pltpu.VMEM(shape, BF16) for shape in shapes]
            + [
                pltpu.SemaphoreType.DMA((2 * sum(len(plan) for plan in plans),)),
                pltpu.SemaphoreType.DMA((len(plans),)),
            ],
        ),
        out_shape=[jax.ShapeDtypeStruct(shape, BF16) for shape in shapes],
        compiler_params=pltpu.CompilerParams(vmem_limit_bytes=VMEM_LIMIT),
        cost_estimate=call_cost(0, 4 * size),
        name="merge_rows",
    )(shifts, *arrays, *after)


def swap(array, axis, flip):
    count = lax.axis_size(axis)
    return lax.ppermute(array, axis, [(i, i ^ flip) for i in range(count)])


def mask_of(flips, bits):
    return functools.reduce(lambda a, b: a ^ b, [f for f, bit in zip(flips, bits) if bit], 0)


def flips_of(half):
    return (1, 3) if half == 0 else (3, 1)


def swap_gather(array, axis, flip):
    count = lax.axis_size(axis)
    groups = [[i, i ^ flip] for i in range(count) if i < i ^ flip]
    both = lax.all_gather(array, axis, axis_index_groups=groups)
    return both.reshape((-1,) + array.shape[1:])


def second_parts(keep, first):
    return [(keep, range(4, 8), None), (first, range(4, 8), None)]


def third_parts(keep, first, second):
    return [
        (keep, (2, 3), None),
        (first, (2, 3), None),
        (second, (2, 3, 6, 7), None),
    ]


def fourth_parts(keep, first, second, third):
    return [
        (keep, (1,), None),
        (first, (1,), None),
        (second, (1, 5), None),
        (third, (1, 3, 5, 7), None),
    ]


def grad_places(flips):
    found = {}
    found[0, 0, 0, 0] = (0, 0)
    found[1, 0, 0, 0] = (1, 0)
    found[0, 1, 0, 0] = (2, 0)
    found[1, 1, 0, 0] = (2, 4)
    for index, start in enumerate([(0, 0), (1, 0), (0, 1), (1, 1)]):
        found[start + (1, 0)] = (3, 2 * index)
        found[start + (0, 1)] = (4, index)
        found[start + (1, 1)] = (4, 4 + index)
    return {mask_of(flips, bits): at for bits, at in found.items()}


def per_device(
    qkv_in,
    qkv_grad,
    conv_weight,
    doc_ids,
    qkv_weight,
    resid,
    norm_gain,
    out_grad,
    routes,
    route_weights,
    expert_weights,
):
    rows, width = qkv_in.shape
    tokens, dim = resid.shape
    per_token = routes.shape[1]
    hidden = expert_weights.shape[2] // 3
    n_seq, n_exp = lax.axis_size("seq"), lax.axis_size("exp")
    experts = n_seq * n_exp
    capacity = 2 * tokens * per_token // experts
    seq_index, exp_index = lax.axis_index("seq"), lax.axis_index("exp")
    own_weights = expert_weights[0]

    place = jnp.stack([seq_index, exp_index]).astype(jnp.int32)
    forward = [(i, i + 1) for i in range(n_exp - 1)]
    backward = [(i + 1, i) for i in range(n_exp - 1)]
    low = lax.ppermute(qkv_in[-HALO:], "exp", forward)
    high = lax.ppermute(qkv_in[:HALO], "exp", backward)
    grad_high = lax.ppermute(qkv_grad[:HALO], "exp", backward)
    weight_far = swap(qkv_weight, "seq", 1)

    table = jnp.concatenate([routes.astype(F32), route_weights], 1).T
    normed = norm_rows(resid, norm_gain, routes.T)
    normed, conv_weight = lax.optimization_barrier((normed, conv_weight))
    exp_normed = lax.all_gather(normed, "exp")

    edge = jnp.full((HALO,), -1, jnp.int32)
    ids = lax.dynamic_slice_in_dim(
        jnp.concatenate([edge, doc_ids, edge]), exp_index * rows, rows + 2 * HALO
    )
    local_grad, local_keep, local_send = conv_back(
        place, qkv_in, low, high, qkv_grad, grad_high, ids.reshape(-1, 1), conv_weight, tokens
    )
    local_got = swap(local_send, "seq", 1)
    partial = project(place, local_keep, local_got, qkv_weight, weight_far, out_grad)
    table, partial = lax.optimization_barrier((table, partial))
    tables = jnp.broadcast_to(table[None], (n_seq,) + table.shape)
    tables = lax.all_to_all(tables, "seq", split_axis=0, concat_axis=0, tiled=True)
    same_core = [[s for s in range(n_seq) if s % 2 == core] for core in range(2)]
    flow = lax.psum(partial, "seq", axis_index_groups=same_core)

    exp_normed, tables = lax.optimization_barrier((exp_normed, tables))
    flips_a, flips_b = flips_of(0), flips_of(1)
    shifts = [(seq_index < seq_index ^ 2 * f).astype(jnp.int32) * 4 for f in flips_b]
    shifts = jnp.stack(shifts)
    turns = []
    for near in (flips_a, flips_b):
        near = (0, near[1], near[0], near[0] ^ near[1])
        turns.append(tuple(2 * m for m in near) + tuple(2 * m + 1 for m in near))
    picks = pick_norm(place, exp_normed, tuple(turns), dim, per_token, capacity)
    (keep_a, send_a, keep_far_a, send_far_a) = picks[:4]
    (keep_b, send_b, keep_far_b, send_far_b) = picks[4:]
    got_a, got_b = swap(send_far_a, "seq", 1), swap(send_far_b, "seq", 1)
    message_a, message_b = merge(
        shifts,
        [
            [(send_a, (0, 1), None), (got_a, (0, 1), None)],
            [(send_b, (0, 1), None), (got_b, (0, 1), None)],
        ],
    )
    first_a = swap(message_a, "seq", 2 * flips_a[0])
    far_a, far_b = swap(keep_far_a, "seq", 1), swap(keep_far_b, "seq", 1)
    flow, far_a, far_b, message_b, local_grad = lax.optimization_barrier(
        (flow, far_a, far_b, message_b, local_grad)
    )
    first_b = swap_gather(message_b, "seq", 2 * flips_b[0])
    qkv_in_grad = lax.all_to_all(local_grad, "seq", split_axis=0, concat_axis=1, tiled=True)
    flow_far = swap(flow, "seq", 1)

    flips = (1, 3, 4, 12)
    quarters = len(flips)
    orders = [flips[k:] + flips[:k] for k in range(quarters)]
    bit_rows = [tuple((j >> (3 - b)) & 1 for b in range(4)) for j in range(n_exp)]
    turns = [[mask_of(order, bits) for bits in bit_rows] for order in orders]
    half = n_exp // 2
    flows = (flow, flow_far)
    sends = pick_grad(
        place, tables, flows, [t[half:] for t in turns], n_exp, per_token, capacity
    )
    keeps = pick_grad(
        place, tables, flows, [t[:half] for t in turns], n_exp, per_token, capacity
    )
    streams = range(quarters)
    firsts = [swap(sends[k], "exp", orders[k][0]) for k in streams]
    messages = merge(shifts, [second_parts(keeps[k], firsts[k]) for k in streams])
    seconds = [swap(messages[k], "exp", orders[k][1]) for k in streams]
    thirds_out = merge(shifts, [third_parts(keeps[k], firsts[k], seconds[k]) for k in streams])
    thirds = [swap(thirds_out[k], "exp", orders[k][2]) for k in streams]
    (message_a,) = merge(
        shifts,
        [[(keep_a, (1,), None), (far_a, (1,), None), (first_a, (1, 3), None)]],
        thirds_out,
    )
    (message_b,) = merge(
        shifts,
        [[(keep_b, (1,), None), (far_b, (1,), None), (first_b, (1, 3), 0)]],
        thirds_out,
    )
    second_a = swap(message_a, "seq", 2 * flips_a[1])
    second_b = swap_gather(message_b, "seq", 2 * flips_b[1])
    calls = [
        [(keep_a, 0, None), (far_a, 0, None), (first_a, 0, None), (first_a, 2, None)],
        [(keep_b, 0, None), (far_b, 0, None), (first_b, 0, 0), (first_b, 2, 0)],
        [(second_a, i, None) for i in range(4)],
        [(second_b, i, 1) for i in range(4)],
    ]
    results = ()
    for part, pieces in enumerate(calls):
        results = expert_forward(
            pieces, own_weights, hidden, shifts, len(calls), part, results
        )
        if part == 1:
            results, thirds = lax.optimization_barrier((results, thirds))
    rows_all, act, gate, up = results

    def row_of(mask, quarter):
        half, inner = mask >> 3, mask & 7
        flips = flips_of(half)
        order = (0, flips[0], flips[1], flips[0] ^ flips[1])
        spot = order.index(quarter)
        call = (spot >> 1) * 2 + half
        tile = call * 2 + (inner >> 2)
        return tile * n_exp * capacity + (inner & 3) * 4 * capacity + (spot & 1) * 2 * capacity

    messages = merge(
        shifts, [fourth_parts(keeps[k], firsts[k], seconds[k], thirds[k]) for k in streams]
    )
    fourths = [swap(messages[k], "exp", orders[k][3]) for k in streams]
    arrays, places = [], []
    for k in streams:
        got = [keeps[k], firsts[k], seconds[k], thirds[k], fourths[k]]
        for mask, (array, unit) in sorted(grad_places(orders[k]).items()):
            places.append((len(arrays) + array, unit, row_of(mask, k), 2 * capacity))
        arrays += got
    expert_grads = expert_backward(arrays, tuple(places), gate, up, own_weights, rows_all, act)
    return (qkv_in_grad, expert_grads[None])


def solution(mesh):
    return jax.shard_map(
        per_device,
        mesh=mesh,
        in_specs=(
            P("exp", "seq"),
            P("exp", "seq"),
            P(None, "seq"),
            P(),
            P("seq", None),
            P(("exp", "seq"), None),
            P(),
            P(("exp", "seq"), None),
            P(("exp", "seq"), None),
            P(("exp", "seq"), None),
            P(("seq", "exp"), None, None),
        ),
        out_specs=(P(("exp", "seq"), None), P(("seq", "exp"), None, None)),
        check_vma=False,
    )
```

```python
import functools

import jax
import jax.numpy as jnp
from jax import lax
from jax.experimental import pallas as pl
from jax.experimental.pallas import tpu as pltpu
from jax.sharding import PartitionSpec as P

BF16 = jnp.bfloat16
F32 = jnp.float32
HALO = 16
MIB = 1024 * 1024
VMEM_LIMIT = 127 * MIB // 2
EXTRA = 128


def call_cost(flops, nbytes):
    return pl.CostEstimate(flops=int(flops), bytes_accessed=int(nbytes), transcendentals=0)


def norm_kernel(resid_ref, gain_ref, routes_ref, out_ref):
    rows = resid_ref[...].astype(F32)
    dim = rows.shape[1]
    scale = lax.rsqrt(jnp.mean(rows * rows, axis=1, keepdims=True) + 1e-06)
    out_ref[:, :dim] = (rows * scale * gain_ref[...]).astype(BF16)
    out_ref[:, dim:] = jnp.zeros((rows.shape[0], EXTRA), BF16)
    names = routes_ref[...].astype(F32)
    pad = jnp.zeros((HALO - names.shape[0], EXTRA), F32)
    out_ref[:HALO, dim:] = jnp.concatenate([names, pad]).astype(BF16)


def norm_rows(resid, gain, names):
    tokens, dim = resid.shape
    return pl.pallas_call(
        norm_kernel,
        out_shape=jax.ShapeDtypeStruct((tokens, dim + EXTRA), BF16),
        compiler_params=pltpu.CompilerParams(vmem_limit_bytes=VMEM_LIMIT),
        cost_estimate=call_cost(resid.size * 6, resid.size * 4),
        name="norm_rows",
    )(resid, gain.reshape(1, -1), names)


def conv_kernel(
    tile,
    place_ref,
    in_ref,
    in_low_ref,
    in_high_ref,
    grad_ref,
    grad_high_ref,
    ids_ref,
    taps_ref,
    local_ref,
    keep_ref,
    send_ref,
    in_ext,
    grad_ext,
):
    step = pl.program_id(0)
    rows = in_ref.shape[0]

    @pl.when(step == 0)
    def _():
        in_ext[:HALO] = in_low_ref[...].astype(F32)
        in_ext[HALO : HALO + rows] = in_ref[...].astype(F32)
        in_ext[HALO + rows :] = in_high_ref[...].astype(F32)
        grad_ext[:rows] = grad_ref[...].astype(F32)
        grad_ext[rows:] = grad_high_ref[...].astype(F32)

    first = pl.multiple_of(step * tile, tile)
    span = tile + 8
    taps = taps_ref[...]
    window = in_ext[pl.ds(first + HALO - 8, span + 8)]
    ids = ids_ref[pl.ds(first + HALO - 8, span + 8)]
    here = ids[8:]
    same = [None] + [(ids[8 - j : 8 - j + span] == here).astype(F32) for j in (1, 2, 3)]
    conv = taps[0:1] * window[8:]
    for j in (1, 2, 3):
        conv = conv + taps[j : j + 1] * window[8 - j : 8 - j + span] * same[j]
    gate = jax.nn.sigmoid(conv)
    pre = grad_ext[pl.ds(first, span)] * gate * (1.0 + conv * (1.0 - gate))
    result = taps[0:1] * pre[:tile]
    for j in (1, 2, 3):
        result = result + taps[j : j + 1] * (pre * same[j])[j : j + tile]
    local = result.astype(BF16)
    local_ref[...] = local
    half = tile // 2
    core = place_ref[0] & 1

    @pl.when(core == 0)
    def _():
        keep_ref[...] = local[:half]
        send_ref[...] = local[half:]

    @pl.when(core == 1)
    def _():
        keep_ref[...] = local[half:]
        send_ref[...] = local[:half]


def conv_back(place, qkv_in, low, high, qkv_grad, grad_high, ids, taps, block):
    rows, width = qkv_in.shape
    tile = 2 * block
    whole = lambda shape: pl.BlockSpec(shape, lambda i, p: (0,) * len(shape))
    part = lambda size: pl.BlockSpec((size, width), lambda i, p: (i, 0))
    return pl.pallas_call(
        functools.partial(conv_kernel, tile),
        grid_spec=pltpu.PrefetchScalarGridSpec(
            num_scalar_prefetch=1,
            grid=(rows // tile,),
            in_specs=[
                whole(qkv_in.shape),
                whole(low.shape),
                whole(high.shape),
                whole(qkv_grad.shape),
                whole(grad_high.shape),
                whole(ids.shape),
                whole(taps.shape),
            ],
            out_specs=[part(tile), part(block), part(block)],
            scratch_shapes=[
                pltpu.VMEM((rows + 2 * HALO, width), F32),
                pltpu.VMEM((rows + HALO, width), F32),
            ],
        ),
        out_shape=[
            jax.ShapeDtypeStruct((rows, width), BF16),
            jax.ShapeDtypeStruct((rows // 2, width), BF16),
            jax.ShapeDtypeStruct((rows // 2, width), BF16),
        ],
        compiler_params=pltpu.CompilerParams(vmem_limit_bytes=VMEM_LIMIT),
        cost_estimate=call_cost(40 * rows * width, 8 * rows * width),
        name="conv_back",
    )(place, qkv_in, low, high, qkv_grad, grad_high, ids, taps)


def project_kernel(place_ref, own_ref, other_ref, own_weight, other_weight, flow_ref, out_ref):
    block = flow_ref.shape[0]
    total = jnp.dot(own_ref[...], own_weight[...], preferred_element_type=F32)
    total = total + jnp.dot(other_ref[...], other_weight[...], preferred_element_type=F32)
    out_ref[...] = total.astype(BF16)
    for index in range(out_ref.shape[0] // block):

        @pl.when(index == place_ref[0] >> 1)
        def _():
            own = slice(index * block, (index + 1) * block)
            out_ref[own] = (total[own] + flow_ref[...].astype(F32)).astype(BF16)


def project(place, own, other, own_weight, other_weight, out_grad):
    rows, width = own.shape
    dim = own_weight.shape[1]
    tile = dim // 3
    whole = pl.BlockSpec((rows, width), lambda i, p: (0, 0))
    columns = lambda size: pl.BlockSpec((size, tile), lambda i, p: (0, i))
    return pl.pallas_call(
        project_kernel,
        grid_spec=pltpu.PrefetchScalarGridSpec(
            num_scalar_prefetch=1,
            grid=(dim // tile,),
            in_specs=[whole, whole, columns(width), columns(width), columns(out_grad.shape[0])],
            out_specs=columns(rows),
        ),
        out_shape=jax.ShapeDtypeStruct((rows, dim), BF16),
        compiler_params=pltpu.CompilerParams(vmem_limit_bytes=VMEM_LIMIT),
        cost_estimate=call_cost(4 * rows * width * dim, 4 * (rows + dim) * width + 2 * rows * dim),
        name="project",
    )(place, own, other, own_weight, other_weight, out_grad)


def slot_picker(names, own, capacity):
    count, tokens = own.shape
    match = [(names[k : k + 1] == own) for k in range(names.shape[0])]
    named = functools.reduce(jnp.logical_or, match)
    source = lax.broadcasted_iota(jnp.int32, (tokens, tokens), 0)
    target = lax.broadcasted_iota(jnp.int32, (tokens, tokens), 1)
    earlier = (source < target).astype(BF16)
    rank = jnp.dot(named.astype(BF16), earlier, preferred_element_type=F32).astype(jnp.int32)
    rank = jnp.where(named, rank, -1)
    slot = lax.broadcasted_iota(jnp.int32, (count, capacity, tokens), 1)
    picker = (rank[:, None, :] == slot).astype(F32)
    return picker, match


def pick_norm_kernel(per_token, capacity, n_exp, turns, place_ref, *refs):
    halves = len(turns)
    out_refs = refs[halves:]
    outs = len(out_refs) // halves
    for half in range(halves):
        rows_ref = refs[half]
        tokens = rows_ref.shape[1]
        dim = out_refs[0].shape[3]
        count = len(turns[half])
        names = rows_ref[0, :HALO, dim:].astype(F32)[:per_token].astype(jnp.int32)
        own = jnp.concatenate(
            [
                jnp.full((1, tokens), (place_ref[0] ^ t) * n_exp + place_ref[1], jnp.int32)
                for t in turns[half]
            ]
        )
        picker, _ = slot_picker(names, own, capacity)
        picker = picker.reshape(count * capacity, tokens).astype(BF16)
        picked = jnp.dot(picker, rows_ref[0, :, :dim], preferred_element_type=F32).astype(BF16)
        for index in range(count):
            out_refs[half * outs + index // 2][index % 2, 0] = picked[
                index * capacity : (index + 1) * capacity
            ]


def pick_norm(place, rows, turns, dim, per_token, capacity):
    blocks, tokens, width = rows.shape
    halves = len(turns)
    count = blocks // halves
    outs = len(turns[0]) // 2 * halves
    row_spec = lambda first: pl.BlockSpec(
        (1, tokens, width), lambda i, p: (p[1] ^ (i + first), 0, 0)
    )
    return pl.pallas_call(
        functools.partial(pick_norm_kernel, per_token, capacity, blocks, turns),
        grid_spec=pltpu.PrefetchScalarGridSpec(
            num_scalar_prefetch=1,
            grid=(count,),
            in_specs=[row_spec(half * count) for half in range(halves)],
            out_specs=[pl.BlockSpec((2, 1, capacity, dim), lambda i, p: (0, i, 0, 0))] * outs,
        ),
        out_shape=[jax.ShapeDtypeStruct((2, count, capacity, dim), BF16)] * outs,
        compiler_params=pltpu.CompilerParams(vmem_limit_bytes=VMEM_LIMIT),
        cost_estimate=call_cost(
            2 * len(turns[0]) * capacity * blocks * tokens * dim,
            2 * dim * blocks * (tokens + len(turns[0]) * capacity),
        ),
        name="pick_norm",
    )(place, *[rows] * halves)


def pick_grad_kernel(per_token, capacity, n_exp, turns, cores, place_ref, tables_ref, *refs):
    flow_refs, out_refs = refs[: len(cores)], refs[-2 - len(turns) : -2]
    buffer, sems = refs[-2:]
    tokens = tables_ref.shape[2]
    copies = []
    for quarter, turn in enumerate(turns):
        count = len(turn)
        own = jnp.concatenate(
            [
                jnp.full((1, tokens), place_ref[0] * n_exp + (place_ref[1] ^ t), jnp.int32)
                for t in turn
            ]
        )
        first = pl.multiple_of(((place_ref[0] >> 1) ^ quarter) * tokens, tokens)
        for spot, core in enumerate(cores):
            table = tables_ref[place_ref[0] ^ (2 * quarter + core)]
            names = table[:per_token].astype(jnp.int32)
            picker, match = slot_picker(names, own, capacity)
            weights = table[per_token:]
            scale = functools.reduce(
                jnp.add, [jnp.where(match[k], weights[k : k + 1], 0.0) for k in range(per_token)]
            )
            scales = jnp.sum(picker * scale[:, None, :], axis=2, keepdims=True)
            picker = picker.reshape(count * capacity, tokens).astype(BF16)
            picked = jnp.dot(
                picker, flow_refs[spot][pl.ds(first, tokens)], preferred_element_type=F32
            )
            picked = (picked * scales.reshape(count * capacity, 1)).astype(BF16)
            buffer[quarter, spot] = picked.reshape(count, capacity, -1)
            at = quarter * len(cores) + spot
            copy = pltpu.make_async_copy(
                buffer.at[quarter, spot],
                out_refs[quarter].at[:, pl.ds(core * capacity, capacity)],
                sems.at[at],
            )
            copy.start()
            copies.append(copy)
    for copy in copies:
        copy.wait()


def pick_grad(place, tables, flows, cores, turns, n_exp, per_token, capacity, before=()):
    dim = flows[0].shape[1]
    rows, count = 2 * capacity, len(turns[0])
    whole = lambda array: pl.BlockSpec(array.shape, lambda i, p: (0,) * array.ndim)
    any_spec = pl.BlockSpec(memory_space=pl.ANY)
    outs = len(turns)
    return pl.pallas_call(
        functools.partial(pick_grad_kernel, per_token, capacity, n_exp, turns, cores),
        grid_spec=pltpu.PrefetchScalarGridSpec(
            num_scalar_prefetch=1,
            grid=(1,),
            in_specs=[whole(tables)] + [whole(flow) for flow in flows] + [any_spec] * len(before),
            out_specs=[any_spec] * outs,
            scratch_shapes=[
                pltpu.VMEM((outs, len(cores), count, capacity, dim), BF16),
                pltpu.SemaphoreType.DMA((outs * len(cores),)),
            ],
        ),
        out_shape=[jax.ShapeDtypeStruct((count, rows, dim), BF16)] * outs,
        input_output_aliases={2 + len(flows) + i: i for i in range(len(before))},
        compiler_params=pltpu.CompilerParams(vmem_limit_bytes=VMEM_LIMIT),
        cost_estimate=call_cost(
            2 * outs * count * capacity * len(cores) * tables.shape[2] * dim,
            2 * dim * len(cores) * (flows[0].shape[0] + outs * count * capacity),
        ),
        name="pick_grad",
    )(place, tables, *flows, *before)


def forward_kernel(sources, *refs):
    row_refs = refs[1 : 1 + sources]
    weight_ref = refs[1 + sources]
    rows_out, act_ref, gate_ref, up_ref, rows = refs[-5:]
    _, group, capacity, _ = row_refs[0].shape
    for inner in range(group):
        for index in range(sources):
            at = (inner * sources + index) * capacity
            rows[at : at + capacity] = row_refs[index][0, inner]
    hidden = act_ref.shape[0]
    mixed = jnp.dot(rows[...], weight_ref[...], preferred_element_type=F32)
    rows_out[...] = rows[...].T
    gate = mixed[:, :hidden]
    up = mixed[:, hidden:]
    sig = jax.nn.sigmoid(gate)
    silu = gate * sig
    act_ref[...] = (silu * up).astype(BF16).T
    gate_ref[...] = (up * sig * (1.0 + gate * (1.0 - sig))).astype(BF16)
    up_ref[...] = silu.astype(BF16)


def expert_forward(pieces, weight, hidden, shifts, parts, part, before):
    sources = len(pieces)
    _, blocks, capacity, dim = pieces[0][0].shape
    group = 16 // sources
    tile = sources * group * capacity
    steps = blocks // group
    total = tile * steps * parts
    at = lambda i: i + part * steps
    row_spec = lambda width: pl.BlockSpec((tile, width), lambda i, p: (at(i), 0))
    column_spec = lambda height: pl.BlockSpec((height, tile), lambda i, p: (0, at(i)))

    def piece_spec(unit, shift):
        return pl.BlockSpec(
            (1, group, capacity, dim),
            lambda i, p: (unit if shift is None else unit + p[shift], i, 0, 0),
        )

    return pl.pallas_call(
        functools.partial(forward_kernel, sources),
        grid_spec=pltpu.PrefetchScalarGridSpec(
            num_scalar_prefetch=1,
            grid=(steps,),
            in_specs=[piece_spec(unit, shift) for _, unit, shift in pieces]
            + [pl.BlockSpec((dim, 2 * hidden), lambda i, p: (0, 0))]
            + [pl.BlockSpec(memory_space=pl.ANY)] * len(before),
            out_specs=[column_spec(dim), column_spec(hidden), row_spec(hidden), row_spec(hidden)],
            scratch_shapes=[pltpu.VMEM((tile, dim), BF16)],
        ),
        out_shape=[
            jax.ShapeDtypeStruct((dim, total), BF16),
            jax.ShapeDtypeStruct((hidden, total), BF16),
            jax.ShapeDtypeStruct((total, hidden), BF16),
            jax.ShapeDtypeStruct((total, hidden), BF16),
        ],
        input_output_aliases={sources + 2 + i: i for i in range(len(before))},
        compiler_params=pltpu.CompilerParams(vmem_limit_bytes=VMEM_LIMIT),
        cost_estimate=call_cost(
            4 * total * dim * hidden // parts, (4 * total * dim + 10 * total * hidden) // parts
        ),
        name="expert_forward",
    )(shifts, *[array for array, _, _ in pieces], weight, *before)


def backward_kernel(places, arrays, *refs):
    grad_refs = refs[:arrays]
    gate_ref, up_ref, weight_ref, rows_ref, act_ref, out_ref = refs[arrays : arrays + 6]
    grads_all, hidden_all, sems = refs[arrays + 6 :]
    step = pl.program_id(0)
    tile = gate_ref.shape[0]
    hidden = act_ref.shape[0]
    width = rows_ref.shape[0]
    row_steps = grads_all.shape[0] // tile
    copies = []
    for index, (array, unit, row, size) in enumerate(places):
        copy = pltpu.make_async_copy(
            grad_refs[array].at[unit], grads_all.at[pl.ds(row, size)], sems.at[index]
        )
        copies.append((row // tile, copy))

    @pl.when(step == 0)
    def _():
        for turn in range(row_steps):
            for at, copy in copies:
                if at == turn:
                    copy.start()

    for turn in range(row_steps):

        @pl.when(step == turn)
        def _():
            for at, copy in copies:
                if at == turn:
                    copy.wait()

    @pl.when(step < row_steps)
    def _():
        where = pl.ds(pl.multiple_of(step * tile, tile), tile)
        act_grad = jnp.dot(grads_all[where], weight_ref[...], preferred_element_type=F32)
        hidden_all[where, :hidden] = (act_grad * gate_ref[...].astype(F32)).astype(BF16)
        hidden_all[where, hidden:] = (act_grad * up_ref[...].astype(F32)).astype(BF16)

    @pl.when(step >= row_steps)
    def _():
        columns = pl.ds(pl.multiple_of((step - row_steps) * width, width), width)
        out_ref[:, : 2 * hidden] = jnp.dot(
            rows_ref[...], hidden_all[...], preferred_element_type=F32
        ).astype(BF16)
        down = jnp.dot(act_ref[...], grads_all[:, columns], preferred_element_type=F32)
        out_ref[:, 2 * hidden :] = down.T.astype(BF16)


def expert_backward(arrays, places, gate, up, weights, rows, act):
    dim, total = rows.shape
    hidden = act.shape[0]
    tile, width = 512, 768
    row_steps, column_steps = total // tile, dim // width
    row_spec = lambda cols: pl.BlockSpec(
        (tile, cols), lambda i: (jnp.minimum(i, row_steps - 1), 0)
    )
    column_of = lambda i: jnp.maximum(i - row_steps, 0)
    return pl.pallas_call(
        functools.partial(backward_kernel, places, len(arrays)),
        grid=(row_steps + column_steps,),
        in_specs=[pl.BlockSpec(memory_space=pl.ANY)] * len(arrays)
        + [
            row_spec(hidden),
            row_spec(hidden),
            pl.BlockSpec((dim, hidden), lambda i: (0, 2)),
            pl.BlockSpec((width, total), lambda i: (column_of(i), 0)),
            pl.BlockSpec((hidden, total), lambda i: (0, 0)),
        ],
        out_specs=pl.BlockSpec((width, 3 * hidden), lambda i: (column_of(i), 0)),
        out_shape=jax.ShapeDtypeStruct((dim, 3 * hidden), BF16),
        scratch_shapes=[
            pltpu.VMEM((total, dim), BF16),
            pltpu.VMEM((total, 2 * hidden), BF16),
            pltpu.SemaphoreType.DMA((len(places),)),
        ],
        compiler_params=pltpu.CompilerParams(vmem_limit_bytes=VMEM_LIMIT),
        cost_estimate=call_cost(8 * total * dim * hidden, 4 * total * dim + 20 * total * hidden),
        name="expert_backward",
    )(*arrays, gate, up, weights, rows, act)


def merge_kernel(plans, arrays, shift_ref, *refs):
    sources, refs = refs[:arrays], refs[arrays + refs_after(refs, arrays, plans) :]
    outs, buffers = refs[: len(plans)], refs[len(plans) : 2 * len(plans)]
    in_sems, out_sems = refs[2 * len(plans) :]
    reads, count = [], 0
    for plan, buffer in zip(plans, buffers):
        copies = []
        for at, (array, unit, shift) in enumerate(plan):
            first = unit if shift is None else unit + shift_ref[shift]
            half = buffer.shape[1] // 2
            for piece in range(2):
                rows = pl.ds(piece * half, half)
                copies.append(
                    pltpu.make_async_copy(
                        sources[array].at[first, rows], buffer.at[at, rows], in_sems.at[count]
                    )
                )
                count += 1
        reads.append(copies)
    for copies in reads:
        for copy in copies:
            copy.start()
    writes = []
    for index, copies in enumerate(reads):
        for copy in copies:
            copy.wait()
        writes.append(pltpu.make_async_copy(buffers[index], outs[index], out_sems.at[index]))
        writes[-1].start()
    for copy in writes:
        copy.wait()


def refs_after(refs, arrays, plans):
    return len(refs) - arrays - 2 * len(plans) - 2


def merge(shifts, messages, after=()):
    arrays, plans = [], []
    for parts in messages:
        plan = []
        for array, units, shift in parts:
            known = [i for i, other in enumerate(arrays) if other is array]
            if not known:
                arrays.append(array)
                known = [len(arrays) - 1]
            plan += [(known[0], unit, shift) for unit in units]
        plans.append(tuple(plan))
    shapes = [(len(plan),) + arrays[plan[0][0]].shape[1:] for plan in plans]
    size = sum(functools.reduce(lambda a, b: a * b, shape, 1) for shape in shapes)
    any_spec = pl.BlockSpec(memory_space=pl.ANY)
    return pl.pallas_call(
        functools.partial(merge_kernel, tuple(plans), len(arrays)),
        grid_spec=pltpu.PrefetchScalarGridSpec(
            num_scalar_prefetch=1,
            grid=(1,),
            in_specs=[any_spec] * (len(arrays) + len(after)),
            out_specs=[any_spec] * len(plans),
            scratch_shapes=[pltpu.VMEM(shape, BF16) for shape in shapes]
            + [
                pltpu.SemaphoreType.DMA((2 * sum(len(plan) for plan in plans),)),
                pltpu.SemaphoreType.DMA((len(plans),)),
            ],
        ),
        out_shape=[jax.ShapeDtypeStruct(shape, BF16) for shape in shapes],
        compiler_params=pltpu.CompilerParams(vmem_limit_bytes=VMEM_LIMIT),
        cost_estimate=call_cost(0, 4 * size),
        name="merge_rows",
    )(shifts, *arrays, *after)


def swap(array, axis, flip):
    count = lax.axis_size(axis)
    return lax.ppermute(array, axis, [(i, i ^ flip) for i in range(count)])


def mask_of(flips, bits):
    return functools.reduce(lambda a, b: a ^ b, [f for f, bit in zip(flips, bits) if bit], 0)


def flips_of(half):
    return (1, 3) if half == 0 else (3, 1)


def swap_gather(array, axis, flip):
    count = lax.axis_size(axis)
    groups = [[i, i ^ flip] for i in range(count) if i < i ^ flip]
    both = lax.all_gather(array, axis, axis_index_groups=groups)
    return both.reshape((-1,) + array.shape[1:])


def second_parts(keep, first):
    return [(keep, range(4, 8), None), (first, range(4, 8), None)]


def third_parts(keep, first, second):
    return [
        (keep, (2, 3), None),
        (first, (2, 3), None),
        (second, (2, 3, 6, 7), None),
    ]


def fourth_parts(keep, first, second, third):
    return [
        (keep, (1,), None),
        (first, (1,), None),
        (second, (1, 5), None),
        (third, (1, 3, 5, 7), None),
    ]


def grad_places(flips):
    found = {}
    found[0, 0, 0, 0] = (0, 0)
    found[1, 0, 0, 0] = (1, 0)
    found[0, 1, 0, 0] = (2, 0)
    found[1, 1, 0, 0] = (2, 4)
    for index, start in enumerate([(0, 0), (1, 0), (0, 1), (1, 1)]):
        found[start + (1, 0)] = (3, 2 * index)
        found[start + (0, 1)] = (4, index)
        found[start + (1, 1)] = (4, 4 + index)
    return {mask_of(flips, bits): at for bits, at in found.items()}


def per_device(
    qkv_in,
    qkv_grad,
    conv_weight,
    doc_ids,
    qkv_weight,
    resid,
    norm_gain,
    out_grad,
    routes,
    route_weights,
    expert_weights,
):
    rows, width = qkv_in.shape
    tokens, dim = resid.shape
    per_token = routes.shape[1]
    hidden = expert_weights.shape[2] // 3
    n_seq, n_exp = lax.axis_size("seq"), lax.axis_size("exp")
    experts = n_seq * n_exp
    capacity = 2 * tokens * per_token // experts
    seq_index, exp_index = lax.axis_index("seq"), lax.axis_index("exp")
    own_weights = expert_weights[0]

    place = jnp.stack([seq_index, exp_index]).astype(jnp.int32)
    forward = [(i, i + 1) for i in range(n_exp - 1)]
    backward = [(i + 1, i) for i in range(n_exp - 1)]
    low = lax.ppermute(qkv_in[-HALO:], "exp", forward)
    high = lax.ppermute(qkv_in[:HALO], "exp", backward)
    grad_high = lax.ppermute(qkv_grad[:HALO], "exp", backward)
    weight_far = swap(qkv_weight, "seq", 1)

    table = jnp.concatenate([routes.astype(F32), route_weights], 1).T
    normed = norm_rows(resid, norm_gain, routes.T)
    normed, conv_weight = lax.optimization_barrier((normed, conv_weight))
    exp_normed = lax.all_gather(normed, "exp")

    edge = jnp.full((HALO,), -1, jnp.int32)
    ids = lax.dynamic_slice_in_dim(
        jnp.concatenate([edge, doc_ids, edge]), exp_index * rows, rows + 2 * HALO
    )
    local_grad, local_keep, local_send = conv_back(
        place, qkv_in, low, high, qkv_grad, grad_high, ids.reshape(-1, 1), conv_weight, tokens
    )
    local_got = swap(local_send, "seq", 1)
    partial = project(place, local_keep, local_got, qkv_weight, weight_far, out_grad)
    table, partial = lax.optimization_barrier((table, partial))
    tables = jnp.broadcast_to(table[None], (n_seq,) + table.shape)
    tables = lax.all_to_all(tables, "seq", split_axis=0, concat_axis=0, tiled=True)
    same_core = [[s for s in range(n_seq) if s % 2 == core] for core in range(2)]
    flow = lax.psum(partial, "seq", axis_index_groups=same_core)

    exp_normed, tables = lax.optimization_barrier((exp_normed, tables))
    flips_a, flips_b = flips_of(0), flips_of(1)
    shifts = [
        (seq_index < seq_index ^ 2 * f).astype(jnp.int32) * 4 for f in flips_b
    ]
    shifts = jnp.stack(shifts)
    turns = []
    for near in (flips_a, flips_b):
        near = (0, near[1], near[0], near[0] ^ near[1])
        turns.append(tuple(2 * m for m in near) + tuple(2 * m + 1 for m in near))
    picks = pick_norm(place, exp_normed, tuple(turns), dim, per_token, capacity)
    (keep_a, send_a, keep_far_a, send_far_a) = picks[:4]
    (keep_b, send_b, keep_far_b, send_far_b) = picks[4:]
    got_a, got_b = swap(send_far_a, "seq", 1), swap(send_far_b, "seq", 1)
    message_a, message_b = merge(
        shifts,
        [
            [(send_a, (0, 1), None), (got_a, (0, 1), None)],
            [(send_b, (0, 1), None), (got_b, (0, 1), None)],
        ],
    )
    first_a = swap(message_a, "seq", 2 * flips_a[0])
    far_a, far_b = swap(keep_far_a, "seq", 1), swap(keep_far_b, "seq", 1)
    flow, far_a, far_b, message_b, local_grad = lax.optimization_barrier(
        (flow, far_a, far_b, message_b, local_grad)
    )
    qkv_parts = local_grad.reshape(n_seq, tokens, width)
    qkv_parts = lax.all_to_all(qkv_parts, "seq", split_axis=0, concat_axis=0, tiled=True)
    qkv_in_grad = qkv_parts.swapaxes(0, 1).reshape(tokens, n_seq * width)
    first_b = swap_gather(message_b, "seq", 2 * flips_b[0])
    flow_far = swap(flow, "seq", 1)

    flips = (1, 3, 4, 12)
    quarters = len(flips)
    orders = [flips[k:] + flips[:k] for k in range(quarters)]
    bit_rows = [tuple((j >> (3 - b)) & 1 for b in range(4)) for j in range(n_exp)]
    turns = [[mask_of(order, bits) for bits in bit_rows] for order in orders]
    half = n_exp // 2
    late = [t[half:] for t in turns]
    sends = pick_grad(place, tables, [flow], (0,), late, n_exp, per_token, capacity)
    sends = pick_grad(place, tables, [flow_far], (1,), late, n_exp, per_token, capacity, sends)
    early = [t[:half] for t in turns]
    keeps = pick_grad(
        place, tables, [flow, flow_far], (0, 1), early, n_exp, per_token, capacity
    )
    streams = range(quarters)
    firsts = [swap(sends[k], "exp", orders[k][0]) for k in streams]
    messages = merge(shifts, [second_parts(keeps[k], firsts[k]) for k in streams], [first_a])
    seconds = [swap(messages[k], "exp", orders[k][1]) for k in streams]
    messages = merge(
        shifts,
        [third_parts(keeps[k], firsts[k], seconds[k]) for k in streams]
        + [
            [(keep_a, (1,), None), (far_a, (1,), None), (first_a, (1, 3), None)],
            [(keep_b, (1,), None), (far_b, (1,), None), (first_b, (1, 3), 0)],
        ],
        [qkv_parts],
    )
    thirds_out, (message_a, message_b) = messages[:quarters], messages[quarters:]
    thirds = [swap(thirds_out[k], "exp", orders[k][2]) for k in streams]
    second_a = swap(message_a, "seq", 2 * flips_a[1])
    second_b = swap_gather(message_b, "seq", 2 * flips_b[1])
    calls = [
        [(keep_a, 0, None), (far_a, 0, None), (first_a, 0, None), (first_a, 2, None)],
        [(keep_b, 0, None), (far_b, 0, None), (first_b, 0, 0), (first_b, 2, 0)],
        [(second_a, i, None) for i in range(4)],
        [(second_b, i, 1) for i in range(4)],
    ]
    results = ()
    for part, pieces in enumerate(calls):
        results = expert_forward(
            pieces, own_weights, hidden, shifts, len(calls), part, results
        )
        if part == 1:
            results, thirds = lax.optimization_barrier((results, thirds))
    rows_all, act, gate, up = results

    def row_of(mask, quarter):
        half, inner = mask >> 3, mask & 7
        flips = flips_of(half)
        order = (0, flips[0], flips[1], flips[0] ^ flips[1])
        spot = order.index(quarter)
        call = (spot >> 1) * 2 + half
        tile = call * 2 + (inner >> 2)
        return tile * n_exp * capacity + (inner & 3) * 4 * capacity + (spot & 1) * 2 * capacity

    messages = merge(
        shifts, [fourth_parts(keeps[k], firsts[k], seconds[k], thirds[k]) for k in streams]
    )
    fourths = [swap(messages[k], "exp", orders[k][3]) for k in streams]
    arrays, places = [], []
    for k in streams:
        got = [keeps[k], firsts[k], seconds[k], thirds[k], fourths[k]]
        for mask, (array, unit) in sorted(grad_places(orders[k]).items()):
            places.append((len(arrays) + array, unit, row_of(mask, k), 2 * capacity))
        arrays += got
    expert_grads = expert_backward(arrays, tuple(places), gate, up, own_weights, rows_all, act)
    return (qkv_in_grad, expert_grads[None])


def solution(mesh):
    return jax.shard_map(
        per_device,
        mesh=mesh,
        in_specs=(
            P("exp", "seq"),
            P("exp", "seq"),
            P(None, "seq"),
            P(),
            P("seq", None),
            P(("exp", "seq"), None),
            P(),
            P(("exp", "seq"), None),
            P(("exp", "seq"), None),
            P(("exp", "seq"), None),
            P(("seq", "exp"), None, None),
        ),
        out_specs=(P(("exp", "seq"), None), P(("seq", "exp"), None, None)),
        check_vma=False,
    )
```

```python
import functools

import jax
import jax.numpy as jnp
from jax import lax
from jax.experimental import pallas as pl
from jax.experimental.pallas import tpu as pltpu
from jax.sharding import PartitionSpec as P

BF16 = jnp.bfloat16
F32 = jnp.float32
HALO = 16
MIB = 1024 * 1024
VMEM_LIMIT = 127 * MIB // 2
EXTRA = 128


def call_cost(flops, nbytes):
    return pl.CostEstimate(flops=int(flops), bytes_accessed=int(nbytes), transcendentals=0)


def norm_kernel(resid_ref, gain_ref, routes_ref, out_ref):
    rows = resid_ref[...].astype(F32)
    dim = rows.shape[1]
    scale = lax.rsqrt(jnp.mean(rows * rows, axis=1, keepdims=True) + 1e-06)
    out_ref[:, :dim] = (rows * scale * gain_ref[...]).astype(BF16)
    out_ref[:, dim:] = jnp.zeros((rows.shape[0], EXTRA), BF16)
    names = routes_ref[...].astype(F32)
    pad = jnp.zeros((HALO - names.shape[0], EXTRA), F32)
    out_ref[:HALO, dim:] = jnp.concatenate([names, pad]).astype(BF16)


def norm_rows(resid, gain, names):
    tokens, dim = resid.shape
    return pl.pallas_call(
        norm_kernel,
        out_shape=jax.ShapeDtypeStruct((tokens, dim + EXTRA), BF16),
        compiler_params=pltpu.CompilerParams(vmem_limit_bytes=VMEM_LIMIT),
        cost_estimate=call_cost(resid.size * 6, resid.size * 4),
        name="norm_rows",
    )(resid, gain.reshape(1, -1), names)


def conv_kernel(
    tile,
    place_ref,
    in_ref,
    in_low_ref,
    in_high_ref,
    grad_ref,
    grad_high_ref,
    ids_ref,
    taps_ref,
    local_ref,
    keep_ref,
    send_ref,
    in_ext,
    grad_ext,
):
    step = pl.program_id(0)
    rows = in_ref.shape[0]

    @pl.when(step == 0)
    def _():
        in_ext[:HALO] = in_low_ref[...].astype(F32)
        in_ext[HALO : HALO + rows] = in_ref[...].astype(F32)
        in_ext[HALO + rows :] = in_high_ref[...].astype(F32)
        grad_ext[:rows] = grad_ref[...].astype(F32)
        grad_ext[rows:] = grad_high_ref[...].astype(F32)

    first = pl.multiple_of(step * tile, tile)
    span = tile + 8
    taps = taps_ref[...]
    window = in_ext[pl.ds(first + HALO - 8, span + 8)]
    ids = ids_ref[pl.ds(first + HALO - 8, span + 8)]
    here = ids[8:]
    same = [None] + [(ids[8 - j : 8 - j + span] == here).astype(F32) for j in (1, 2, 3)]
    conv = taps[0:1] * window[8:]
    for j in (1, 2, 3):
        conv = conv + taps[j : j + 1] * window[8 - j : 8 - j + span] * same[j]
    gate = jax.nn.sigmoid(conv)
    pre = grad_ext[pl.ds(first, span)] * gate * (1.0 + conv * (1.0 - gate))
    result = taps[0:1] * pre[:tile]
    for j in (1, 2, 3):
        result = result + taps[j : j + 1] * (pre * same[j])[j : j + tile]
    local = result.astype(BF16)
    local_ref[...] = local
    half = tile // 2
    core = place_ref[0] & 1

    @pl.when(core == 0)
    def _():
        keep_ref[...] = local[:half]
        send_ref[...] = local[half:]

    @pl.when(core == 1)
    def _():
        keep_ref[...] = local[half:]
        send_ref[...] = local[:half]


def conv_back(place, qkv_in, low, high, qkv_grad, grad_high, ids, taps, block):
    rows, width = qkv_in.shape
    tile = 2 * block
    whole = lambda shape: pl.BlockSpec(shape, lambda i, p: (0,) * len(shape))
    part = lambda size: pl.BlockSpec((size, width), lambda i, p: (i, 0))
    return pl.pallas_call(
        functools.partial(conv_kernel, tile),
        grid_spec=pltpu.PrefetchScalarGridSpec(
            num_scalar_prefetch=1,
            grid=(rows // tile,),
            in_specs=[
                whole(qkv_in.shape),
                whole(low.shape),
                whole(high.shape),
                whole(qkv_grad.shape),
                whole(grad_high.shape),
                whole(ids.shape),
                whole(taps.shape),
            ],
            out_specs=[part(tile), part(block), part(block)],
            scratch_shapes=[
                pltpu.VMEM((rows + 2 * HALO, width), F32),
                pltpu.VMEM((rows + HALO, width), F32),
            ],
        ),
        out_shape=[
            jax.ShapeDtypeStruct((rows, width), BF16),
            jax.ShapeDtypeStruct((rows // 2, width), BF16),
            jax.ShapeDtypeStruct((rows // 2, width), BF16),
        ],
        compiler_params=pltpu.CompilerParams(vmem_limit_bytes=VMEM_LIMIT),
        cost_estimate=call_cost(40 * rows * width, 8 * rows * width),
        name="conv_back",
    )(place, qkv_in, low, high, qkv_grad, grad_high, ids, taps)


def project_kernel(place_ref, own_ref, other_ref, own_weight, other_weight, flow_ref, out_ref):
    block = flow_ref.shape[0]
    total = jnp.dot(own_ref[...], own_weight[...], preferred_element_type=F32)
    total = total + jnp.dot(other_ref[...], other_weight[...], preferred_element_type=F32)
    out_ref[...] = total.astype(BF16)
    for index in range(out_ref.shape[0] // block):

        @pl.when(index == place_ref[0] >> 1)
        def _():
            own = slice(index * block, (index + 1) * block)
            out_ref[own] = (total[own] + flow_ref[...].astype(F32)).astype(BF16)


def project(place, own, other, own_weight, other_weight, out_grad):
    rows, width = own.shape
    dim = own_weight.shape[1]
    tile = dim // 3
    whole = pl.BlockSpec((rows, width), lambda i, p: (0, 0))
    columns = lambda size: pl.BlockSpec((size, tile), lambda i, p: (0, i))
    return pl.pallas_call(
        project_kernel,
        grid_spec=pltpu.PrefetchScalarGridSpec(
            num_scalar_prefetch=1,
            grid=(dim // tile,),
            in_specs=[whole, whole, columns(width), columns(width), columns(out_grad.shape[0])],
            out_specs=columns(rows),
        ),
        out_shape=jax.ShapeDtypeStruct((rows, dim), BF16),
        compiler_params=pltpu.CompilerParams(vmem_limit_bytes=VMEM_LIMIT),
        cost_estimate=call_cost(4 * rows * width * dim, 4 * (rows + dim) * width + 2 * rows * dim),
        name="project",
    )(place, own, other, own_weight, other_weight, out_grad)


def slot_picker(names, own, capacity):
    count, tokens = own.shape
    match = [(names[k : k + 1] == own) for k in range(names.shape[0])]
    named = functools.reduce(jnp.logical_or, match)
    source = lax.broadcasted_iota(jnp.int32, (tokens, tokens), 0)
    target = lax.broadcasted_iota(jnp.int32, (tokens, tokens), 1)
    earlier = (source < target).astype(BF16)
    rank = jnp.dot(named.astype(BF16), earlier, preferred_element_type=F32).astype(jnp.int32)
    rank = jnp.where(named, rank, -1)
    slot = lax.broadcasted_iota(jnp.int32, (count, capacity, tokens), 1)
    picker = (rank[:, None, :] == slot).astype(F32)
    return picker, match


def pick_norm_kernel(per_token, capacity, n_exp, turns, place_ref, *refs):
    halves = len(turns)
    out_refs = refs[halves:]
    outs = len(out_refs) // halves
    for half in range(halves):
        rows_ref = refs[half]
        tokens = rows_ref.shape[1]
        dim = out_refs[0].shape[3]
        count = len(turns[half])
        names = rows_ref[0, :HALO, dim:].astype(F32)[:per_token].astype(jnp.int32)
        own = jnp.concatenate(
            [
                jnp.full((1, tokens), (place_ref[0] ^ t) * n_exp + place_ref[1], jnp.int32)
                for t in turns[half]
            ]
        )
        picker, _ = slot_picker(names, own, capacity)
        picker = picker.reshape(count * capacity, tokens).astype(BF16)
        picked = jnp.dot(picker, rows_ref[0, :, :dim], preferred_element_type=F32).astype(BF16)
        for index in range(count):
            out_refs[half * outs + index // 2][index % 2, 0] = picked[
                index * capacity : (index + 1) * capacity
            ]


def pick_norm(place, rows, turns, dim, per_token, capacity):
    blocks, tokens, width = rows.shape
    halves = len(turns)
    count = blocks // halves
    outs = len(turns[0]) // 2 * halves
    row_spec = lambda first: pl.BlockSpec(
        (1, tokens, width), lambda i, p: (p[1] ^ (i + first), 0, 0)
    )
    return pl.pallas_call(
        functools.partial(pick_norm_kernel, per_token, capacity, blocks, turns),
        grid_spec=pltpu.PrefetchScalarGridSpec(
            num_scalar_prefetch=1,
            grid=(count,),
            in_specs=[row_spec(half * count) for half in range(halves)],
            out_specs=[pl.BlockSpec((2, 1, capacity, dim), lambda i, p: (0, i, 0, 0))] * outs,
        ),
        out_shape=[jax.ShapeDtypeStruct((2, count, capacity, dim), BF16)] * outs,
        compiler_params=pltpu.CompilerParams(vmem_limit_bytes=VMEM_LIMIT),
        cost_estimate=call_cost(
            2 * len(turns[0]) * capacity * blocks * tokens * dim,
            2 * dim * blocks * (tokens + len(turns[0]) * capacity),
        ),
        name="pick_norm",
    )(place, *[rows] * halves)


def pick_grad_kernel(per_token, capacity, n_exp, turns, cores, place_ref, tables_ref, *refs):
    flow_refs, out_refs = refs[: len(cores)], refs[-2 - len(turns) : -2]
    buffer, sems = refs[-2:]
    tokens = tables_ref.shape[2]
    copies = []
    for quarter, turn in enumerate(turns):
        count = len(turn)
        own = jnp.concatenate(
            [
                jnp.full((1, tokens), place_ref[0] * n_exp + (place_ref[1] ^ t), jnp.int32)
                for t in turn
            ]
        )
        first = pl.multiple_of(((place_ref[0] >> 1) ^ quarter) * tokens, tokens)
        for spot, core in enumerate(cores):
            table = tables_ref[place_ref[0] ^ (2 * quarter + core)]
            names = table[:per_token].astype(jnp.int32)
            picker, match = slot_picker(names, own, capacity)
            weights = table[per_token:]
            scale = functools.reduce(
                jnp.add, [jnp.where(match[k], weights[k : k + 1], 0.0) for k in range(per_token)]
            )
            scales = jnp.sum(picker * scale[:, None, :], axis=2, keepdims=True)
            picker = picker.reshape(count * capacity, tokens).astype(BF16)
            picked = jnp.dot(
                picker, flow_refs[spot][pl.ds(first, tokens)], preferred_element_type=F32
            )
            picked = (picked * scales.reshape(count * capacity, 1)).astype(BF16)
            buffer[quarter, spot] = picked.reshape(count, capacity, -1)
            at = quarter * len(cores) + spot
            copy = pltpu.make_async_copy(
                buffer.at[quarter, spot],
                out_refs[quarter].at[:, pl.ds(core * capacity, capacity)],
                sems.at[at],
            )
            copy.start()
            copies.append(copy)
    for copy in copies:
        copy.wait()


def pick_grad(place, tables, flows, cores, turns, n_exp, per_token, capacity, before=()):
    dim = flows[0].shape[1]
    rows, count = 2 * capacity, len(turns[0])
    whole = lambda array: pl.BlockSpec(array.shape, lambda i, p: (0,) * array.ndim)
    any_spec = pl.BlockSpec(memory_space=pl.ANY)
    outs = len(turns)
    return pl.pallas_call(
        functools.partial(pick_grad_kernel, per_token, capacity, n_exp, turns, cores),
        grid_spec=pltpu.PrefetchScalarGridSpec(
            num_scalar_prefetch=1,
            grid=(1,),
            in_specs=[whole(tables)] + [whole(flow) for flow in flows] + [any_spec] * len(before),
            out_specs=[any_spec] * outs,
            scratch_shapes=[
                pltpu.VMEM((outs, len(cores), count, capacity, dim), BF16),
                pltpu.SemaphoreType.DMA((outs * len(cores),)),
            ],
        ),
        out_shape=[jax.ShapeDtypeStruct((count, rows, dim), BF16)] * outs,
        input_output_aliases={2 + len(flows) + i: i for i in range(len(before))},
        compiler_params=pltpu.CompilerParams(vmem_limit_bytes=VMEM_LIMIT),
        cost_estimate=call_cost(
            2 * outs * count * capacity * len(cores) * tables.shape[2] * dim,
            2 * dim * len(cores) * (flows[0].shape[0] + outs * count * capacity),
        ),
        name="pick_grad",
    )(place, tables, *flows, *before)


def forward_kernel(sources, *refs):
    row_refs = refs[1 : 1 + sources]
    weight_ref = refs[1 + sources]
    rows_out, act_ref, gate_ref, up_ref, rows = refs[-5:]
    _, group, capacity, _ = row_refs[0].shape
    for inner in range(group):
        for index in range(sources):
            at = (inner * sources + index) * capacity
            rows[at : at + capacity] = row_refs[index][0, inner]
    hidden = act_ref.shape[0]
    mixed = jnp.dot(rows[...], weight_ref[...], preferred_element_type=F32)
    rows_out[...] = rows[...].T
    gate = mixed[:, :hidden]
    up = mixed[:, hidden:]
    sig = jax.nn.sigmoid(gate)
    silu = gate * sig
    act_ref[...] = (silu * up).astype(BF16).T
    gate_ref[...] = (up * sig * (1.0 + gate * (1.0 - sig))).astype(BF16)
    up_ref[...] = silu.astype(BF16)


def expert_forward(pieces, weight, hidden, shifts, parts, part, before):
    sources = len(pieces)
    _, blocks, capacity, dim = pieces[0][0].shape
    group = 16 // sources
    tile = sources * group * capacity
    steps = blocks // group
    total = tile * steps * parts
    at = lambda i: i + part * steps
    row_spec = lambda width: pl.BlockSpec((tile, width), lambda i, p: (at(i), 0))
    column_spec = lambda height: pl.BlockSpec((height, tile), lambda i, p: (0, at(i)))

    def piece_spec(unit, shift):
        return pl.BlockSpec(
            (1, group, capacity, dim),
            lambda i, p: (unit if shift is None else unit + p[shift], i, 0, 0),
        )

    return pl.pallas_call(
        functools.partial(forward_kernel, sources),
        grid_spec=pltpu.PrefetchScalarGridSpec(
            num_scalar_prefetch=1,
            grid=(steps,),
            in_specs=[piece_spec(unit, shift) for _, unit, shift in pieces]
            + [pl.BlockSpec((dim, 2 * hidden), lambda i, p: (0, 0))]
            + [pl.BlockSpec(memory_space=pl.ANY)] * len(before),
            out_specs=[column_spec(dim), column_spec(hidden), row_spec(hidden), row_spec(hidden)],
            scratch_shapes=[pltpu.VMEM((tile, dim), BF16)],
        ),
        out_shape=[
            jax.ShapeDtypeStruct((dim, total), BF16),
            jax.ShapeDtypeStruct((hidden, total), BF16),
            jax.ShapeDtypeStruct((total, hidden), BF16),
            jax.ShapeDtypeStruct((total, hidden), BF16),
        ],
        input_output_aliases={sources + 2 + i: i for i in range(len(before))},
        compiler_params=pltpu.CompilerParams(vmem_limit_bytes=VMEM_LIMIT),
        cost_estimate=call_cost(
            4 * total * dim * hidden // parts, (4 * total * dim + 10 * total * hidden) // parts
        ),
        name="expert_forward",
    )(shifts, *[array for array, _, _ in pieces], weight, *before)


def backward_kernel(places, arrays, *refs):
    grad_refs = refs[:arrays]
    gate_ref, up_ref, weight_ref, rows_ref, act_ref, out_ref = refs[arrays : arrays + 6]
    grads_all, hidden_all, sems = refs[arrays + 6 :]
    step = pl.program_id(0)
    tile = gate_ref.shape[0]
    hidden = act_ref.shape[0]
    width = rows_ref.shape[0]
    row_steps = grads_all.shape[0] // tile
    copies = []
    for index, (array, unit, row, size) in enumerate(places):
        copy = pltpu.make_async_copy(
            grad_refs[array].at[unit], grads_all.at[pl.ds(row, size)], sems.at[index]
        )
        copies.append((row // tile, copy))

    @pl.when(step == 0)
    def _():
        for turn in range(row_steps):
            for at, copy in copies:
                if at == turn:
                    copy.start()

    for turn in range(row_steps):

        @pl.when(step == turn)
        def _():
            for at, copy in copies:
                if at == turn:
                    copy.wait()

    @pl.when(step < row_steps)
    def _():
        where = pl.ds(pl.multiple_of(step * tile, tile), tile)
        act_grad = jnp.dot(grads_all[where], weight_ref[...], preferred_element_type=F32)
        hidden_all[where, :hidden] = (act_grad * gate_ref[...].astype(F32)).astype(BF16)
        hidden_all[where, hidden:] = (act_grad * up_ref[...].astype(F32)).astype(BF16)

    @pl.when(step >= row_steps)
    def _():
        columns = pl.ds(pl.multiple_of((step - row_steps) * width, width), width)
        out_ref[:, : 2 * hidden] = jnp.dot(
            rows_ref[...], hidden_all[...], preferred_element_type=F32
        ).astype(BF16)
        down = jnp.dot(act_ref[...], grads_all[:, columns], preferred_element_type=F32)
        out_ref[:, 2 * hidden :] = down.T.astype(BF16)


def expert_backward(arrays, places, gate, up, weights, rows, act):
    dim, total = rows.shape
    hidden = act.shape[0]
    tile, width = 512, 768
    row_steps, column_steps = total // tile, dim // width
    row_spec = lambda cols: pl.BlockSpec(
        (tile, cols), lambda i: (jnp.minimum(i, row_steps - 1), 0)
    )
    column_of = lambda i: jnp.maximum(i - row_steps, 0)
    return pl.pallas_call(
        functools.partial(backward_kernel, places, len(arrays)),
        grid=(row_steps + column_steps,),
        in_specs=[pl.BlockSpec(memory_space=pl.ANY)] * len(arrays)
        + [
            row_spec(hidden),
            row_spec(hidden),
            pl.BlockSpec((dim, hidden), lambda i: (0, 2)),
            pl.BlockSpec((width, total), lambda i: (column_of(i), 0)),
            pl.BlockSpec((hidden, total), lambda i: (0, 0)),
        ],
        out_specs=pl.BlockSpec((width, 3 * hidden), lambda i: (column_of(i), 0)),
        out_shape=jax.ShapeDtypeStruct((dim, 3 * hidden), BF16),
        scratch_shapes=[
            pltpu.VMEM((total, dim), BF16),
            pltpu.VMEM((total, 2 * hidden), BF16),
            pltpu.SemaphoreType.DMA((len(places),)),
        ],
        compiler_params=pltpu.CompilerParams(vmem_limit_bytes=VMEM_LIMIT),
        cost_estimate=call_cost(8 * total * dim * hidden, 4 * total * dim + 20 * total * hidden),
        name="expert_backward",
    )(*arrays, gate, up, weights, rows, act)


def merge_kernel(plans, arrays, shift_ref, *refs):
    sources, refs = refs[:arrays], refs[arrays + refs_after(refs, arrays, plans) :]
    outs, buffers = refs[: len(plans)], refs[len(plans) : 2 * len(plans)]
    in_sems, out_sems = refs[2 * len(plans) :]
    reads, count = [], 0
    for plan, buffer in zip(plans, buffers):
        copies = []
        for at, (array, unit, shift) in enumerate(plan):
            first = unit if shift is None else unit + shift_ref[shift]
            half = buffer.shape[1] // 2
            for piece in range(2):
                rows = pl.ds(piece * half, half)
                copies.append(
                    pltpu.make_async_copy(
                        sources[array].at[first, rows], buffer.at[at, rows], in_sems.at[count]
                    )
                )
                count += 1
        reads.append(copies)
    for copies in reads:
        for copy in copies:
            copy.start()
    writes = []
    for index, copies in enumerate(reads):
        for copy in copies:
            copy.wait()
        writes.append(pltpu.make_async_copy(buffers[index], outs[index], out_sems.at[index]))
        writes[-1].start()
    for copy in writes:
        copy.wait()


def refs_after(refs, arrays, plans):
    return len(refs) - arrays - 2 * len(plans) - 2


def merge(shifts, messages, after=()):
    arrays, plans = [], []
    for parts in messages:
        plan = []
        for array, units, shift in parts:
            known = [i for i, other in enumerate(arrays) if other is array]
            if not known:
                arrays.append(array)
                known = [len(arrays) - 1]
            plan += [(known[0], unit, shift) for unit in units]
        plans.append(tuple(plan))
    shapes = [(len(plan),) + arrays[plan[0][0]].shape[1:] for plan in plans]
    size = sum(functools.reduce(lambda a, b: a * b, shape, 1) for shape in shapes)
    any_spec = pl.BlockSpec(memory_space=pl.ANY)
    return pl.pallas_call(
        functools.partial(merge_kernel, tuple(plans), len(arrays)),
        grid_spec=pltpu.PrefetchScalarGridSpec(
            num_scalar_prefetch=1,
            grid=(1,),
            in_specs=[any_spec] * (len(arrays) + len(after)),
            out_specs=[any_spec] * len(plans),
            scratch_shapes=[pltpu.VMEM(shape, BF16) for shape in shapes]
            + [
                pltpu.SemaphoreType.DMA((2 * sum(len(plan) for plan in plans),)),
                pltpu.SemaphoreType.DMA((len(plans),)),
            ],
        ),
        out_shape=[jax.ShapeDtypeStruct(shape, BF16) for shape in shapes],
        compiler_params=pltpu.CompilerParams(vmem_limit_bytes=VMEM_LIMIT),
        cost_estimate=call_cost(0, 4 * size),
        name="merge_rows",
    )(shifts, *arrays, *after)


def swap(array, axis, flip):
    count = lax.axis_size(axis)
    return lax.ppermute(array, axis, [(i, i ^ flip) for i in range(count)])


def mask_of(flips, bits):
    return functools.reduce(lambda a, b: a ^ b, [f for f, bit in zip(flips, bits) if bit], 0)


def flips_of(half):
    return (1, 3) if half == 0 else (3, 1)


def swap_gather(array, axis, flip):
    count = lax.axis_size(axis)
    groups = [[i, i ^ flip] for i in range(count) if i < i ^ flip]
    both = lax.all_gather(array, axis, axis_index_groups=groups)
    return both.reshape((-1,) + array.shape[1:])


def second_parts(keep, first):
    return [(keep, range(4, 8), None), (first, range(4, 8), None)]


def third_parts(keep, first, second):
    return [
        (keep, (2, 3), None),
        (first, (2, 3), None),
        (second, (2, 3, 6, 7), None),
    ]


def fourth_parts(keep, first, second, third):
    return [
        (keep, (1,), None),
        (first, (1,), None),
        (second, (1, 5), None),
        (third, (1, 3, 5, 7), None),
    ]


def grad_places(flips):
    found = {}
    found[0, 0, 0, 0] = (0, 0)
    found[1, 0, 0, 0] = (1, 0)
    found[0, 1, 0, 0] = (2, 0)
    found[1, 1, 0, 0] = (2, 4)
    for index, start in enumerate([(0, 0), (1, 0), (0, 1), (1, 1)]):
        found[start + (1, 0)] = (3, 2 * index)
        found[start + (0, 1)] = (4, index)
        found[start + (1, 1)] = (4, 4 + index)
    return {mask_of(flips, bits): at for bits, at in found.items()}


def per_device(
    qkv_in,
    qkv_grad,
    conv_weight,
    doc_ids,
    qkv_weight,
    resid,
    norm_gain,
    out_grad,
    routes,
    route_weights,
    expert_weights,
):
    rows, width = qkv_in.shape
    tokens, dim = resid.shape
    per_token = routes.shape[1]
    hidden = expert_weights.shape[2] // 3
    n_seq, n_exp = lax.axis_size("seq"), lax.axis_size("exp")
    experts = n_seq * n_exp
    capacity = 2 * tokens * per_token // experts
    seq_index, exp_index = lax.axis_index("seq"), lax.axis_index("exp")
    own_weights = expert_weights[0]

    place = jnp.stack([seq_index, exp_index]).astype(jnp.int32)
    forward = [(i, i + 1) for i in range(n_exp - 1)]
    backward = [(i + 1, i) for i in range(n_exp - 1)]
    low = lax.ppermute(qkv_in[-HALO:], "exp", forward)
    high = lax.ppermute(qkv_in[:HALO], "exp", backward)
    grad_high = lax.ppermute(qkv_grad[:HALO], "exp", backward)
    weight_far = swap(qkv_weight, "seq", 1)

    table = jnp.concatenate([routes.astype(F32), route_weights], 1).T
    normed = norm_rows(resid, norm_gain, routes.T)
    normed, conv_weight = lax.optimization_barrier((normed, conv_weight))
    exp_normed = lax.all_gather(normed, "exp")

    edge = jnp.full((HALO,), -1, jnp.int32)
    ids = lax.dynamic_slice_in_dim(
        jnp.concatenate([edge, doc_ids, edge]), exp_index * rows, rows + 2 * HALO
    )
    local_grad, local_keep, local_send = conv_back(
        place, qkv_in, low, high, qkv_grad, grad_high, ids.reshape(-1, 1), conv_weight, tokens
    )
    local_got = swap(local_send, "seq", 1)
    partial = project(place, local_keep, local_got, qkv_weight, weight_far, out_grad)
    table, partial = lax.optimization_barrier((table, partial))
    tables = jnp.broadcast_to(table[None], (n_seq,) + table.shape)
    tables = lax.all_to_all(tables, "seq", split_axis=0, concat_axis=0, tiled=True)
    same_core = [[s for s in range(n_seq) if s % 2 == core] for core in range(2)]
    flow = lax.psum(partial, "seq", axis_index_groups=same_core)

    exp_normed, tables = lax.optimization_barrier((exp_normed, tables))
    flips_a, flips_b = flips_of(0), flips_of(1)
    shifts = [
        (seq_index < seq_index ^ 2 * f).astype(jnp.int32) * 4 for f in flips_b
    ]
    shifts = jnp.stack(shifts)
    turns = []
    for near in (flips_a, flips_b):
        near = (0, near[1], near[0], near[0] ^ near[1])
        turns.append(tuple(2 * m for m in near) + tuple(2 * m + 1 for m in near))
    picks = pick_norm(place, exp_normed, tuple(turns), dim, per_token, capacity)
    (keep_a, send_a, keep_far_a, send_far_a) = picks[:4]
    (keep_b, send_b, keep_far_b, send_far_b) = picks[4:]
    got_a, got_b = swap(send_far_a, "seq", 1), swap(send_far_b, "seq", 1)
    message_a, message_b = merge(
        shifts,
        [
            [(send_a, (0, 1), None), (got_a, (0, 1), None)],
            [(send_b, (0, 1), None), (got_b, (0, 1), None)],
        ],
    )
    first_a = swap(message_a, "seq", 2 * flips_a[0])
    far_a, far_b = swap(keep_far_a, "seq", 1), swap(keep_far_b, "seq", 1)
    flow, far_a, far_b, message_b = lax.optimization_barrier((flow, far_a, far_b, message_b))
    flow_far = swap(flow, "seq", 1)

    flips = (1, 3, 4, 12)
    quarters = len(flips)
    orders = [flips[k:] + flips[:k] for k in range(quarters)]
    bit_rows = [tuple((j >> (3 - b)) & 1 for b in range(4)) for j in range(n_exp)]
    turns = [[mask_of(order, bits) for bits in bit_rows] for order in orders]
    half = n_exp // 2
    late = [t[half:] for t in turns]
    sends = pick_grad(place, tables, [flow], (0,), late, n_exp, per_token, capacity)
    sends = pick_grad(place, tables, [flow_far], (1,), late, n_exp, per_token, capacity, sends)
    early = [t[:half] for t in turns]
    keeps = pick_grad(
        place, tables, [flow, flow_far], (0, 1), early, n_exp, per_token, capacity
    )
    streams = range(quarters)
    firsts = [swap(sends[k], "exp", orders[k][0]) for k in streams]
    messages = merge(shifts, [second_parts(keeps[k], firsts[k]) for k in streams], [first_a])
    seconds = [swap(messages[k], "exp", orders[k][1]) for k in streams]
    firsts, local_grad = lax.optimization_barrier((firsts, local_grad))
    qkv_parts = local_grad.reshape(n_seq, tokens, width)
    qkv_parts = lax.all_to_all(qkv_parts, "seq", split_axis=0, concat_axis=0, tiled=True)
    qkv_in_grad = qkv_parts.swapaxes(0, 1).reshape(tokens, n_seq * width)
    first_b = swap_gather(message_b, "seq", 2 * flips_b[0])
    messages = merge(
        shifts,
        [third_parts(keeps[k], firsts[k], seconds[k]) for k in streams]
        + [
            [(keep_a, (1,), None), (far_a, (1,), None), (first_a, (1, 3), None)],
            [(keep_b, (1,), None), (far_b, (1,), None), (first_b, (1, 3), 0)],
        ],
        [qkv_parts],
    )
    thirds_out, (message_a, message_b) = messages[:quarters], messages[quarters:]
    thirds = [swap(thirds_out[k], "exp", orders[k][2]) for k in streams]
    second_a = swap(message_a, "seq", 2 * flips_a[1])
    second_b = swap_gather(message_b, "seq", 2 * flips_b[1])
    calls = [
        [(keep_a, 0, None), (far_a, 0, None), (first_a, 0, None), (first_a, 2, None)],
        [(keep_b, 0, None), (far_b, 0, None), (first_b, 0, 0), (first_b, 2, 0)],
        [(second_a, i, None) for i in range(4)],
        [(second_b, i, 1) for i in range(4)],
    ]
    results = ()
    for part, pieces in enumerate(calls):
        results = expert_forward(
            pieces, own_weights, hidden, shifts, len(calls), part, results
        )
        if part == 1:
            results, thirds = lax.optimization_barrier((results, thirds))
    rows_all, act, gate, up = results

    def row_of(mask, quarter):
        half, inner = mask >> 3, mask & 7
        flips = flips_of(half)
        order = (0, flips[0], flips[1], flips[0] ^ flips[1])
        spot = order.index(quarter)
        call = (spot >> 1) * 2 + half
        tile = call * 2 + (inner >> 2)
        return tile * n_exp * capacity + (inner & 3) * 4 * capacity + (spot & 1) * 2 * capacity

    messages = merge(
        shifts, [fourth_parts(keeps[k], firsts[k], seconds[k], thirds[k]) for k in streams]
    )
    fourths = [swap(messages[k], "exp", orders[k][3]) for k in streams]
    arrays, places = [], []
    for k in streams:
        got = [keeps[k], firsts[k], seconds[k], thirds[k], fourths[k]]
        for mask, (array, unit) in sorted(grad_places(orders[k]).items()):
            places.append((len(arrays) + array, unit, row_of(mask, k), 2 * capacity))
        arrays += got
    expert_grads = expert_backward(arrays, tuple(places), gate, up, own_weights, rows_all, act)
    return (qkv_in_grad, expert_grads[None])


def solution(mesh):
    return jax.shard_map(
        per_device,
        mesh=mesh,
        in_specs=(
            P("exp", "seq"),
            P("exp", "seq"),
            P(None, "seq"),
            P(),
            P("seq", None),
            P(("exp", "seq"), None),
            P(),
            P(("exp", "seq"), None),
            P(("exp", "seq"), None),
            P(("exp", "seq"), None),
            P(("seq", "exp"), None, None),
        ),
        out_specs=(P(("exp", "seq"), None), P(("seq", "exp"), None, None)),
        check_vma=False,
    )
```

```python
import functools

import jax
import jax.numpy as jnp
from jax import lax
from jax.experimental import pallas as pl
from jax.experimental.pallas import tpu as pltpu
from jax.sharding import PartitionSpec as P

BF16 = jnp.bfloat16
F32 = jnp.float32
HALO = 16
MIB = 1024 * 1024
VMEM_LIMIT = 127 * MIB // 2
EXTRA = 128


def call_cost(flops, nbytes):
    return pl.CostEstimate(flops=int(flops), bytes_accessed=int(nbytes), transcendentals=0)


def norm_kernel(resid_ref, gain_ref, routes_ref, out_ref):
    rows = resid_ref[...].astype(F32)
    dim = rows.shape[1]
    scale = lax.rsqrt(jnp.mean(rows * rows, axis=1, keepdims=True) + 1e-06)
    out_ref[:, :dim] = (rows * scale * gain_ref[...]).astype(BF16)
    out_ref[:, dim:] = jnp.zeros((rows.shape[0], EXTRA), BF16)
    names = routes_ref[...].astype(F32)
    pad = jnp.zeros((HALO - names.shape[0], EXTRA), F32)
    out_ref[:HALO, dim:] = jnp.concatenate([names, pad]).astype(BF16)


def norm_rows(resid, gain, names):
    tokens, dim = resid.shape
    return pl.pallas_call(
        norm_kernel,
        out_shape=jax.ShapeDtypeStruct((tokens, dim + EXTRA), BF16),
        compiler_params=pltpu.CompilerParams(vmem_limit_bytes=VMEM_LIMIT),
        cost_estimate=call_cost(resid.size * 6, resid.size * 4),
        name="norm_rows",
    )(resid, gain.reshape(1, -1), names)


def conv_kernel(
    tile,
    place_ref,
    in_ref,
    in_low_ref,
    in_high_ref,
    grad_ref,
    grad_high_ref,
    ids_ref,
    taps_ref,
    local_ref,
    keep_ref,
    send_ref,
    in_ext,
    grad_ext,
):
    step = pl.program_id(0)
    rows = in_ref.shape[0]

    @pl.when(step == 0)
    def _():
        in_ext[:HALO] = in_low_ref[...].astype(F32)
        in_ext[HALO : HALO + rows] = in_ref[...].astype(F32)
        in_ext[HALO + rows :] = in_high_ref[...].astype(F32)
        grad_ext[:rows] = grad_ref[...].astype(F32)
        grad_ext[rows:] = grad_high_ref[...].astype(F32)

    first = pl.multiple_of(step * tile, tile)
    span = tile + 8
    taps = taps_ref[...]
    window = in_ext[pl.ds(first + HALO - 8, span + 8)]
    ids = ids_ref[pl.ds(first + HALO - 8, span + 8)]
    here = ids[8:]
    same = [None] + [(ids[8 - j : 8 - j + span] == here).astype(F32) for j in (1, 2, 3)]
    conv = taps[0:1] * window[8:]
    for j in (1, 2, 3):
        conv = conv + taps[j : j + 1] * window[8 - j : 8 - j + span] * same[j]
    gate = jax.nn.sigmoid(conv)
    pre = grad_ext[pl.ds(first, span)] * gate * (1.0 + conv * (1.0 - gate))
    result = taps[0:1] * pre[:tile]
    for j in (1, 2, 3):
        result = result + taps[j : j + 1] * (pre * same[j])[j : j + tile]
    local = result.astype(BF16)
    local_ref[...] = local
    half = tile // 2
    core = place_ref[0] & 1

    @pl.when(core == 0)
    def _():
        keep_ref[...] = local[:half]
        send_ref[...] = local[half:]

    @pl.when(core == 1)
    def _():
        keep_ref[...] = local[half:]
        send_ref[...] = local[:half]


def conv_back(place, qkv_in, low, high, qkv_grad, grad_high, ids, taps, block):
    rows, width = qkv_in.shape
    tile = 2 * block
    whole = lambda shape: pl.BlockSpec(shape, lambda i, p: (0,) * len(shape))
    part = lambda size: pl.BlockSpec((size, width), lambda i, p: (i, 0))
    return pl.pallas_call(
        functools.partial(conv_kernel, tile),
        grid_spec=pltpu.PrefetchScalarGridSpec(
            num_scalar_prefetch=1,
            grid=(rows // tile,),
            in_specs=[
                whole(qkv_in.shape),
                whole(low.shape),
                whole(high.shape),
                whole(qkv_grad.shape),
                whole(grad_high.shape),
                whole(ids.shape),
                whole(taps.shape),
            ],
            out_specs=[part(tile), part(block), part(block)],
            scratch_shapes=[
                pltpu.VMEM((rows + 2 * HALO, width), F32),
                pltpu.VMEM((rows + HALO, width), F32),
            ],
        ),
        out_shape=[
            jax.ShapeDtypeStruct((rows, width), BF16),
            jax.ShapeDtypeStruct((rows // 2, width), BF16),
            jax.ShapeDtypeStruct((rows // 2, width), BF16),
        ],
        compiler_params=pltpu.CompilerParams(vmem_limit_bytes=VMEM_LIMIT),
        cost_estimate=call_cost(40 * rows * width, 8 * rows * width),
        name="conv_back",
    )(place, qkv_in, low, high, qkv_grad, grad_high, ids, taps)


def project_kernel(place_ref, own_ref, other_ref, own_weight, other_weight, flow_ref, out_ref):
    block = flow_ref.shape[0]
    total = jnp.dot(own_ref[...], own_weight[...], preferred_element_type=F32)
    total = total + jnp.dot(other_ref[...], other_weight[...], preferred_element_type=F32)
    out_ref[...] = total.astype(BF16)
    for index in range(out_ref.shape[0] // block):

        @pl.when(index == place_ref[0] >> 1)
        def _():
            own = slice(index * block, (index + 1) * block)
            out_ref[own] = (total[own] + flow_ref[...].astype(F32)).astype(BF16)


def project(place, own, other, own_weight, other_weight, out_grad):
    rows, width = own.shape
    dim = own_weight.shape[1]
    tile = dim // 9
    whole = pl.BlockSpec((rows, width), lambda i, p: (0, 0))
    columns = lambda size: pl.BlockSpec((size, tile), lambda i, p: (0, i))
    return pl.pallas_call(
        project_kernel,
        grid_spec=pltpu.PrefetchScalarGridSpec(
            num_scalar_prefetch=1,
            grid=(dim // tile,),
            in_specs=[whole, whole, columns(width), columns(width), columns(out_grad.shape[0])],
            out_specs=columns(rows),
        ),
        out_shape=jax.ShapeDtypeStruct((rows, dim), BF16),
        compiler_params=pltpu.CompilerParams(vmem_limit_bytes=VMEM_LIMIT),
        cost_estimate=call_cost(4 * rows * width * dim, 4 * (rows + dim) * width + 2 * rows * dim),
        name="project",
    )(place, own, other, own_weight, other_weight, out_grad)


def slot_picker(names, own, capacity):
    count, tokens = own.shape
    match = [(names[k : k + 1] == own) for k in range(names.shape[0])]
    named = functools.reduce(jnp.logical_or, match)
    source = lax.broadcasted_iota(jnp.int32, (tokens, tokens), 0)
    target = lax.broadcasted_iota(jnp.int32, (tokens, tokens), 1)
    earlier = (source < target).astype(BF16)
    rank = jnp.dot(named.astype(BF16), earlier, preferred_element_type=F32).astype(jnp.int32)
    rank = jnp.where(named, rank, -1)
    slot = lax.broadcasted_iota(jnp.int32, (count, capacity, tokens), 1)
    picker = (rank[:, None, :] == slot).astype(F32)
    return picker, match


def pick_norm_kernel(per_token, capacity, n_exp, turns, place_ref, *refs):
    halves = len(turns)
    out_refs = refs[halves:]
    outs = len(out_refs) // halves
    for half in range(halves):
        rows_ref = refs[half]
        tokens = rows_ref.shape[1]
        dim = out_refs[0].shape[3]
        count = len(turns[half])
        names = rows_ref[0, :HALO, dim:].astype(F32)[:per_token].astype(jnp.int32)
        own = jnp.concatenate(
            [
                jnp.full((1, tokens), (place_ref[0] ^ t) * n_exp + place_ref[1], jnp.int32)
                for t in turns[half]
            ]
        )
        picker, _ = slot_picker(names, own, capacity)
        picker = picker.reshape(count * capacity, tokens).astype(BF16)
        picked = jnp.dot(picker, rows_ref[0, :, :dim], preferred_element_type=F32).astype(BF16)
        for index in range(count):
            out_refs[half * outs + index // 2][index % 2, 0] = picked[
                index * capacity : (index + 1) * capacity
            ]


def pick_norm(place, rows, turns, dim, per_token, capacity):
    blocks, tokens, width = rows.shape
    halves = len(turns)
    count = blocks // halves
    outs = len(turns[0]) // 2 * halves
    row_spec = lambda first: pl.BlockSpec(
        (1, tokens, width), lambda i, p: (p[1] ^ (i + first), 0, 0)
    )
    return pl.pallas_call(
        functools.partial(pick_norm_kernel, per_token, capacity, blocks, turns),
        grid_spec=pltpu.PrefetchScalarGridSpec(
            num_scalar_prefetch=1,
            grid=(count,),
            in_specs=[row_spec(half * count) for half in range(halves)],
            out_specs=[pl.BlockSpec((2, 1, capacity, dim), lambda i, p: (0, i, 0, 0))] * outs,
        ),
        out_shape=[jax.ShapeDtypeStruct((2, count, capacity, dim), BF16)] * outs,
        compiler_params=pltpu.CompilerParams(vmem_limit_bytes=VMEM_LIMIT),
        cost_estimate=call_cost(
            2 * len(turns[0]) * capacity * blocks * tokens * dim,
            2 * dim * blocks * (tokens + len(turns[0]) * capacity),
        ),
        name="pick_norm",
    )(place, *[rows] * halves)


def pick_grad_kernel(per_token, capacity, n_exp, turns, cores, place_ref, tables_ref, *refs):
    flow_refs, out_refs = refs[: len(cores)], refs[-2 - len(turns) : -2]
    buffer, sems = refs[-2:]
    tokens = tables_ref.shape[2]
    copies = []
    for quarter, turn in enumerate(turns):
        count = len(turn)
        own = jnp.concatenate(
            [
                jnp.full((1, tokens), place_ref[0] * n_exp + (place_ref[1] ^ t), jnp.int32)
                for t in turn
            ]
        )
        first = pl.multiple_of(((place_ref[0] >> 1) ^ quarter) * tokens, tokens)
        for spot, core in enumerate(cores):
            table = tables_ref[place_ref[0] ^ (2 * quarter + core)]
            names = table[:per_token].astype(jnp.int32)
            picker, match = slot_picker(names, own, capacity)
            weights = table[per_token:]
            scale = functools.reduce(
                jnp.add, [jnp.where(match[k], weights[k : k + 1], 0.0) for k in range(per_token)]
            )
            scales = jnp.sum(picker * scale[:, None, :], axis=2, keepdims=True)
            picker = picker.reshape(count * capacity, tokens).astype(BF16)
            picked = jnp.dot(
                picker, flow_refs[spot][pl.ds(first, tokens)], preferred_element_type=F32
            )
            picked = (picked * scales.reshape(count * capacity, 1)).astype(BF16)
            buffer[quarter, spot] = picked.reshape(count, capacity, -1)
            at = quarter * len(cores) + spot
            copy = pltpu.make_async_copy(
                buffer.at[quarter, spot],
                out_refs[quarter].at[:, pl.ds(core * capacity, capacity)],
                sems.at[at],
            )
            copy.start()
            copies.append(copy)
    for copy in copies:
        copy.wait()


def pick_grad(place, tables, flows, cores, turns, n_exp, per_token, capacity, before=()):
    dim = flows[0].shape[1]
    rows, count = 2 * capacity, len(turns[0])
    whole = lambda array: pl.BlockSpec(array.shape, lambda i, p: (0,) * array.ndim)
    any_spec = pl.BlockSpec(memory_space=pl.ANY)
    outs = len(turns)
    return pl.pallas_call(
        functools.partial(pick_grad_kernel, per_token, capacity, n_exp, turns, cores),
        grid_spec=pltpu.PrefetchScalarGridSpec(
            num_scalar_prefetch=1,
            grid=(1,),
            in_specs=[whole(tables)] + [whole(flow) for flow in flows] + [any_spec] * len(before),
            out_specs=[any_spec] * outs,
            scratch_shapes=[
                pltpu.VMEM((outs, len(cores), count, capacity, dim), BF16),
                pltpu.SemaphoreType.DMA((outs * len(cores),)),
            ],
        ),
        out_shape=[jax.ShapeDtypeStruct((count, rows, dim), BF16)] * outs,
        input_output_aliases={2 + len(flows) + i: i for i in range(len(before))},
        compiler_params=pltpu.CompilerParams(vmem_limit_bytes=VMEM_LIMIT),
        cost_estimate=call_cost(
            2 * outs * count * capacity * len(cores) * tables.shape[2] * dim,
            2 * dim * len(cores) * (flows[0].shape[0] + outs * count * capacity),
        ),
        name="pick_grad",
    )(place, tables, *flows, *before)


def forward_kernel(sources, *refs):
    row_refs = refs[1 : 1 + sources]
    weight_ref = refs[1 + sources]
    rows_out, act_ref, gate_ref, up_ref, rows = refs[-5:]
    _, group, capacity, _ = row_refs[0].shape
    for inner in range(group):
        for index in range(sources):
            at = (inner * sources + index) * capacity
            rows[at : at + capacity] = row_refs[index][0, inner]
    hidden = act_ref.shape[0]
    mixed = jnp.dot(rows[...], weight_ref[...], preferred_element_type=F32)
    rows_out[...] = rows[...].T
    gate = mixed[:, :hidden]
    up = mixed[:, hidden:]
    sig = jax.nn.sigmoid(gate)
    silu = gate * sig
    act_ref[...] = (silu * up).astype(BF16).T
    gate_ref[...] = (up * sig * (1.0 + gate * (1.0 - sig))).astype(BF16)
    up_ref[...] = silu.astype(BF16)


def expert_forward(pieces, weight, hidden, shifts, parts, part, before):
    sources = len(pieces)
    _, blocks, capacity, dim = pieces[0][0].shape
    group = 16 // sources
    tile = sources * group * capacity
    steps = blocks // group
    total = tile * steps * parts
    at = lambda i: i + part * steps
    row_spec = lambda width: pl.BlockSpec((tile, width), lambda i, p: (at(i), 0))
    column_spec = lambda height: pl.BlockSpec((height, tile), lambda i, p: (0, at(i)))

    def piece_spec(unit, shift):
        return pl.BlockSpec(
            (1, group, capacity, dim),
            lambda i, p: (unit if shift is None else unit + p[shift], i, 0, 0),
        )

    return pl.pallas_call(
        functools.partial(forward_kernel, sources),
        grid_spec=pltpu.PrefetchScalarGridSpec(
            num_scalar_prefetch=1,
            grid=(steps,),
            in_specs=[piece_spec(unit, shift) for _, unit, shift in pieces]
            + [pl.BlockSpec((dim, 2 * hidden), lambda i, p: (0, 0))]
            + [pl.BlockSpec(memory_space=pl.ANY)] * len(before),
            out_specs=[column_spec(dim), column_spec(hidden), row_spec(hidden), row_spec(hidden)],
            scratch_shapes=[pltpu.VMEM((tile, dim), BF16)],
        ),
        out_shape=[
            jax.ShapeDtypeStruct((dim, total), BF16),
            jax.ShapeDtypeStruct((hidden, total), BF16),
            jax.ShapeDtypeStruct((total, hidden), BF16),
            jax.ShapeDtypeStruct((total, hidden), BF16),
        ],
        input_output_aliases={sources + 2 + i: i for i in range(len(before))},
        compiler_params=pltpu.CompilerParams(vmem_limit_bytes=VMEM_LIMIT),
        cost_estimate=call_cost(
            4 * total * dim * hidden // parts, (4 * total * dim + 10 * total * hidden) // parts
        ),
        name="expert_forward",
    )(shifts, *[array for array, _, _ in pieces], weight, *before)


def backward_kernel(places, arrays, *refs):
    grad_refs = refs[:arrays]
    gate_ref, up_ref, weight_ref, rows_ref, act_ref, out_ref = refs[arrays : arrays + 6]
    grads_all, hidden_all, sems = refs[arrays + 6 :]
    step = pl.program_id(0)
    tile = gate_ref.shape[0]
    hidden = act_ref.shape[0]
    width = rows_ref.shape[0]
    row_steps = grads_all.shape[0] // tile
    copies = []
    for index, (array, unit, row, size) in enumerate(places):
        copy = pltpu.make_async_copy(
            grad_refs[array].at[unit], grads_all.at[pl.ds(row, size)], sems.at[index]
        )
        copies.append((row // tile, copy))

    @pl.when(step == 0)
    def _():
        for turn in range(row_steps):
            for at, copy in copies:
                if at == turn:
                    copy.start()

    for turn in range(row_steps):

        @pl.when(step == turn)
        def _():
            for at, copy in copies:
                if at == turn:
                    copy.wait()

    @pl.when(step < row_steps)
    def _():
        where = pl.ds(pl.multiple_of(step * tile, tile), tile)
        act_grad = jnp.dot(grads_all[where], weight_ref[...], preferred_element_type=F32)
        hidden_all[where, :hidden] = (act_grad * gate_ref[...].astype(F32)).astype(BF16)
        hidden_all[where, hidden:] = (act_grad * up_ref[...].astype(F32)).astype(BF16)

    @pl.when(step >= row_steps)
    def _():
        columns = pl.ds(pl.multiple_of((step - row_steps) * width, width), width)
        out_ref[:, : 2 * hidden] = jnp.dot(
            rows_ref[...], hidden_all[...], preferred_element_type=F32
        ).astype(BF16)
        down = jnp.dot(act_ref[...], grads_all[:, columns], preferred_element_type=F32)
        out_ref[:, 2 * hidden :] = down.T.astype(BF16)


def expert_backward(arrays, places, gate, up, weights, rows, act):
    dim, total = rows.shape
    hidden = act.shape[0]
    tile, width = 512, 768
    row_steps, column_steps = total // tile, dim // width
    row_spec = lambda cols: pl.BlockSpec(
        (tile, cols), lambda i: (jnp.minimum(i, row_steps - 1), 0)
    )
    column_of = lambda i: jnp.maximum(i - row_steps, 0)
    return pl.pallas_call(
        functools.partial(backward_kernel, places, len(arrays)),
        grid=(row_steps + column_steps,),
        in_specs=[pl.BlockSpec(memory_space=pl.ANY)] * len(arrays)
        + [
            row_spec(hidden),
            row_spec(hidden),
            pl.BlockSpec((dim, hidden), lambda i: (0, 2)),
            pl.BlockSpec((width, total), lambda i: (column_of(i), 0)),
            pl.BlockSpec((hidden, total), lambda i: (0, 0)),
        ],
        out_specs=pl.BlockSpec((width, 3 * hidden), lambda i: (column_of(i), 0)),
        out_shape=jax.ShapeDtypeStruct((dim, 3 * hidden), BF16),
        scratch_shapes=[
            pltpu.VMEM((total, dim), BF16),
            pltpu.VMEM((total, 2 * hidden), BF16),
            pltpu.SemaphoreType.DMA((len(places),)),
        ],
        compiler_params=pltpu.CompilerParams(vmem_limit_bytes=VMEM_LIMIT),
        cost_estimate=call_cost(8 * total * dim * hidden, 4 * total * dim + 20 * total * hidden),
        name="expert_backward",
    )(*arrays, gate, up, weights, rows, act)


def merge_kernel(plans, arrays, shift_ref, *refs):
    sources, refs = refs[:arrays], refs[arrays + refs_after(refs, arrays, plans) :]
    outs, buffers = refs[: len(plans)], refs[len(plans) : 2 * len(plans)]
    in_sems, out_sems = refs[2 * len(plans) :]
    reads, count = [], 0
    for plan, buffer in zip(plans, buffers):
        copies = []
        for at, (array, unit, shift) in enumerate(plan):
            first = unit if shift is None else unit + shift_ref[shift]
            half = buffer.shape[1] // 2
            for piece in range(2):
                rows = pl.ds(piece * half, half)
                copies.append(
                    pltpu.make_async_copy(
                        sources[array].at[first, rows], buffer.at[at, rows], in_sems.at[count]
                    )
                )
                count += 1
        reads.append(copies)
    for copies in reads:
        for copy in copies:
            copy.start()
    writes = []
    for index, copies in enumerate(reads):
        for copy in copies:
            copy.wait()
        writes.append(pltpu.make_async_copy(buffers[index], outs[index], out_sems.at[index]))
        writes[-1].start()
    for copy in writes:
        copy.wait()


def refs_after(refs, arrays, plans):
    return len(refs) - arrays - 2 * len(plans) - 2


def merge(shifts, messages, after=()):
    arrays, plans = [], []
    for parts in messages:
        plan = []
        for array, units, shift in parts:
            known = [i for i, other in enumerate(arrays) if other is array]
            if not known:
                arrays.append(array)
                known = [len(arrays) - 1]
            plan += [(known[0], unit, shift) for unit in units]
        plans.append(tuple(plan))
    shapes = [(len(plan),) + arrays[plan[0][0]].shape[1:] for plan in plans]
    size = sum(functools.reduce(lambda a, b: a * b, shape, 1) for shape in shapes)
    any_spec = pl.BlockSpec(memory_space=pl.ANY)
    return pl.pallas_call(
        functools.partial(merge_kernel, tuple(plans), len(arrays)),
        grid_spec=pltpu.PrefetchScalarGridSpec(
            num_scalar_prefetch=1,
            grid=(1,),
            in_specs=[any_spec] * (len(arrays) + len(after)),
            out_specs=[any_spec] * len(plans),
            scratch_shapes=[pltpu.VMEM(shape, BF16) for shape in shapes]
            + [
                pltpu.SemaphoreType.DMA((2 * sum(len(plan) for plan in plans),)),
                pltpu.SemaphoreType.DMA((len(plans),)),
            ],
        ),
        out_shape=[jax.ShapeDtypeStruct(shape, BF16) for shape in shapes],
        compiler_params=pltpu.CompilerParams(vmem_limit_bytes=VMEM_LIMIT),
        cost_estimate=call_cost(0, 4 * size),
        name="merge_rows",
    )(shifts, *arrays, *after)


def swap(array, axis, flip):
    count = lax.axis_size(axis)
    return lax.ppermute(array, axis, [(i, i ^ flip) for i in range(count)])


def mask_of(flips, bits):
    return functools.reduce(lambda a, b: a ^ b, [f for f, bit in zip(flips, bits) if bit], 0)


def flips_of(half):
    return (1, 3) if half == 0 else (3, 1)


def swap_gather(array, axis, flip):
    count = lax.axis_size(axis)
    groups = [[i, i ^ flip] for i in range(count) if i < i ^ flip]
    both = lax.all_gather(array, axis, axis_index_groups=groups)
    return both.reshape((-1,) + array.shape[1:])


def second_parts(keep, first):
    return [(keep, range(4, 8), None), (first, range(4, 8), None)]


def third_parts(keep, first, second):
    return [
        (keep, (2, 3), None),
        (first, (2, 3), None),
        (second, (2, 3, 6, 7), None),
    ]


def fourth_parts(keep, first, second, third):
    return [
        (keep, (1,), None),
        (first, (1,), None),
        (second, (1, 5), None),
        (third, (1, 3, 5, 7), None),
    ]


def grad_places(flips):
    found = {}
    found[0, 0, 0, 0] = (0, 0)
    found[1, 0, 0, 0] = (1, 0)
    found[0, 1, 0, 0] = (2, 0)
    found[1, 1, 0, 0] = (2, 4)
    for index, start in enumerate([(0, 0), (1, 0), (0, 1), (1, 1)]):
        found[start + (1, 0)] = (3, 2 * index)
        found[start + (0, 1)] = (4, index)
        found[start + (1, 1)] = (4, 4 + index)
    return {mask_of(flips, bits): at for bits, at in found.items()}


def per_device(
    qkv_in,
    qkv_grad,
    conv_weight,
    doc_ids,
    qkv_weight,
    resid,
    norm_gain,
    out_grad,
    routes,
    route_weights,
    expert_weights,
):
    rows, width = qkv_in.shape
    tokens, dim = resid.shape
    per_token = routes.shape[1]
    hidden = expert_weights.shape[2] // 3
    n_seq, n_exp = lax.axis_size("seq"), lax.axis_size("exp")
    experts = n_seq * n_exp
    capacity = 2 * tokens * per_token // experts
    seq_index, exp_index = lax.axis_index("seq"), lax.axis_index("exp")
    own_weights = expert_weights[0]

    place = jnp.stack([seq_index, exp_index]).astype(jnp.int32)
    forward = [(i, i + 1) for i in range(n_exp - 1)]
    backward = [(i + 1, i) for i in range(n_exp - 1)]
    low = lax.ppermute(qkv_in[-HALO:], "exp", forward)
    high = lax.ppermute(qkv_in[:HALO], "exp", backward)
    grad_high = lax.ppermute(qkv_grad[:HALO], "exp", backward)
    weight_far = swap(qkv_weight, "seq", 1)

    table = jnp.concatenate([routes.astype(F32), route_weights], 1).T
    normed = norm_rows(resid, norm_gain, routes.T)
    normed, conv_weight = lax.optimization_barrier((normed, conv_weight))
    exp_normed = lax.all_gather(normed, "exp")

    edge = jnp.full((HALO,), -1, jnp.int32)
    ids = lax.dynamic_slice_in_dim(
        jnp.concatenate([edge, doc_ids, edge]), exp_index * rows, rows + 2 * HALO
    )
    local_grad, local_keep, local_send = conv_back(
        place, qkv_in, low, high, qkv_grad, grad_high, ids.reshape(-1, 1), conv_weight, tokens
    )
    local_got = swap(local_send, "seq", 1)
    partial = project(place, local_keep, local_got, qkv_weight, weight_far, out_grad)
    table, partial = lax.optimization_barrier((table, partial))
    tables = jnp.broadcast_to(table[None], (n_seq,) + table.shape)
    tables = lax.all_to_all(tables, "seq", split_axis=0, concat_axis=0, tiled=True)
    same_core = [[s for s in range(n_seq) if s % 2 == core] for core in range(2)]
    flow = lax.psum(partial, "seq", axis_index_groups=same_core)

    exp_normed, tables = lax.optimization_barrier((exp_normed, tables))
    flips_a, flips_b = flips_of(0), flips_of(1)
    shifts = [
        (seq_index < seq_index ^ 2 * f).astype(jnp.int32) * 4 for f in flips_b
    ]
    shifts = jnp.stack(shifts)
    turns = []
    for near in (flips_a, flips_b):
        near = (0, near[1], near[0], near[0] ^ near[1])
        turns.append(tuple(2 * m for m in near) + tuple(2 * m + 1 for m in near))
    picks = pick_norm(place, exp_normed, tuple(turns), dim, per_token, capacity)
    (keep_a, send_a, keep_far_a, send_far_a) = picks[:4]
    (keep_b, send_b, keep_far_b, send_far_b) = picks[4:]
    got_a, got_b = swap(send_far_a, "seq", 1), swap(send_far_b, "seq", 1)
    message_a, message_b = merge(
        shifts,
        [
            [(send_a, (0, 1), None), (got_a, (0, 1), None)],
            [(send_b, (0, 1), None), (got_b, (0, 1), None)],
        ],
    )
    first_a = swap(message_a, "seq", 2 * flips_a[0])
    far_a, far_b = swap(keep_far_a, "seq", 1), swap(keep_far_b, "seq", 1)
    flow, far_a, far_b, message_b, local_grad = lax.optimization_barrier(
        (flow, far_a, far_b, message_b, local_grad)
    )
    qkv_parts = local_grad.reshape(n_seq, tokens, width)
    qkv_parts = lax.all_to_all(qkv_parts, "seq", split_axis=0, concat_axis=0, tiled=True)
    qkv_in_grad = qkv_parts.swapaxes(0, 1).reshape(tokens, n_seq * width)
    first_b = swap_gather(message_b, "seq", 2 * flips_b[0])
    flow_far = swap(flow, "seq", 1)

    flips = (1, 3, 4, 12)
    quarters = len(flips)
    orders = [flips[k:] + flips[:k] for k in range(quarters)]
    bit_rows = [tuple((j >> (3 - b)) & 1 for b in range(4)) for j in range(n_exp)]
    turns = [[mask_of(order, bits) for bits in bit_rows] for order in orders]
    half = n_exp // 2
    late = [t[half:] for t in turns]
    sends = pick_grad(place, tables, [flow], (0,), late, n_exp, per_token, capacity)
    sends = pick_grad(place, tables, [flow_far], (1,), late, n_exp, per_token, capacity, sends)
    early = [t[:half] for t in turns]
    keeps = pick_grad(
        place, tables, [flow, flow_far], (0, 1), early, n_exp, per_token, capacity
    )
    streams = range(quarters)
    firsts = [swap(sends[k], "exp", orders[k][0]) for k in streams]
    messages = merge(shifts, [second_parts(keeps[k], firsts[k]) for k in streams], [first_a])
    seconds = [swap(messages[k], "exp", orders[k][1]) for k in streams]
    messages = merge(
        shifts,
        [third_parts(keeps[k], firsts[k], seconds[k]) for k in streams]
        + [
            [(keep_a, (1,), None), (far_a, (1,), None), (first_a, (1, 3), None)],
            [(keep_b, (1,), None), (far_b, (1,), None), (first_b, (1, 3), 0)],
        ],
        [qkv_parts],
    )
    thirds_out, (message_a, message_b) = messages[:quarters], messages[quarters:]
    thirds = [swap(thirds_out[k], "exp", orders[k][2]) for k in streams]
    second_a = swap(message_a, "seq", 2 * flips_a[1])
    second_b = swap_gather(message_b, "seq", 2 * flips_b[1])
    calls = [
        [(keep_a, 0, None), (far_a, 0, None), (first_a, 0, None), (first_a, 2, None)],
        [(keep_b, 0, None), (far_b, 0, None), (first_b, 0, 0), (first_b, 2, 0)],
        [(second_a, i, None) for i in range(4)],
        [(second_b, i, 1) for i in range(4)],
    ]
    results = ()
    for part, pieces in enumerate(calls):
        results = expert_forward(
            pieces, own_weights, hidden, shifts, len(calls), part, results
        )
        if part == 1:
            results, thirds = lax.optimization_barrier((results, thirds))
    rows_all, act, gate, up = results

    def row_of(mask, quarter):
        half, inner = mask >> 3, mask & 7
        flips = flips_of(half)
        order = (0, flips[0], flips[1], flips[0] ^ flips[1])
        spot = order.index(quarter)
        call = (spot >> 1) * 2 + half
        tile = call * 2 + (inner >> 2)
        return tile * n_exp * capacity + (inner & 3) * 4 * capacity + (spot & 1) * 2 * capacity

    messages = merge(
        shifts, [fourth_parts(keeps[k], firsts[k], seconds[k], thirds[k]) for k in streams]
    )
    fourths = [swap(messages[k], "exp", orders[k][3]) for k in streams]
    arrays, places = [], []
    for k in streams:
        got = [keeps[k], firsts[k], seconds[k], thirds[k], fourths[k]]
        for mask, (array, unit) in sorted(grad_places(orders[k]).items()):
            places.append((len(arrays) + array, unit, row_of(mask, k), 2 * capacity))
        arrays += got
    expert_grads = expert_backward(arrays, tuple(places), gate, up, own_weights, rows_all, act)
    return (qkv_in_grad, expert_grads[None])


def solution(mesh):
    return jax.shard_map(
        per_device,
        mesh=mesh,
        in_specs=(
            P("exp", "seq"),
            P("exp", "seq"),
            P(None, "seq"),
            P(),
            P("seq", None),
            P(("exp", "seq"), None),
            P(),
            P(("exp", "seq"), None),
            P(("exp", "seq"), None),
            P(("exp", "seq"), None),
            P(("seq", "exp"), None, None),
        ),
        out_specs=(P(("exp", "seq"), None), P(("seq", "exp"), None, None)),
        check_vma=False,
    )
```
